32 devices in a mesh: dp: 8 (over y, x, core), tensor: 4 (over z).
Axes of the slice: x: 2, y: 2, z: 4, core: 2. Of those that a mesh axis runs over, the one named last changes fastest.
Arguments:
- block_input: bfloat16 [8192, 768], P(('dp', 'tensor')), may hold values from -6 to 6
- doc_lengths: int32 [8, 2], P('dp'), may hold values from 0 to 1024, as said below
- first_gain: bfloat16 [768], P(('dp', 'tensor')), may hold values from 0.5 to 1.5
- first_shift: bfloat16 [768], P(('dp', 'tensor')), may hold values from -1 to 1
- qkv_weight: bfloat16 [768, 3, 768], P('dp', None, 'tensor'), may hold values from -0.21875 to 0.21875
- attn_bias: bfloat16 [1536], P(('dp', 'tensor')), may hold values from -1.5 to 1.5
- out_weight: bfloat16 [768, 768], P('tensor', 'dp'), may hold values from -3.5 to 3.5
- out_bias: bfloat16 [768], P(('dp', 'tensor')), may hold values from -1.5 to 1.5
- second_gain: bfloat16 [768], P(('dp', 'tensor')), may hold values from 0.5 to 1.5
- second_shift: bfloat16 [768], P(('dp', 'tensor')), may hold values from -1 to 1
- fc_weight: bfloat16 [768, 3072], P('dp', 'tensor'), may hold values from -0.21875 to 0.21875
- fc_bias: bfloat16 [3072], P(('dp', 'tensor')), may hold values from -1.5 to 1.5
- proj_weight: bfloat16 [3072, 768], P('tensor', 'dp'), may hold values from -0.109375 to 0.109375
- proj_bias: bfloat16 [768], P(('dp', 'tensor')), may hold values from -1.5 to 1.5
- block_grad: bfloat16 [8192, 768], P(('dp', 'tensor')), may hold values from -6 to 6
Outputs:
- block_out: bfloat16 [8192, 768], P(('dp', 'tensor'))
- input_grad: float32 [8192, 768], P(('dp', 'tensor'))
- first_gain_grad: float32 [768], P(('dp', 'tensor'))
- first_shift_grad: float32 [768], P(('dp', 'tensor'))
- qkv_weight_grad: float32 [768, 3, 768], P('dp', None, 'tensor')
- attn_bias_grad: float32 [1536], P(('dp', 'tensor'))
- out_weight_grad: float32 [768, 768], P('tensor', 'dp')
- out_bias_grad: float32 [768], P(('dp', 'tensor'))
- second_gain_grad: float32 [768], P(('dp', 'tensor'))
- second_shift_grad: float32 [768], P(('dp', 'tensor'))
- fc_weight_grad: float32 [768, 3072], P('dp', 'tensor')
- fc_bias_grad: float32 [3072], P(('dp', 'tensor'))
- proj_weight_grad: float32 [3072, 768], P('tensor', 'dp')
- proj_bias_grad: float32 [768], P(('dp', 'tensor'))
The draws below stay inside these ranges and needn't reach their ends.
Inputs may be any that keep to these rules, and one draw needn't show every extreme that they name: `doc_lengths`: each row holds the lengths of its group's two documents in order; they sum to 1024, and one of them is longer than 768.
All inputs are finite; a program needn't handle non-finite values.
Results may differ from the reference program's by a relative error of at most 0.019.
Values may be sent and summed in bfloat16 or wider, within the bound.
No kernel may reach another device: no remote copies, remote signals or barrier semaphores. Data moves between devices by JAX's collectives and lax.ppermute only.
A program may use at most 128 MiB of HBM per device.

```python
import jax
import jax.numpy as jnp
from jax import lax

D = 768
HEADS = 12
HEAD_DIM = 64
FF = 3072
TOK_DEV = 256
GROUP = 1024
TOKENS = 8192
N_DP = 8
N_TENSOR = 4


def draw_doc_lengths(key, part):
    key = jax.random.fold_in(key, 11)
    key_long, key_order, key_full = jax.random.split(key, 3)
    longer = jax.random.randint(key_long, (N_DP,), 3 * TOK_DEV + 1, GROUP + 1)
    full_group = jax.random.randint(key_full, (), 0, N_DP)
    longer = jnp.where(jnp.arange(N_DP) == full_group, GROUP, longer)
    order_bits = jax.random.randint(key_order, (N_DP,), 0, 2)
    leading = jnp.where(order_bits == 1, longer, GROUP - longer)
    return jnp.stack([leading, GROUP - leading], axis=1).astype(jnp.int32)


def with_spikes(drawn, own_key, source, target, shards_of, factor):
    owner, partner = [(jnp.arange(drawn.shape[dim]) // (drawn.shape[dim] // shards_of)).reshape([-1 if axis == dim else 1 for axis in range(drawn.ndim)]) for dim in (source, target)]
    chosen = jax.random.permutation(own_key, shards_of)[partner]
    strong = (owner == chosen) | (owner == (partner + shards_of // 2) % shards_of)
    return jnp.where(strong, factor * drawn, drawn)


def levels(rng, extent, cuts, low, high):
    factor_of = 1.0
    for position, shards_of in cuts:
        steps = jax.random.uniform(jax.random.fold_in(jax.random.fold_in(rng, 6), position), (shards_of,), jnp.float32, low / len(cuts), high / len(cuts))
        factor_of = factor_of * jnp.repeat(jnp.exp(steps), extent[position] // shards_of).reshape((-1,) + (1,) * (len(extent) - 1 - position))
    return factor_of


def bell_draw(own_key, dims, scale, reach, pieces=(), held_as=jnp.bfloat16):
    loudness = levels(own_key, dims, pieces, -0.22, 0.18) if pieces else 1.0
    values = jax.random.normal(own_key, dims, jnp.float32) * scale * loudness
    return jnp.minimum(jnp.maximum(values, -reach), reach).astype(held_as)


def bell_draw_with(rng, shape, scale, bound, cuts, heavy, kind=jnp.bfloat16):
    values = scale * jax.random.normal(rng, shape, jnp.float32)
    if cuts:
        values = values * levels(rng, shape, cuts, -0.22, 0.18)
    return jnp.clip(with_spikes(values, jax.random.fold_in(rng, 3), *heavy), -bound, bound).astype(kind)


def setup_inputs(seed: int = 0) -> dict:
    streams_of = jax.random.split(jax.random.key(seed), 16)
    return {
        "block_input": bell_draw_with(streams_of[0], (TOKENS, D), 1.0, 6.0, ((0, 32),), (0, 1, 32, 2.75)),
        "doc_lengths": draw_doc_lengths(jax.random.fold_in(streams_of[15], 71), 0),
        "first_gain": jnp.clip(1.0 + 0.1 * jax.random.normal(streams_of[2], (D,), jnp.float32), 0.5, 1.5).astype(jnp.bfloat16),
        "first_shift": bell_draw(streams_of[3], (D,), 0.2, 1.0, ((0, 32),)),
        "qkv_weight": bell_draw(streams_of[4], (D, 3, D), D ** -0.5, 0.21875, ((0, 8), (2, 4))),
        "attn_bias": bell_draw(streams_of[5], (2 * D,), 0.3, 1.5, ((0, 32),)),
        "out_weight": bell_draw(streams_of[6], (D, D), (D * 4 // (TOK_DEV * N_TENSOR)) ** -0.5, 3.5, ((0, 4), (1, 8))),
        "out_bias": bell_draw(streams_of[7], (D,), 0.3, 1.5, ((0, 32),)),
        "second_gain": jnp.clip(1.0 + 0.1 * jax.random.normal(streams_of[8], (D,), jnp.float32), 0.5, 1.5).astype(jnp.bfloat16),
        "second_shift": bell_draw(streams_of[9], (D,), 0.2, 1.0, ((0, 32),)),
        "fc_weight": bell_draw(streams_of[10], (D, FF), D ** -0.5, 0.21875, ((0, 8), (1, 4))),
        "fc_bias": bell_draw(streams_of[11], (FF,), 0.3, 1.5, ((0, 32),)),
        "proj_weight": bell_draw(streams_of[12], (FF, D), FF ** -0.5, 0.109375, ((0, 4), (1, 8))),
        "proj_bias": bell_draw(streams_of[13], (D,), 0.3, 1.5, ((0, 32),)),
        "block_grad": bell_draw_with(streams_of[14], (TOKENS, D), 1.0, 6.0, ((0, 32),), (0, 1, 32, 2.75)),
    }


EPS = 1e-05
HIGH = lax.Precision.HIGHEST

@jax.custom_vjp
def low(v):
    return lax.optimization_barrier(v.astype(jnp.bfloat16)).astype(jnp.float32)

@jax.custom_vjp
def low_back(v):
    return v

def low_keep(v):
    return (low(v), None)

def low_pass(kept, grad):
    return (grad,)

def back_keep(v):
    return (v, None)

def back_low(kept, grad):
    return (low(grad),)
low.defvjp(low_keep, low_pass)
low_back.defvjp(back_keep, back_low)

def layer_norm(values, gain_vec, shift_vec):
    center = lax.optimization_barrier(jnp.mean(values, axis=-1, keepdims=True))
    offset = values - center
    spread = lax.rsqrt(lax.optimization_barrier(jnp.mean(offset * offset, axis=-1, keepdims=True)) + EPS)
    return offset * spread * gain_vec + shift_vec

def both_ways(values):
    return low(low_back(values))

def matmul(left, right):
    return jnp.dot(left, right, precision=HIGH)

def forward(inputs, params, boundary):
    first_gain, first_shift, qkv_weight, attn_bias, out_weight, out_bias, second_gain, second_shift, fc_weight, fc_bias, proj_weight, proj_bias = params
    row_count = inputs.shape[0]
    normed_one = low(layer_norm(inputs, first_gain, first_shift))
    queries = both_ways(matmul(normed_one, qkv_weight[:, 0, :]) + attn_bias[:D])
    key_rows = both_ways(matmul(normed_one, qkv_weight[:, 1, :]))
    value_rows = both_ways(matmul(normed_one, qkv_weight[:, 2, :]) + attn_bias[D:])
    head_shape = (row_count, HEADS, HEAD_DIM)
    scores = jnp.einsum('ihd,jhd->hij', queries.reshape(head_shape), key_rows.reshape(head_shape), precision=HIGH)
    scores = low_back(scores * HEAD_DIM ** (-0.5))
    positions = jnp.arange(row_count)
    second_doc = positions >= boundary
    allowed = (positions[None, :] <= positions[:, None]) & (second_doc[None, :] == second_doc[:, None])
    scores = jnp.where(allowed[None], scores, -jnp.inf)
    probs_low = low(jax.nn.softmax(scores, axis=-1))
    mixed_heads = jnp.einsum('hij,jhd->ihd', probs_low, value_rows.reshape(head_shape), precision=HIGH)
    mixed_heads = both_ways(mixed_heads.reshape(row_count, D))
    hidden = inputs + low_back(matmul(mixed_heads, out_weight) + out_bias)
    normed_two = low(layer_norm(hidden, second_gain, second_shift))
    pre_act = low_back(matmul(normed_two, fc_weight) + fc_bias)
    activated = low(jax.nn.gelu(pre_act, approximate=True))
    return hidden + low_back(matmul(activated, proj_weight) + proj_bias)

def reference(block_input, doc_lengths, first_gain, first_shift, qkv_weight, attn_bias, out_weight, out_bias, second_gain, second_shift, fc_weight, fc_bias, proj_weight, proj_bias, block_grad):
    params = tuple((param.astype(jnp.float32) for param in (first_gain, first_shift, qkv_weight, attn_bias, out_weight, out_bias, second_gain, second_shift, fc_weight, fc_bias, proj_weight, proj_bias)))
    inputs = block_input.astype(jnp.float32).reshape(N_DP, GROUP, D)
    grads_in = block_grad.astype(jnp.float32).reshape(N_DP, GROUP, D)

    def one_group(running, group_item):
        group_rows, group_grad, boundary = group_item
        result, pullback = jax.vjp(lambda rows_in, params_in: forward(rows_in, params_in, boundary), group_rows, params)
        row_grad, param_grads = pullback(group_grad)
        running = tuple((before + adding for before, adding in zip(running, param_grads)))
        return (running, (result, row_grad))
    initial = tuple((jnp.zeros_like(param) for param in params))
    totals, (outputs, row_grads) = lax.scan(one_group, initial, (inputs, grads_in, doc_lengths[:, 0]))
    return (outputs.reshape(TOKENS, D).astype(jnp.bfloat16), row_grads.reshape(TOKENS, D), totals[0], totals[1], totals[2], totals[3], totals[4], totals[5], totals[6], totals[7], totals[8], totals[9], totals[10], totals[11])
```

```python
import functools
import jax
import jax.numpy as jnp
from jax import lax
from jax.experimental import pallas as pl
from jax.experimental.pallas import tpu as pltpu
from jax.sharding import Mesh, PartitionSpec as P

HEAD_DIM = 64
EPS = 1e-05
F32, BF16 = jnp.float32, jnp.bfloat16
EVERY = ("chip", "core", "tensor")


def swap_bit(values, axis, mask):
    size = lax.axis_size(axis)
    return lax.ppermute(values, axis, [(i, i ^ mask) for i in range(size)])


def swap_core(values):
    return swap_bit(values, "core", 1)


def shift_tensor(values, step):
    size = lax.axis_size("tensor")
    return lax.ppermute(values, "tensor", [(i, (i + step) % size) for i in range(size)])


def after(values, *first):
    return lax.optimization_barrier((values, *first))[0]


def sort_pieces(pieces, offsets):
    rows = pieces[0].shape[0]
    out = jnp.zeros((rows * len(pieces),) + pieces[0].shape[1:], pieces[0].dtype)
    for piece, at in zip(pieces, offsets):
        out = lax.dynamic_update_slice_in_dim(out, piece, at * rows, 0)
    return out


def gather_chips(block):
    return lax.all_gather(block, "chip", axis=0, tiled=True)


def scatter_chips(full):
    arrived = lax.all_to_all(full, "chip", 0, 0, tiled=True)
    return arrived.astype(F32).sum(axis=0)


def norm_stats(values):
    center = jnp.mean(values, axis=-1, keepdims=True)
    offset = values - center
    spread = lax.rsqrt(jnp.mean(offset * offset, axis=-1, keepdims=True) + EPS)
    return offset * spread, spread


def norm_back(grad_out, unit_rows, spread, gain_vec):
    scaled = grad_out * gain_vec
    centred = scaled - jnp.mean(scaled, axis=-1, keepdims=True)
    centred = centred - unit_rows * jnp.mean(scaled * unit_rows, axis=-1, keepdims=True)
    return spread * centred


def gelu_tanh(values):
    return jax.nn.gelu(values, approximate=True)


def score_block(query_block, key_heads, block_start, boundary, score_scale):
    block_rows = query_block.shape[0]
    key_pos = jnp.arange(key_heads.shape[0])
    query_pos = block_start + jnp.arange(block_rows)
    allowed = (key_pos[None, :] <= query_pos[:, None]) & (
        (key_pos[None, :] >= boundary) == (query_pos[:, None] >= boundary)
    )
    scores = (
        jnp.einsum("ihd,jhd->hij", query_block, key_heads, preferred_element_type=F32)
        * score_scale
    )
    return jnp.where(allowed[None], scores, -jnp.inf)


def attend(query_heads, key_heads, value_heads, boundary, score_scale):
    row_count, heads_dev, head_dim = query_heads.shape
    block_rows = min(512, row_count)
    outputs, totals = [], []
    for block_start in range(0, row_count, block_rows):
        scores = score_block(
            query_heads[block_start : block_start + block_rows],
            key_heads, block_start, boundary, score_scale,
        )
        row_peak = jnp.max(scores, axis=-1, keepdims=True)
        log_total = row_peak + jnp.log(jnp.sum(jnp.exp(scores - row_peak), axis=-1, keepdims=True))
        probs_low = jnp.exp(scores - log_total).astype(BF16)
        mixed_block = jnp.einsum("hij,jhd->ihd", probs_low, value_heads, preferred_element_type=F32)
        outputs.append(mixed_block.reshape(block_rows, heads_dev * head_dim).astype(BF16))
        totals.append(log_total)
    return jnp.concatenate(outputs, axis=0), totals


def attend_back(query_heads, key_heads, value_heads, totals, grad_heads, boundary, score_scale):
    row_count = query_heads.shape[0]
    block_rows = min(512, row_count)
    query_grads = []
    key_acc = jnp.zeros(key_heads.shape, F32)
    value_acc = jnp.zeros(value_heads.shape, F32)
    for block_index, block_start in enumerate(range(0, row_count, block_rows)):
        query_block = query_heads[block_start : block_start + block_rows]
        grad_block = grad_heads[block_start : block_start + block_rows]
        scores = score_block(query_block, key_heads, block_start, boundary, score_scale)
        probs = jnp.exp(scores - totals[block_index])
        probs_low = probs.astype(BF16)
        prob_grads = jnp.einsum("ihd,jhd->hij", grad_block, value_heads, preferred_element_type=F32)
        row_dot = jnp.sum(probs * prob_grads, axis=-1, keepdims=True)
        score_grads = (probs * (prob_grads - row_dot)).astype(BF16)
        query_grads.append(
            jnp.einsum("hij,jhd->ihd", score_grads, key_heads, preferred_element_type=F32) * score_scale
        )
        key_acc = key_acc + jnp.einsum("hij,ihd->jhd", score_grads, query_block, preferred_element_type=F32)
        value_acc = value_acc + jnp.einsum("hij,ihd->jhd", probs_low, grad_block, preferred_element_type=F32)
    return jnp.concatenate(query_grads, axis=0), key_acc * score_scale, value_acc


def body(
    block_input, doc_lengths, first_gain, first_shift, qkv_weight, attn_bias, out_weight, out_bias,
    second_gain, second_shift, fc_weight, fc_bias, proj_weight, proj_bias, block_grad,
):
    n_tensor = lax.axis_size("tensor")
    n_chip = lax.axis_size("chip")
    n_dev = n_tensor * n_chip * 2
    rank = lax.axis_index("tensor")
    core = lax.axis_index("core")
    tok, width = block_input.shape
    boundary = doc_lengths[0, 0]

    small = [first_gain, first_shift, attn_bias, out_bias, second_gain, second_shift, fc_bias, proj_bias]
    small_flat = jnp.concatenate(small)
    small_all = lax.all_to_all(
        jnp.broadcast_to(small_flat[None], (n_dev,) + small_flat.shape), EVERY, 0, 0, tiled=True
    ).astype(F32)
    params, at = [], 0
    for p in small:
        params.append(small_all[:, at : at + p.shape[0]].reshape(-1))
        at += p.shape[0]
    gain_one, shift_one, attn_shift, out_shift, gain_two, shift_two, fc_shift, proj_shift = params

    def ffn_rows(shard):
        rows, cols = shard.shape
        half = cols // 2
        mine = lax.dynamic_slice_in_dim(shard, core * half, half, 1)
        other = swap_core(lax.dynamic_slice_in_dim(shard, (1 - core) * half, half, 1))
        first = jnp.where(core == 0, mine, other)
        last = jnp.where(core == 0, other, mine)
        return jnp.concatenate([first, last], axis=0)

    def tensor_pieces(block):
        return [block] + [swap_bit(block, "tensor", m) for m in range(1, n_tensor)]

    fc_block = jnp.concatenate(tensor_pieces(ffn_rows(fc_weight)), axis=1)
    fc_full = gather_chips(fc_block)

    width_dev = qkv_weight.shape[2]
    out_t = out_weight.T
    out_block = jnp.concatenate(tensor_pieces(out_t), axis=1)
    attn_block = jnp.concatenate([qkv_weight.reshape(-1, 3 * width_dev), out_block], axis=1)
    rows_dev = attn_block.shape[0]
    attn_chips = gather_chips(attn_block).reshape(n_chip, rows_dev, -1)
    attn_other = swap_core(attn_chips)
    attn_pair = jnp.where(core == 0, jnp.stack([attn_chips, attn_other], 1), jnp.stack([attn_other, attn_chips], 1))
    attn_full = attn_pair.reshape(width, -1)
    qkv_full, out_full = attn_full[:, : 3 * width_dev], attn_full[:, 3 * width_dev :]

    half = tok // 2
    cur = [block_input[:half], block_input[half:]]
    pieces = [block_input]
    for step in range(1, n_tensor):
        cur = [shift_tensor(c, 1) for c in cur]
        pieces.append(jnp.concatenate(cur, axis=0))
    rows_in = sort_pieces(pieces, [(rank - s) % n_tensor for s in range(n_tensor)])

    proj_block = after(proj_weight.T, pieces[-1])
    proj_block = jnp.concatenate(tensor_pieces(ffn_rows(proj_block)), axis=1)
    proj_full = gather_chips(proj_block)

    unit_rows, _ = norm_stats(rows_in.astype(F32))
    normed_one = (unit_rows * gain_one + shift_one).astype(BF16)
    row_count = normed_one.shape[0]
    heads_dev = width_dev // HEAD_DIM
    score_scale = HEAD_DIM ** (-0.5)
    projected = jnp.dot(normed_one, qkv_full, preferred_element_type=F32).reshape(row_count, 3, width_dev)
    query_shift = lax.dynamic_slice_in_dim(attn_shift, rank * width_dev, width_dev)
    value_shift = lax.dynamic_slice_in_dim(attn_shift, width + rank * width_dev, width_dev)
    head_shape = (row_count, heads_dev, HEAD_DIM)
    queries = (projected[:, 0] + query_shift).astype(BF16).reshape(head_shape)
    key_rows = projected[:, 1].astype(BF16).reshape(head_shape)
    value_rows = (projected[:, 2] + value_shift).astype(BF16).reshape(head_shape)
    mixed_heads, totals = attend(queries, key_rows, value_rows, boundary, score_scale)

    def to_tokens(block_of):
        return jnp.concatenate(
            [block_of(rank)] + [swap_bit(block_of(rank ^ m), "tensor", m) for m in range(1, n_tensor)], axis=1
        )

    mixed = to_tokens(lambda z: lax.dynamic_slice_in_dim(mixed_heads, z * tok, tok, 0))

    inputs = block_input.astype(F32)
    attn_out = lax.dot_general(mixed, out_full, (((1,), (1,)), ((), ())), preferred_element_type=F32)
    hidden = inputs + (attn_out + out_shift)
    unit_two, spread_two = norm_stats(hidden)
    normed_two = (unit_two * gain_two + shift_two).astype(BF16)

    rows_two = jnp.concatenate([normed_two, swap_core(normed_two)], axis=0)
    rows_grad = jnp.concatenate([block_grad, swap_core(block_grad)], axis=0)
    fc_cols = fc_shift.reshape(n_tensor, 2, -1)
    fc_cols = lax.dynamic_index_in_dim(fc_cols, core, 1, False)
    fc_cols = jnp.stack([lax.dynamic_index_in_dim(fc_cols, rank ^ m, 0, False) for m in range(n_tensor)])
    pre_act = jnp.dot(rows_two, fc_full, preferred_element_type=F32) + fc_cols.reshape(-1)
    gelu_values, gelu_pull = jax.vjp(gelu_tanh, pre_act)
    activated = gelu_values.astype(BF16)
    act_grad = jnp.dot(rows_grad, proj_full, preferred_element_type=F32)
    pre_grad = gelu_pull(act_grad)[0].astype(BF16)
    n2g_part = lax.dot_general(pre_grad, fc_full, (((1,), (1,)), ((), ())), preferred_element_type=F32)
    normed_two_grad = n2g_part[:tok] + swap_core(n2g_part[tok:].astype(BF16)).astype(F32)
    mlp_part = lax.dot_general(activated, proj_full, (((1,), (1,)), ((), ())), preferred_element_type=F32)
    mlp_out = mlp_part[:tok] + swap_core(mlp_part[tok:].astype(BF16)).astype(F32)
    block_out = (hidden + (mlp_out + proj_shift)).astype(BF16)

    top_grad = block_grad.astype(F32)
    hidden_grad = top_grad + norm_back(normed_two_grad, unit_two, spread_two, gain_two)
    attn_grad = hidden_grad.astype(BF16)

    heads_grad = jnp.dot(attn_grad, out_full, preferred_element_type=F32).astype(BF16)
    grad_pieces = [heads_grad[:, m * width_dev : (m + 1) * width_dev] for m in range(n_tensor)]
    grad_pieces = [grad_pieces[0]] + [swap_bit(grad_pieces[m], "tensor", m) for m in range(1, n_tensor)]
    heads_rows = sort_pieces(grad_pieces, [rank ^ m for m in range(n_tensor)])

    def ffn_scatter(partial):
        cols = partial.shape[1]
        block = scatter_chips(partial.reshape(n_chip, -1, cols))
        part = cols // n_tensor
        total = block[:, :part]
        for m in range(1, n_tensor):
            total = total + swap_bit(block[:, m * part : (m + 1) * part].astype(BF16), "tensor", m).astype(F32)
        rows = total.shape[0] // 2
        mine = lax.dynamic_slice_in_dim(total, core * rows, rows, 0)
        other = swap_core(lax.dynamic_slice_in_dim(total, (1 - core) * rows, rows, 0))
        first = jnp.where(core == 0, mine, other)
        last = jnp.where(core == 0, other, mine)
        return jnp.concatenate([first, last], axis=1)

    proj_grad = lax.dot_general(rows_grad, activated, (((0,), (0,)), ((), ())), preferred_element_type=F32)
    proj_weight_grad = ffn_scatter(proj_grad.astype(BF16)).T
    fc_grad = lax.dot_general(rows_two, pre_grad, (((0,), (0,)), ((), ())), preferred_element_type=F32)
    fc_weight_grad = ffn_scatter(fc_grad.astype(BF16))

    def core_scatter(partial):
        cols = partial.shape[1]
        split = partial.reshape(n_chip, 2, -1, cols)
        keep = lax.dynamic_index_in_dim(split, core, 1, False)
        send = lax.dynamic_index_in_dim(split, 1 - core, 1, False)
        return keep.astype(F32) + swap_core(send.astype(BF16)).astype(F32)

    out_grad = lax.dot_general(attn_grad, mixed, (((0,), (0,)), ((), ())), preferred_element_type=F32)
    out_block_grad = scatter_chips(core_scatter(out_grad).astype(BF16))
    out_total = out_block_grad[:, :width_dev]
    for m in range(1, n_tensor):
        piece = out_block_grad[:, m * width_dev : (m + 1) * width_dev].astype(BF16)
        out_total = out_total + swap_bit(piece, "tensor", m).astype(F32)
    out_weight_grad = out_total.T

    query_grad, key_grad, value_grad = attend_back(
        queries, key_rows, value_rows, totals, heads_rows.reshape(head_shape), boundary, score_scale
    )
    flat_shape = (row_count, width_dev)
    query_low = query_grad.reshape(flat_shape).astype(BF16)
    key_low = key_grad.reshape(flat_shape).astype(BF16)
    value_low = value_grad.reshape(flat_shape).astype(BF16)
    projection_grads = jnp.concatenate([query_low, key_low, value_low], axis=1)
    n1g_part = lax.dot_general(projection_grads, qkv_full, (((1,), (1,)), ((), ())), preferred_element_type=F32)
    n1g_blocks = n1g_part.reshape(n_tensor, tok, width)

    def part_block(z):
        return lax.dynamic_index_in_dim(n1g_blocks, z % n_tensor, 0, False)

    running = part_block(rank - 1)
    acc = [running[:half], running[half:]]
    for step in range(1, n_tensor):
        mine = part_block(rank - 1 - step)
        acc = [
            shift_tensor(a.astype(BF16), 1).astype(F32) + m
            for a, m in zip(acc, (mine[:half], mine[half:]))
        ]
    normed_one_grad = jnp.concatenate(acc, axis=0)

    first_gain_grad = jnp.sum(n1g_part * unit_rows, axis=0)
    first_shift_grad = jnp.sum(n1g_part, axis=0)
    zeros = jnp.zeros((2 * width,), F32)
    attn_bias_grad = lax.dynamic_update_slice_in_dim(
        zeros, jnp.sum(query_low.astype(F32), axis=0), rank * width_dev, 0
    )
    attn_bias_grad = lax.dynamic_update_slice_in_dim(
        attn_bias_grad, jnp.sum(value_low.astype(F32), axis=0), width + rank * width_dev, 0
    )
    out_bias_grad = jnp.sum(attn_grad.astype(F32), axis=0)
    second_gain_grad = jnp.sum(normed_two_grad * unit_two, axis=0)
    second_shift_grad = jnp.sum(normed_two_grad, axis=0)
    proj_bias_grad = jnp.sum(top_grad, axis=0)
    fc_sums = jnp.sum(pre_grad.astype(F32), axis=0).reshape(n_tensor, -1)
    fc_bias_grad = jnp.zeros((n_tensor, 2, fc_sums.shape[1]), F32)
    for m in range(n_tensor):
        fc_bias_grad = lax.dynamic_update_slice(fc_bias_grad, fc_sums[m][None, None], (rank ^ m, core, 0))
    fc_bias_grad = fc_bias_grad.reshape(-1)

    smalls = [
        first_gain_grad, first_shift_grad, attn_bias_grad, out_bias_grad,
        second_gain_grad, second_shift_grad, fc_bias_grad, proj_bias_grad,
    ]
    small_grads = jnp.concatenate([g.reshape(n_dev, -1) for g in smalls], axis=1)
    small_grads = lax.all_to_all(small_grads, EVERY, 0, 0, tiled=True).sum(axis=0)
    small_outs, at = [], 0
    for g in smalls:
        n = g.shape[0] // n_dev
        small_outs.append(small_grads[at : at + n])
        at += n

    qkv_grad = lax.dot_general(normed_one, projection_grads, (((0,), (0,)), ((), ())), preferred_element_type=F32)
    qkv_weight_grad = scatter_chips(core_scatter(qkv_grad).astype(BF16)).reshape(qkv_weight.shape)

    own_unit, own_spread = norm_stats(inputs)
    input_grad = hidden_grad + norm_back(normed_one_grad, own_unit, own_spread, gain_one)
    return (
        block_out, input_grad, small_outs[0], small_outs[1], qkv_weight_grad, small_outs[2], out_weight_grad,
        small_outs[3], small_outs[4], small_outs[5], fc_weight_grad, small_outs[6], proj_weight_grad, small_outs[7],
    )


def pcall(kernel, outs, scratch=(), n_scalar=0, n_in=0, us=2):
    whole = pl.BlockSpec(memory_space=pltpu.VMEM)
    return pl.pallas_call(
        kernel,
        in_specs=[pl.BlockSpec(memory_space=pltpu.SMEM)] * n_scalar + [whole] * n_in,
        out_specs=[whole] * len(outs),
        out_shape=[jax.ShapeDtypeStruct(s, d) for s, d in outs],
        scratch_shapes=list(scratch),
        cost_estimate=pl.CostEstimate(flops=1, bytes_accessed=1, transcendentals=0),
        compiler_params=pltpu.CompilerParams(vmem_limit_bytes=56 * 1024 * 1024),
    )


def dg(a, b, ca, cb):
    return lax.dot_general(a, b, (((ca,), (cb,)), ((), ())), preferred_element_type=F32)


def prep_kernel(sizes, scal, fc, proj, out_w, *refs):
    ins, (mine, other, block, tile) = refs[: len(sizes)], refs[len(sizes) :]
    core = scal[2]
    half = mine.shape[2]
    rows = fc.shape[0]
    flipped = proj[...].T
    for to, side in ((mine, core), (other, 1 - core)):
        to[0] = fc[:, pl.ds(pl.multiple_of(side * half, 128), half)]
        first, last = flipped[:, 0:half], flipped[:, half:]
        to[1] = jnp.where(side == 0, first, last)
    tile[...] = jnp.zeros_like(tile)
    for i, n in enumerate(sizes):
        tile[i : i + 1, 0:n] = ins[i][...].astype(F32)
    block[0:rows, :] = out_w[...].T
    block[rows:, :] = tile[...].astype(BF16)


def spread(n, cols):
    lane = lax.broadcasted_iota(jnp.int32, (128, cols), 1).astype(F32)
    row = lax.broadcasted_iota(jnp.int32, (128, cols), 0).astype(F32)
    rest = lane - n * jnp.floor((lane + 0.5) * (1.0 / n))
    return jnp.where(rest == row, 1.0, 0.0)


def owner(n, rows, cols):
    lane = lax.broadcasted_iota(jnp.int32, (rows, cols), 1)
    first = lax.broadcasted_iota(jnp.int32, (rows, cols), 0) * n
    return (lane >= first) & (lane < first + n)


def unpack_kernel(sizes, n_t, scal, mine, other, *refs):
    outs, every = refs[:-1], refs[-1]
    rank, chip, core = scal[0], scal[1], scal[2]
    n_dev = every.shape[0]
    rows = mine.shape[1] - 16
    wide = outs[2].shape[1]
    for m in range(4):
        for j, ref in ((0, mine), (1, other)):
            for s in range(n_t):
                at = ((chip ^ m) * 2 + (core ^ j)) * n_t + (rank ^ s)
                every[at] = ref[m, rows : rows + 16, s * wide : s * wide + 128].astype(F32)[0:8]
    values = every[...]
    cached = {}
    for i, n in enumerate(sizes):
        cols = n * n_dev
        if n not in cached:
            cached[n] = (spread(n, cols).astype(BF16), owner(n, n_dev, cols))
        full = jnp.dot(values[:, i, :].astype(BF16), cached[n][0], preferred_element_type=F32)
        full = jnp.sum(jnp.where(cached[n][1], full, 0.0), axis=0, keepdims=True)
        lanes = outs[i].shape[1]
        for r in range(outs[i].shape[0]):
            outs[i][r : r + 1, :] = full[:, r * lanes : (r + 1) * lanes]


def pack_kernel(sizes, *refs):
    ins, out = refs[: len(sizes)], refs[len(sizes)]
    n_dev = out.shape[0]
    cached = {}
    for i, n in enumerate(sizes):
        cols = n * n_dev
        if n not in cached:
            cached[n] = (spread(n, cols), owner(n, n_dev, cols))
        rows = jnp.where(cached[n][1], ins[i][...], 0.0)
        out[:, i, :] = lax.dot_general(
            rows, cached[n][0], (((1,), (1,)), ((), ())),
            precision=lax.Precision.HIGHEST, preferred_element_type=F32,
        )


def finish_kernel(sizes, all_ref, *outs):
    total = jnp.sum(all_ref[...], axis=0)
    for i, n in enumerate(sizes):
        outs[i][...] = total[i : i + 1, 0:n]


def row_stats(values):
    center = jnp.mean(values, axis=-1, keepdims=True)
    offset = values - center
    spread_rows = lax.rsqrt(jnp.mean(offset * offset, axis=-1, keepdims=True) + EPS)
    return offset * spread_rows, spread_rows


def mask_of(boundary, first, block, keys):
    qpos = first + lax.broadcasted_iota(jnp.int32, (keys, block), 1)
    kpos = lax.broadcasted_iota(jnp.int32, (keys, block), 0)
    low = jnp.where(qpos >= boundary, boundary, 0)
    return (kpos >= low) & (kpos <= qpos)


LOG2E = 1.4426950408889634


def attn_kernel(n_t, heads, *refs):
    (scal,) = refs[:1]
    own, two, odd = refs[1:4]
    at = 4
    stacks = refs[at : at + 2]
    gain, shift, bias = refs[at + 2 : at + 5]
    outs = refs[at + 5 :]
    q_o, k_o, v_o, lse_o, normed_o, unit_o, w_o = outs[:7]
    send = outs[7 : 7 + n_t]
    mixed = outs[7 + n_t]
    rank, chip, core, boundary = scal[0], scal[1], scal[2], scal[3]
    tok, width = own.shape
    wide = w_o.shape[1]
    rows_dev = stacks[0].shape[1] - 16
    for m in range(4):
        for j in range(2):
            to = pl.multiple_of(((chip ^ m) * 2 + (core ^ j)) * rows_dev, 16)
            w_o[pl.ds(to, rows_dev), :] = stacks[j][m, 0:rows_dev, width : width + wide]

    def put(values, to):
        unit, _ = row_stats(values.astype(F32))
        unit_o[pl.ds(to, values.shape[0]), :] = unit.astype(BF16)
        normed_o[pl.ds(to, values.shape[0]), :] = (unit * gain[...] + shift[...]).astype(BF16)

    put(own[...], pl.multiple_of(rank * tok, tok))
    put(two[...], pl.multiple_of((rank ^ 2) * tok, tok))
    put(odd[0], pl.multiple_of((rank ^ 1) * tok, tok))
    put(odd[1], pl.multiple_of((rank ^ 3) * tok, tok))
    third = wide // 3
    qb = bias[pl.ds(rank, 1), :]
    vb = bias[pl.ds(n_t + rank, 1), :]
    projected = jnp.dot(normed_o[...], w_o[...], preferred_element_type=F32)
    zero = jnp.zeros_like(qb)
    full_bias = jnp.concatenate([qb, zero, vb], axis=1)
    flipped = (projected + full_bias).astype(BF16).T
    q_o[...] = flipped[0:third]
    k_o[...] = flipped[third : 2 * third]
    v_o[...] = flipped[2 * third : 3 * third]
    lse_o[...] = jnp.zeros_like(lse_o)
    masks = [mask_of(boundary, b * tok, tok, (b + 1) * tok) for b in range(n_t)]
    for h in range(heads):
        lo, hi = h * HEAD_DIM, (h + 1) * HEAD_DIM
        keys = k_o[lo:hi, :].T
        for b in range(n_t):
            n = (b + 1) * tok
            cols = slice(b * tok, n)
            scores = dg(keys[0:n], q_o[lo:hi, cols], 1, 0) * (HEAD_DIM**-0.5 * LOG2E)
            scores = jnp.where(masks[b], scores, -jnp.inf)
            peak = jnp.max(scores, axis=0, keepdims=True)
            probs = jnp.exp2(scores - peak)
            total = jnp.sum(probs, axis=0, keepdims=True)
            lse_o[h : h + 1, cols] = peak + jnp.log2(total)
            out = jnp.dot(v_o[lo:hi, 0:n], probs.astype(BF16), preferred_element_type=F32)
            mixed[b, lo:hi, :] = (out * (1.0 / total)).astype(BF16)
    for s in range(n_t):
        send[s][...] = mixed[rank ^ s]


def mid_kernel(n_t, *refs):
    scal = refs[0]
    blocks = refs[1 : 1 + n_t]
    stacks = refs[1 + n_t : 3 + n_t]
    x, bias, gain, shift = refs[3 + n_t : 7 + n_t]
    hidden_o, normed_o, mixed_o, w_o = refs[7 + n_t :]
    chip, core = scal[1], scal[2]
    width = x.shape[1]
    rows_dev = stacks[0].shape[1] - 16
    for m in range(4):
        for j in range(2):
            to = pl.multiple_of(((chip ^ m) * 2 + (core ^ j)) * rows_dev, 16)
            w_o[pl.ds(to, rows_dev), :] = stacks[j][m, 0:rows_dev, 0:width]
    k = blocks[0].shape[0]
    for s in range(n_t):
        mixed_o[s * k : (s + 1) * k, :] = blocks[s][...]
    attn = dg(mixed_o[...], w_o[...], 0, 1)
    hidden = x[...].astype(F32) + (attn + bias[...])
    hidden_o[...] = hidden
    unit, _ = row_stats(hidden)
    normed_o[...] = (unit * gain[...] + shift[...]).astype(BF16)


def ffn_kernel(n_t, *refs):
    scal = refs[0]
    own, other, g_own, g_other, bias = refs[1:6]
    pairs, rest = refs[6:10], (refs[10:14], refs[14:18])
    outs = refs[18:]
    pieces = [[p.at[s] for p in pairs] for s in range(2)] + [list(r) for r in rest]
    own_o, send_o, act_o, pre_o, sums_o, x_s, g_s, fc_s, pj_s, mlp_s, n2_s = outs
    rank, chip, core = scal[0], scal[1], scal[2]
    tok = own.shape[0]
    x_s[0:tok] = own[...]
    x_s[tok:] = other[...]
    g_s[0:tok] = g_own[...]
    g_s[tok:] = g_other[...]
    cols = pieces[2][0].shape[3]
    rows = pieces[2][0].shape[2]
    c0 = 0.7978845608028654
    sums_o[...] = jnp.zeros_like(sums_o)
    for s in range(n_t):
        for w, to_ref in ((0, fc_s), (1, pj_s)):
            for m in range(4):
                for j in range(2):
                    to = pl.multiple_of(((chip ^ m) * 2 + (core ^ j)) * rows, 16)
                    to_ref[pl.ds(to, rows), :] = pieces[s][m][j, w]
        fc_w, pj_w = fc_s[...], pj_s[...]
        lanes = slice(s * cols, (s + 1) * cols)
        b = bias[pl.ds((rank ^ s) * 2 + core, 1), :]
        z = jnp.dot(x_s[...], fc_w, preferred_element_type=F32) + b
        ga = jnp.dot(g_s[...], pj_w, preferred_element_type=F32)
        zz = z * z
        t = jnp.tanh(z * (c0 + (c0 * 0.044715) * zz))
        up = 0.5 + 0.5 * t
        act = (z * up).astype(BF16)
        slope = up + (0.5 * z) * (1.0 - t * t) * (c0 + (3.0 * c0 * 0.044715) * zz)
        pre = (ga * slope).astype(BF16)
        act_o[:, lanes] = act
        pre_o[:, lanes] = pre
        sums_o[pl.ds((rank ^ s) * 2 + core, 1), :] = jnp.sum(pre.astype(F32), axis=0, keepdims=True)
        mlp = dg(act, pj_w, 1, 1)
        n2 = dg(pre, fc_w, 1, 1)
        if s == 0:
            mlp_s[...] = mlp
            n2_s[...] = n2
        else:
            mlp_s[...] += mlp
            n2_s[...] += n2
    for i, ref in ((0, mlp_s), (1, n2_s)):
        own_o[i] = ref[0:tok]
        send_o[i] = ref[tok:].astype(BF16)


def ffn_grads_kernel(n_t, *refs):
    scal, own, other, g_own, g_other, act, pre = refs[:7]
    fc_keep, fc_send, pj_keep, pj_send, x_s, g_s, tmp = refs[7:]
    chip, core = scal[1], scal[2]
    tok = own.shape[0]
    x_s[0:tok] = own[...]
    x_s[tok:] = other[...]
    g_s[0:tok] = g_own[...]
    g_s[tok:] = g_other[...]
    cols = fc_keep.shape[3]
    rows = fc_keep.shape[2] // 2
    for w, (left, right, keep, send, keep_m, send_m) in enumerate((
        (g_s, act, pj_keep, pj_send, (0, 1), (2, 3)),
        (x_s, pre, fc_keep, fc_send, (0, 2), (1, 3)),
    )):
        for s in range(n_t):
            tmp[...] = dg(left[...], right[:, s * cols : (s + 1) * cols], 0, 0).astype(BF16)
            for to, ms in ((keep, keep_m), (send, send_m)):
                for i, m in enumerate(ms):
                    for j in range(2):
                        at = pl.multiple_of(((chip ^ m) * 2 + (core ^ j)) * rows, 16)
                        to[i, s, j * rows : (j + 1) * rows] = tmp[pl.ds(at, rows), :]


def back_mid_kernel(n_t, *refs):
    kept, got, hidden, grad, w, gain, proj_bias = refs[:7]
    block_out, hg_o, attn_o, gain_o, shift_o, outb_o, projb_o = refs[7:14]
    blocks = refs[14 : 14 + n_t]
    hid = hidden[...]
    top = grad[...].astype(F32)
    g = kept[1] + got[1].astype(F32)
    unit, spread_rows = row_stats(hid)
    gain_o[...] = jnp.sum(g * unit, axis=0, keepdims=True)
    shift_o[...] = jnp.sum(g, axis=0, keepdims=True)
    projb_o[...] = jnp.sum(top, axis=0, keepdims=True)
    scaled = g * gain[...]
    centred = scaled - jnp.mean(scaled, axis=-1, keepdims=True)
    centred = centred - unit * jnp.mean(scaled * unit, axis=-1, keepdims=True)
    hg = top + spread_rows * centred
    hg_o[...] = hg
    low = hg.astype(BF16)
    attn_o[...] = low
    outb_o[...] = jnp.sum(low.astype(F32), axis=0, keepdims=True)
    heads = dg(w[...], low, 0, 1).astype(BF16)
    k = blocks[0].shape[0]
    for s in range(n_t):
        blocks[s][...] = heads[s * k : (s + 1) * k]
    block_out[...] = (hid + (kept[0] + got[0].astype(F32) + proj_bias[...])).astype(BF16)


def attn_back_kernel(n_t, heads, *refs):
    scal, q, k, v, lse, unit, w = refs[:7]
    grads = refs[7 : 7 + n_t]
    outs = refs[7 + n_t :]
    p_o = outs[:n_t]
    dqkv_o, gain_o, shift_o, bias_o, g_s, dk_s, dv_s, n1_s = outs[n_t:]
    rank, boundary = scal[0], scal[3]
    tok = grads[0].shape[1]
    third = q.shape[0]
    for s in range(n_t):
        g_s[rank ^ s] = grads[s][...]
    masks = [mask_of(boundary, b * tok, tok, (b + 1) * tok) for b in range(n_t)]
    scale = HEAD_DIM**-0.5
    for h in range(heads):
        lo, hi = h * HEAD_DIM, (h + 1) * HEAD_DIM
        keys = k[lo:hi, :].T
        vals = v[lo:hi, :].T
        dk_s[...] = jnp.zeros_like(dk_s)
        dv_s[...] = jnp.zeros_like(dv_s)
        for b in range(n_t):
            n = (b + 1) * tok
            cols = slice(b * tok, n)
            qb = q[lo:hi, cols]
            gb = g_s[b, lo:hi, :]
            scores = dg(keys[0:n], qb, 1, 0) * (scale * LOG2E)
            probs = jnp.exp2(jnp.where(masks[b], scores - lse[h : h + 1, cols], -jnp.inf))
            pg = dg(vals[0:n], gb, 1, 0)
            dot = jnp.sum(probs * pg, axis=0, keepdims=True)
            ds = (probs * (pg - dot)).astype(BF16)
            low = probs.astype(BF16)
            dq = jnp.dot(k[lo:hi, 0:n], ds, preferred_element_type=F32) * scale
            dqkv_o[lo:hi, cols] = dq.astype(BF16)
            dk_s[:, 0:n] += dg(qb, ds, 1, 1)
            dv_s[:, 0:n] += dg(gb, low, 1, 1)
        dqkv_o[third + lo : third + hi, :] = (dk_s[...] * scale).astype(BF16)
        dqkv_o[2 * third + lo : 2 * third + hi, :] = dv_s[...].astype(BF16)
    flat = dqkv_o[...]
    n1 = dg(flat, w[...], 0, 1)
    n1_s[...] = n1.reshape(n1_s.shape)
    gain_o[...] = jnp.sum(n1 * unit[...].astype(F32), axis=0, keepdims=True)
    shift_o[...] = jnp.sum(n1, axis=0, keepdims=True)
    ones = jnp.ones((8, flat.shape[1]), BF16)
    sums = dg(ones, flat, 1, 1)
    bias_o[...] = jnp.zeros_like(bias_o)
    bias_o[pl.ds(rank, 1), :] = sums[0:1, 0:third]
    bias_o[pl.ds(n_t + rank, 1), :] = sums[0:1, 2 * third : 3 * third]
    p_o[0][...] = n1_s[rank]
    for s in range(1, n_t):
        p_o[s][...] = n1_s[rank ^ s].astype(BF16)


def dp_grads_kernel(scal, attn_grad, mixed, normed, dqkv, keep_o, send_o, out_s, qkv_s):
    chip, core = scal[1], scal[2]
    rows = keep_o.shape[1]
    width = out_s.shape[1]
    out_s[...] = dg(attn_grad[...], mixed[...], 0, 1).astype(BF16)
    qkv_s[...] = dg(normed[...], dqkv[...], 0, 1).astype(BF16)
    for m in range(4):
        for j, to in ((0, keep_o), (1, send_o)):
            at = pl.multiple_of(((chip ^ m) * 2 + (core ^ j)) * rows, 16)
            to[m, :, 0:width] = out_s[pl.ds(at, rows), :]
            to[m, :, width:] = qkv_s[pl.ds(at, rows), :]


def dp_core_kernel(keep, got, own_o, *sends):
    for m in range(4):
        total = keep[m].astype(F32) + got[m].astype(F32)
        if m == 0:
            own_o[...] = total
        else:
            sends[m - 1][...] = total.astype(BF16)


def dp_chip_kernel(n_t, own, *refs):
    got, (qkv_o, out_o), sends = refs[:3], refs[3:5], refs[5:]
    total = own[...]
    for r in got:
        total = total + r[...].astype(F32)
    k = out_o.shape[1]
    qkv_o[...] = total[:, n_t * k :]
    out_o[...] = total[:, 0:k]
    for s in range(1, n_t):
        sends[s - 1][...] = total[:, s * k : (s + 1) * k].astype(BF16)


def dp_last_kernel(n_t, own, *refs):
    total = own[...]
    for r in refs[: n_t - 1]:
        total = total + r[...].astype(F32)
    refs[n_t - 1][...] = total.T


def chips_one_kernel(fc_keep, fc_got, pj_keep, pj_got, base_o, fc_send, pj_send):
    for w, (keep, got, send) in enumerate(((fc_keep, fc_got, fc_send), (pj_keep, pj_got, pj_send))):
        base_o[w] = keep[0].astype(F32) + got[0].astype(F32)
        send[...] = (keep[1].astype(F32) + got[1].astype(F32)).astype(BF16)


def chips_two_kernel(n_t, base, fc_got, pj_got, own_o, *sends):
    for w, got in enumerate((fc_got, pj_got)):
        own_o[w] = base[w, 0] + got[0].astype(F32)
        for s in range(1, n_t):
            sends[s - 1][w] = (base[w, s] + got[s].astype(F32)).astype(BF16)


def tensor_sum_kernel(n_t, own, *refs):
    mine_o, send_o = refs[n_t - 1 :]
    rows = mine_o.shape[1]
    total = own[...]
    for r in refs[: n_t - 1]:
        total = total + r[...].astype(F32)
    mine_o[...] = total[:, 0:rows]
    send_o[...] = total[:, rows:].astype(BF16)


def ffn_last_kernel(scal, mine, got, fc_o, pj_o):
    first = scal[2] == 0
    for w in range(2):
        a, b = mine[w], got[w].astype(F32)
        total = jnp.concatenate([jnp.where(first, a, b), jnp.where(first, b, a)], axis=1)
        if w == 0:
            fc_o[...] = total
        else:
            pj_o[...] = total.T


def last_kernel(n_t, *refs):
    mine, got, (x, hg, gain, out) = refs[0], refs[1:n_t], refs[n_t:]
    g = mine[...]
    for r in got:
        g = g + r[...].astype(F32)
    unit, spread_rows = row_stats(x[...].astype(F32))
    scaled = g * gain[...]
    centred = scaled - jnp.mean(scaled, axis=-1, keepdims=True)
    centred = centred - unit * jnp.mean(scaled * unit, axis=-1, keepdims=True)
    out[...] = hg[...] + spread_rows * centred


def fence(*values):
    return lax.optimization_barrier(values)


def body_four(
    block_input, doc_lengths, first_gain, first_shift, qkv_weight, attn_bias, out_weight, out_bias,
    second_gain, second_shift, fc_weight, fc_bias, proj_weight, proj_bias, block_grad,
):
    n_t = lax.axis_size("tensor")
    n_dev = n_t * 8
    rank, core, chip = lax.axis_index("tensor"), lax.axis_index("core"), lax.axis_index("chip")
    tok, width = block_input.shape
    half = tok // 2
    group = tok * n_t
    width_dev = qkv_weight.shape[2]
    heads = width_dev // HEAD_DIM
    rows_dev = qkv_weight.shape[0]
    hid = fc_weight.shape[1] // 2
    wide = 3 * width_dev
    scal = jnp.stack([rank, chip, core, doc_lengths[0, 0]]).astype(jnp.int32)

    def over_tensor(block):
        return [swap_bit(block, "tensor", m) for m in range(1, n_t)]

    def over_chips(block):
        return [block] + [swap_bit(block, "chip", m) for m in (1, 2, 3)]

    small = [first_gain, first_shift, attn_bias, out_bias, second_gain, second_shift, fc_bias, proj_bias]
    sizes = [p.shape[0] for p in small]
    ffn_mine, ffn_other, out_block = pcall(
        functools.partial(prep_kernel, sizes),
        [((2, rows_dev, hid), BF16)] * 2 + [((rows_dev + 16, width_dev), BF16)],
        scratch=[pltpu.VMEM((16, width_dev), F32)], n_scalar=1, n_in=11,
    )(scal, fc_weight, proj_weight, out_weight, *[p.reshape(1, -1) for p in small])
    out_z = over_tensor(out_block)
    ffn_block = jnp.stack([ffn_mine, swap_core(ffn_other)])
    ffn_one, ffn_two = swap_bit(ffn_block, "tensor", 1), swap_bit(ffn_block, "tensor", 2)
    grad_other = swap_core(block_grad)
    out_z, grad_other, ffn_block, ffn_one, ffn_two, first = fence(
        out_z, grad_other, ffn_block, ffn_one, ffn_two, block_input
    )

    row_two = swap_bit(first, "tensor", 2)
    row_odd = swap_bit(jnp.stack([first, row_two]), "tensor", 1)
    qkv_rows = jnp.pad(qkv_weight.reshape(rows_dev, wide), ((0, 16), (0, 0)))
    attn_block = jnp.concatenate([out_block] + list(out_z) + [qkv_rows], axis=1)
    attn_mine = over_chips(attn_block)
    ffn_pair = over_chips(jnp.stack([ffn_block, ffn_one]))
    row_two, row_odd, attn_mine, ffn_pair, ffn_block, ffn_two = fence(
        row_two, row_odd, attn_mine, ffn_pair, ffn_block, ffn_two
    )

    attn_mine = jnp.stack(attn_mine)
    attn_other = swap_core(attn_mine)
    ffn_two = over_chips(ffn_two)
    ffn_three = swap_bit(ffn_block, "tensor", 3)
    vec = ((1, width), F32)
    params = pcall(
        functools.partial(unpack_kernel, sizes, n_t),
        [vec, vec, ((2 * n_t, width_dev), F32), vec, vec, vec, ((2 * n_t, hid), F32), vec],
        scratch=[pltpu.VMEM((n_dev, 8, 128), F32)], n_scalar=1, n_in=2,
    )(scal, attn_mine, attn_other)
    gain_one, shift_one, attn_shift, out_shift, gain_two, shift_two, fc_shift, proj_shift = params
    attn_outs = pcall(
        functools.partial(attn_kernel, n_t, heads),
        [((width_dev, group), BF16)] * 3 + [((8, group), F32)] + [((group, width), BF16)] * 2
        + [((width, wide), BF16)] + [((width_dev, tok), BF16)] * n_t,
        scratch=[pltpu.VMEM((n_t, width_dev, tok), BF16)],
        n_scalar=1, n_in=3 + 2 + 3, us=12,
    )(scal, block_input, row_two, row_odd, attn_mine, attn_other,
      gain_one, shift_one, attn_shift)
    attn_outs, ffn_two, ffn_three = fence(attn_outs, ffn_two, ffn_three)
    q, k, v, lse, normed_one, unit_one, w_qkv = attn_outs[:7]
    mixed = list(attn_outs[7:])
    mixed = [mixed[0]] + [swap_bit(mixed[m], "tensor", m) for m in range(1, n_t)]
    ffn_three = over_chips(ffn_three)

    hidden, normed_two, mixed_all, w_out = pcall(
        functools.partial(mid_kernel, n_t),
        [((tok, width), F32), ((tok, width), BF16), ((width, tok), BF16), ((width, width), BF16)],
        n_scalar=1, n_in=n_t + 2 + 4, us=4,
    )(scal, *mixed, attn_mine, attn_other, block_input, out_shift, gain_two, shift_two)

    normed_other = swap_core(normed_two)
    cols = n_t * hid
    kept, send, act, pre, fc_sums = pcall(
        functools.partial(ffn_kernel, n_t),
        [((2, tok, width), F32), ((2, tok, width), BF16)] + [((2 * tok, cols), BF16)] * 2 + [((2 * n_t, hid), F32)],
        scratch=[pltpu.VMEM((2 * tok, width), BF16)] * 2 + [pltpu.VMEM((width, hid), BF16)] * 2
        + [pltpu.VMEM((2 * tok, width), F32)] * 2,
        n_scalar=1, n_in=5 + 12, us=13,
    )(scal, normed_two, normed_other, block_grad, grad_other, fc_shift, *ffn_pair, *ffn_two, *ffn_three)
    got = swap_core(send)

    stack = ((2, n_t, 2 * rows_dev, hid), BF16)
    fc_keep, fc_send, pj_keep, pj_send = pcall(
        functools.partial(ffn_grads_kernel, n_t), [stack] * 4,
        scratch=[pltpu.VMEM((2 * tok, width), BF16)] * 2 + [pltpu.VMEM((width, hid), BF16)],
        n_scalar=1, n_in=6, us=8,
    )(scal, normed_two, normed_other, block_grad, grad_other, act, pre)
    got, fc_keep, fc_send, pj_keep, pj_send = fence(got, fc_keep, fc_send, pj_keep, pj_send)
    fc_got, pj_got = swap_bit(fc_send, "chip", 1), swap_bit(pj_send, "chip", 2)

    back = pcall(
        functools.partial(back_mid_kernel, n_t),
        [((tok, width), BF16), ((tok, width), F32), ((tok, width), BF16)] + [((1, width), F32)] * 4
        + [((width_dev, tok), BF16)] * n_t,
        n_in=7, us=4,
    )(kept, got, hidden, block_grad, w_out, gain_two, proj_shift)
    block_out, hidden_grad, attn_grad, gain_two_grad, shift_two_grad, out_bias_grad, proj_bias_grad = back[:7]
    blocks = list(back[7:])
    blocks = [blocks[0]] + [swap_bit(blocks[m], "tensor", m) for m in range(1, n_t)]

    outs = pcall(
        functools.partial(attn_back_kernel, n_t, heads),
        [((tok, width), F32)] + [((tok, width), BF16)] * (n_t - 1)
        + [((wide, group), BF16), ((1, width), F32), ((1, width), F32), ((2 * n_t, width_dev), F32)],
        scratch=[
            pltpu.VMEM((n_t, width_dev, tok), BF16), pltpu.VMEM((HEAD_DIM, group), F32),
            pltpu.VMEM((HEAD_DIM, group), F32), pltpu.VMEM((n_t, tok, width), F32),
        ],
        n_scalar=1, n_in=6 + n_t, us=13,
    )(scal, q, k, v, lse, unit_one, w_qkv, *blocks)
    outs, fc_got, pj_got = fence(outs, fc_got, pj_got)
    parts = list(outs[:n_t])
    dqkv, gain_one_grad, shift_one_grad, bias_grads = outs[n_t:]
    parts = [parts[0]] + [swap_bit(parts[m], "tensor", m) for m in range(1, n_t)]

    half_stack = ((n_t, 2 * rows_dev, hid), BF16)
    base, fc_send, pj_send = pcall(
        chips_one_kernel, [((2, n_t, 2 * rows_dev, hid), F32)] + [half_stack] * 2, n_in=4,
    )(fc_keep, fc_got, pj_keep, pj_got)
    fc_got, pj_got = swap_bit(fc_send, "chip", 2), swap_bit(pj_send, "chip", 1)

    pair = (2, 2 * rows_dev, hid)
    total = pcall(
        functools.partial(chips_two_kernel, n_t), [(pair, F32)] + [(pair, BF16)] * (n_t - 1), n_in=3,
    )(base, fc_got, pj_got)
    grads = [
        gain_one_grad, shift_one_grad, bias_grads.reshape(1, -1), out_bias_grad,
        gain_two_grad, shift_two_grad, fc_sums.reshape(1, -1), proj_bias_grad,
    ]
    (packed,) = pcall(functools.partial(pack_kernel, sizes), [((n_dev, 8, 128), F32)], n_in=8)(*grads)
    packed = lax.all_to_all(packed, EVERY, 0, 0, tiled=True)
    both = (rows_dev, width + wide)
    keep, send = pcall(
        dp_grads_kernel, [((4,) + both, BF16)] * 2,
        scratch=[pltpu.VMEM((width, width), BF16), pltpu.VMEM((width, wide), BF16)], n_scalar=1, n_in=4, us=6,
    )(scal, attn_grad, mixed_all, normed_one, dqkv)
    parts, total, packed, keep, dp_send = fence(parts, total, packed, keep, send)
    total = [total[0]] + [swap_bit(total[m], "tensor", m) for m in range(1, n_t)]
    pair = (2, rows_dev, hid)
    mine, send = pcall(functools.partial(tensor_sum_kernel, n_t), [(pair, F32), (pair, BF16)], n_in=n_t)(*total)
    fc_weight_grad, proj_weight_grad = pcall(
        ffn_last_kernel, [(fc_weight.shape, F32), (proj_weight.shape, F32)], n_scalar=1, n_in=2,
    )(scal, mine, swap_core(send))

    own = pcall(dp_core_kernel, [(both, F32)] + [(both, BF16)] * 3, n_in=2)(keep, swap_core(dp_send))
    own = [own[0]] + [swap_bit(own[m], "chip", m) for m in (1, 2, 3)]
    part = (rows_dev, width_dev)
    qkv_weight_grad, *own = pcall(
        functools.partial(dp_chip_kernel, n_t), [((rows_dev, wide), F32), (part, F32)] + [(part, BF16)] * (n_t - 1),
        n_in=4,
    )(*own)
    own = [own[0]] + [swap_bit(own[m], "tensor", m) for m in range(1, n_t)]
    (out_weight_grad,) = pcall(functools.partial(dp_last_kernel, n_t), [(out_weight.shape, F32)], n_in=n_t)(*own)

    small_outs = pcall(functools.partial(finish_kernel, sizes), [((1, n), F32) for n in sizes], n_in=1)(packed)
    small_outs = [s.reshape(-1) for s in small_outs]

    (input_grad,) = pcall(functools.partial(last_kernel, n_t), [((tok, width), F32)], n_in=n_t + 3)(
        *parts, block_input, hidden_grad, gain_one
    )
    return (
        block_out, input_grad, small_outs[0], small_outs[1], qkv_weight_grad.reshape(qkv_weight.shape),
        small_outs[2], out_weight_grad,
        small_outs[3], small_outs[4], small_outs[5], fc_weight_grad, small_outs[6], proj_weight_grad, small_outs[7],
    )


def solution(mesh):
    n_dp, n_tensor = mesh.shape["dp"], mesh.shape["tensor"]
    grid = Mesh(mesh.devices.reshape(n_dp // 2, 2, n_tensor), EVERY)
    dp = ("chip", "core")
    vec, rows, cols = P(EVERY), P(EVERY, None), P("tensor", dp)
    return jax.shard_map(
        body_four if n_dp == 8 and n_tensor == 4 else body,
        mesh=grid,
        in_specs=(
            rows, P(dp, None), vec, vec, P(dp, None, "tensor"), vec, cols, vec,
            vec, vec, P(dp, "tensor"), vec, cols, vec, rows,
        ),
        out_specs=(
            rows, rows, vec, vec, P(dp, None, "tensor"), vec, cols, vec,
            vec, vec, P(dp, "tensor"), vec, cols, vec,
        ),
        check_vma=False,
    )
```

```python
import functools
import jax
import jax.numpy as jnp
from jax import lax
from jax.experimental import pallas as pl
from jax.experimental.pallas import tpu as pltpu
from jax.sharding import Mesh, PartitionSpec as P

HEAD_DIM = 64
EPS = 1e-05
F32, BF16 = jnp.float32, jnp.bfloat16
EVERY = ("chip", "core", "tensor")


def swap_bit(values, axis, mask):
    size = lax.axis_size(axis)
    return lax.ppermute(values, axis, [(i, i ^ mask) for i in range(size)])


def swap_core(values):
    return swap_bit(values, "core", 1)


def shift_tensor(values, step):
    size = lax.axis_size("tensor")
    return lax.ppermute(values, "tensor", [(i, (i + step) % size) for i in range(size)])


def after(values, *first):
    return lax.optimization_barrier((values, *first))[0]


def sort_pieces(pieces, offsets):
    rows = pieces[0].shape[0]
    out = jnp.zeros((rows * len(pieces),) + pieces[0].shape[1:], pieces[0].dtype)
    for piece, at in zip(pieces, offsets):
        out = lax.dynamic_update_slice_in_dim(out, piece, at * rows, 0)
    return out


def gather_chips(block):
    return lax.all_gather(block, "chip", axis=0, tiled=True)


def scatter_chips(full):
    arrived = lax.all_to_all(full, "chip", 0, 0, tiled=True)
    return arrived.astype(F32).sum(axis=0)


def norm_stats(values):
    center = jnp.mean(values, axis=-1, keepdims=True)
    offset = values - center
    spread = lax.rsqrt(jnp.mean(offset * offset, axis=-1, keepdims=True) + EPS)
    return offset * spread, spread


def norm_back(grad_out, unit_rows, spread, gain_vec):
    scaled = grad_out * gain_vec
    centred = scaled - jnp.mean(scaled, axis=-1, keepdims=True)
    centred = centred - unit_rows * jnp.mean(scaled * unit_rows, axis=-1, keepdims=True)
    return spread * centred


def gelu_tanh(values):
    return jax.nn.gelu(values, approximate=True)


def score_block(query_block, key_heads, block_start, boundary, score_scale):
    block_rows = query_block.shape[0]
    key_pos = jnp.arange(key_heads.shape[0])
    query_pos = block_start + jnp.arange(block_rows)
    allowed = (key_pos[None, :] <= query_pos[:, None]) & (
        (key_pos[None, :] >= boundary) == (query_pos[:, None] >= boundary)
    )
    scores = (
        jnp.einsum("ihd,jhd->hij", query_block, key_heads, preferred_element_type=F32)
        * score_scale
    )
    return jnp.where(allowed[None], scores, -jnp.inf)


def attend(query_heads, key_heads, value_heads, boundary, score_scale):
    row_count, heads_dev, head_dim = query_heads.shape
    block_rows = min(512, row_count)
    outputs, totals = [], []
    for block_start in range(0, row_count, block_rows):
        scores = score_block(
            query_heads[block_start : block_start + block_rows],
            key_heads, block_start, boundary, score_scale,
        )
        row_peak = jnp.max(scores, axis=-1, keepdims=True)
        log_total = row_peak + jnp.log(jnp.sum(jnp.exp(scores - row_peak), axis=-1, keepdims=True))
        probs_low = jnp.exp(scores - log_total).astype(BF16)
        mixed_block = jnp.einsum("hij,jhd->ihd", probs_low, value_heads, preferred_element_type=F32)
        outputs.append(mixed_block.reshape(block_rows, heads_dev * head_dim).astype(BF16))
        totals.append(log_total)
    return jnp.concatenate(outputs, axis=0), totals


def attend_back(query_heads, key_heads, value_heads, totals, grad_heads, boundary, score_scale):
    row_count = query_heads.shape[0]
    block_rows = min(512, row_count)
    query_grads = []
    key_acc = jnp.zeros(key_heads.shape, F32)
    value_acc = jnp.zeros(value_heads.shape, F32)
    for block_index, block_start in enumerate(range(0, row_count, block_rows)):
        query_block = query_heads[block_start : block_start + block_rows]
        grad_block = grad_heads[block_start : block_start + block_rows]
        scores = score_block(query_block, key_heads, block_start, boundary, score_scale)
        probs = jnp.exp(scores - totals[block_index])
        probs_low = probs.astype(BF16)
        prob_grads = jnp.einsum("ihd,jhd->hij", grad_block, value_heads, preferred_element_type=F32)
        row_dot = jnp.sum(probs * prob_grads, axis=-1, keepdims=True)
        score_grads = (probs * (prob_grads - row_dot)).astype(BF16)
        query_grads.append(
            jnp.einsum("hij,jhd->ihd", score_grads, key_heads, preferred_element_type=F32) * score_scale
        )
        key_acc = key_acc + jnp.einsum("hij,ihd->jhd", score_grads, query_block, preferred_element_type=F32)
        value_acc = value_acc + jnp.einsum("hij,ihd->jhd", probs_low, grad_block, preferred_element_type=F32)
    return jnp.concatenate(query_grads, axis=0), key_acc * score_scale, value_acc


def body(
    block_input, doc_lengths, first_gain, first_shift, qkv_weight, attn_bias, out_weight, out_bias,
    second_gain, second_shift, fc_weight, fc_bias, proj_weight, proj_bias, block_grad,
):
    n_tensor = lax.axis_size("tensor")
    n_chip = lax.axis_size("chip")
    n_dev = n_tensor * n_chip * 2
    rank = lax.axis_index("tensor")
    core = lax.axis_index("core")
    tok, width = block_input.shape
    boundary = doc_lengths[0, 0]

    small = [first_gain, first_shift, attn_bias, out_bias, second_gain, second_shift, fc_bias, proj_bias]
    small_flat = jnp.concatenate(small)
    small_all = lax.all_to_all(
        jnp.broadcast_to(small_flat[None], (n_dev,) + small_flat.shape), EVERY, 0, 0, tiled=True
    ).astype(F32)
    params, at = [], 0
    for p in small:
        params.append(small_all[:, at : at + p.shape[0]].reshape(-1))
        at += p.shape[0]
    gain_one, shift_one, attn_shift, out_shift, gain_two, shift_two, fc_shift, proj_shift = params

    def ffn_rows(shard):
        rows, cols = shard.shape
        half = cols // 2
        mine = lax.dynamic_slice_in_dim(shard, core * half, half, 1)
        other = swap_core(lax.dynamic_slice_in_dim(shard, (1 - core) * half, half, 1))
        first = jnp.where(core == 0, mine, other)
        last = jnp.where(core == 0, other, mine)
        return jnp.concatenate([first, last], axis=0)

    def tensor_pieces(block):
        return [block] + [swap_bit(block, "tensor", m) for m in range(1, n_tensor)]

    fc_block = jnp.concatenate(tensor_pieces(ffn_rows(fc_weight)), axis=1)
    fc_full = gather_chips(fc_block)

    width_dev = qkv_weight.shape[2]
    out_t = out_weight.T
    out_block = jnp.concatenate(tensor_pieces(out_t), axis=1)
    attn_block = jnp.concatenate([qkv_weight.reshape(-1, 3 * width_dev), out_block], axis=1)
    rows_dev = attn_block.shape[0]
    attn_chips = gather_chips(attn_block).reshape(n_chip, rows_dev, -1)
    attn_other = swap_core(attn_chips)
    attn_pair = jnp.where(core == 0, jnp.stack([attn_chips, attn_other], 1), jnp.stack([attn_other, attn_chips], 1))
    attn_full = attn_pair.reshape(width, -1)
    qkv_full, out_full = attn_full[:, : 3 * width_dev], attn_full[:, 3 * width_dev :]

    half = tok // 2
    cur = [block_input[:half], block_input[half:]]
    pieces = [block_input]
    for step in range(1, n_tensor):
        cur = [shift_tensor(c, 1) for c in cur]
        pieces.append(jnp.concatenate(cur, axis=0))
    rows_in = sort_pieces(pieces, [(rank - s) % n_tensor for s in range(n_tensor)])

    proj_block = after(proj_weight.T, pieces[-1])
    proj_block = jnp.concatenate(tensor_pieces(ffn_rows(proj_block)), axis=1)
    proj_full = gather_chips(proj_block)

    unit_rows, _ = norm_stats(rows_in.astype(F32))
    normed_one = (unit_rows * gain_one + shift_one).astype(BF16)
    row_count = normed_one.shape[0]
    heads_dev = width_dev // HEAD_DIM
    score_scale = HEAD_DIM ** (-0.5)
    projected = jnp.dot(normed_one, qkv_full, preferred_element_type=F32).reshape(row_count, 3, width_dev)
    query_shift = lax.dynamic_slice_in_dim(attn_shift, rank * width_dev, width_dev)
    value_shift = lax.dynamic_slice_in_dim(attn_shift, width + rank * width_dev, width_dev)
    head_shape = (row_count, heads_dev, HEAD_DIM)
    queries = (projected[:, 0] + query_shift).astype(BF16).reshape(head_shape)
    key_rows = projected[:, 1].astype(BF16).reshape(head_shape)
    value_rows = (projected[:, 2] + value_shift).astype(BF16).reshape(head_shape)
    mixed_heads, totals = attend(queries, key_rows, value_rows, boundary, score_scale)

    def to_tokens(block_of):
        return jnp.concatenate(
            [block_of(rank)] + [swap_bit(block_of(rank ^ m), "tensor", m) for m in range(1, n_tensor)], axis=1
        )

    mixed = to_tokens(lambda z: lax.dynamic_slice_in_dim(mixed_heads, z * tok, tok, 0))

    inputs = block_input.astype(F32)
    attn_out = lax.dot_general(mixed, out_full, (((1,), (1,)), ((), ())), preferred_element_type=F32)
    hidden = inputs + (attn_out + out_shift)
    unit_two, spread_two = norm_stats(hidden)
    normed_two = (unit_two * gain_two + shift_two).astype(BF16)

    rows_two = jnp.concatenate([normed_two, swap_core(normed_two)], axis=0)
    rows_grad = jnp.concatenate([block_grad, swap_core(block_grad)], axis=0)
    fc_cols = fc_shift.reshape(n_tensor, 2, -1)
    fc_cols = lax.dynamic_index_in_dim(fc_cols, core, 1, False)
    fc_cols = jnp.stack([lax.dynamic_index_in_dim(fc_cols, rank ^ m, 0, False) for m in range(n_tensor)])
    pre_act = jnp.dot(rows_two, fc_full, preferred_element_type=F32) + fc_cols.reshape(-1)
    gelu_values, gelu_pull = jax.vjp(gelu_tanh, pre_act)
    activated = gelu_values.astype(BF16)
    act_grad = jnp.dot(rows_grad, proj_full, preferred_element_type=F32)
    pre_grad = gelu_pull(act_grad)[0].astype(BF16)
    n2g_part = lax.dot_general(pre_grad, fc_full, (((1,), (1,)), ((), ())), preferred_element_type=F32)
    normed_two_grad = n2g_part[:tok] + swap_core(n2g_part[tok:].astype(BF16)).astype(F32)
    mlp_part = lax.dot_general(activated, proj_full, (((1,), (1,)), ((), ())), preferred_element_type=F32)
    mlp_out = mlp_part[:tok] + swap_core(mlp_part[tok:].astype(BF16)).astype(F32)
    block_out = (hidden + (mlp_out + proj_shift)).astype(BF16)

    top_grad = block_grad.astype(F32)
    hidden_grad = top_grad + norm_back(normed_two_grad, unit_two, spread_two, gain_two)
    attn_grad = hidden_grad.astype(BF16)

    heads_grad = jnp.dot(attn_grad, out_full, preferred_element_type=F32).astype(BF16)
    grad_pieces = [heads_grad[:, m * width_dev : (m + 1) * width_dev] for m in range(n_tensor)]
    grad_pieces = [grad_pieces[0]] + [swap_bit(grad_pieces[m], "tensor", m) for m in range(1, n_tensor)]
    heads_rows = sort_pieces(grad_pieces, [rank ^ m for m in range(n_tensor)])

    def ffn_scatter(partial):
        cols = partial.shape[1]
        block = scatter_chips(partial.reshape(n_chip, -1, cols))
        part = cols // n_tensor
        total = block[:, :part]
        for m in range(1, n_tensor):
            total = total + swap_bit(block[:, m * part : (m + 1) * part].astype(BF16), "tensor", m).astype(F32)
        rows = total.shape[0] // 2
        mine = lax.dynamic_slice_in_dim(total, core * rows, rows, 0)
        other = swap_core(lax.dynamic_slice_in_dim(total, (1 - core) * rows, rows, 0))
        first = jnp.where(core == 0, mine, other)
        last = jnp.where(core == 0, other, mine)
        return jnp.concatenate([first, last], axis=1)

    proj_grad = lax.dot_general(rows_grad, activated, (((0,), (0,)), ((), ())), preferred_element_type=F32)
    proj_weight_grad = ffn_scatter(proj_grad.astype(BF16)).T
    fc_grad = lax.dot_general(rows_two, pre_grad, (((0,), (0,)), ((), ())), preferred_element_type=F32)
    fc_weight_grad = ffn_scatter(fc_grad.astype(BF16))

    def core_scatter(partial):
        cols = partial.shape[1]
        split = partial.reshape(n_chip, 2, -1, cols)
        keep = lax.dynamic_index_in_dim(split, core, 1, False)
        send = lax.dynamic_index_in_dim(split, 1 - core, 1, False)
        return keep.astype(F32) + swap_core(send.astype(BF16)).astype(F32)

    out_grad = lax.dot_general(attn_grad, mixed, (((0,), (0,)), ((), ())), preferred_element_type=F32)
    out_block_grad = scatter_chips(core_scatter(out_grad).astype(BF16))
    out_total = out_block_grad[:, :width_dev]
    for m in range(1, n_tensor):
        piece = out_block_grad[:, m * width_dev : (m + 1) * width_dev].astype(BF16)
        out_total = out_total + swap_bit(piece, "tensor", m).astype(F32)
    out_weight_grad = out_total.T

    query_grad, key_grad, value_grad = attend_back(
        queries, key_rows, value_rows, totals, heads_rows.reshape(head_shape), boundary, score_scale
    )
    flat_shape = (row_count, width_dev)
    query_low = query_grad.reshape(flat_shape).astype(BF16)
    key_low = key_grad.reshape(flat_shape).astype(BF16)
    value_low = value_grad.reshape(flat_shape).astype(BF16)
    projection_grads = jnp.concatenate([query_low, key_low, value_low], axis=1)
    n1g_part = lax.dot_general(projection_grads, qkv_full, (((1,), (1,)), ((), ())), preferred_element_type=F32)
    n1g_blocks = n1g_part.reshape(n_tensor, tok, width)

    def part_block(z):
        return lax.dynamic_index_in_dim(n1g_blocks, z % n_tensor, 0, False)

    running = part_block(rank - 1)
    acc = [running[:half], running[half:]]
    for step in range(1, n_tensor):
        mine = part_block(rank - 1 - step)
        acc = [
            shift_tensor(a.astype(BF16), 1).astype(F32) + m
            for a, m in zip(acc, (mine[:half], mine[half:]))
        ]
    normed_one_grad = jnp.concatenate(acc, axis=0)

    first_gain_grad = jnp.sum(n1g_part * unit_rows, axis=0)
    first_shift_grad = jnp.sum(n1g_part, axis=0)
    zeros = jnp.zeros((2 * width,), F32)
    attn_bias_grad = lax.dynamic_update_slice_in_dim(
        zeros, jnp.sum(query_low.astype(F32), axis=0), rank * width_dev, 0
    )
    attn_bias_grad = lax.dynamic_update_slice_in_dim(
        attn_bias_grad, jnp.sum(value_low.astype(F32), axis=0), width + rank * width_dev, 0
    )
    out_bias_grad = jnp.sum(attn_grad.astype(F32), axis=0)
    second_gain_grad = jnp.sum(normed_two_grad * unit_two, axis=0)
    second_shift_grad = jnp.sum(normed_two_grad, axis=0)
    proj_bias_grad = jnp.sum(top_grad, axis=0)
    fc_sums = jnp.sum(pre_grad.astype(F32), axis=0).reshape(n_tensor, -1)
    fc_bias_grad = jnp.zeros((n_tensor, 2, fc_sums.shape[1]), F32)
    for m in range(n_tensor):
        fc_bias_grad = lax.dynamic_update_slice(fc_bias_grad, fc_sums[m][None, None], (rank ^ m, core, 0))
    fc_bias_grad = fc_bias_grad.reshape(-1)

    smalls = [
        first_gain_grad, first_shift_grad, attn_bias_grad, out_bias_grad,
        second_gain_grad, second_shift_grad, fc_bias_grad, proj_bias_grad,
    ]
    small_grads = jnp.concatenate([g.reshape(n_dev, -1) for g in smalls], axis=1)
    small_grads = lax.all_to_all(small_grads, EVERY, 0, 0, tiled=True).sum(axis=0)
    small_outs, at = [], 0
    for g in smalls:
        n = g.shape[0] // n_dev
        small_outs.append(small_grads[at : at + n])
        at += n

    qkv_grad = lax.dot_general(normed_one, projection_grads, (((0,), (0,)), ((), ())), preferred_element_type=F32)
    qkv_weight_grad = scatter_chips(core_scatter(qkv_grad).astype(BF16)).reshape(qkv_weight.shape)

    own_unit, own_spread = norm_stats(inputs)
    input_grad = hidden_grad + norm_back(normed_one_grad, own_unit, own_spread, gain_one)
    return (
        block_out, input_grad, small_outs[0], small_outs[1], qkv_weight_grad, small_outs[2], out_weight_grad,
        small_outs[3], small_outs[4], small_outs[5], fc_weight_grad, small_outs[6], proj_weight_grad, small_outs[7],
    )


def pcall(kernel, outs, scratch=(), n_scalar=0, n_in=0, us=2):
    whole = pl.BlockSpec(memory_space=pltpu.VMEM)
    return pl.pallas_call(
        kernel,
        in_specs=[pl.BlockSpec(memory_space=pltpu.SMEM)] * n_scalar + [whole] * n_in,
        out_specs=[whole] * len(outs),
        out_shape=[jax.ShapeDtypeStruct(s, d) for s, d in outs],
        scratch_shapes=list(scratch),
        cost_estimate=pl.CostEstimate(flops=1, bytes_accessed=1, transcendentals=0),
        compiler_params=pltpu.CompilerParams(vmem_limit_bytes=56 * 1024 * 1024),
    )


def place():
    return lax.axis_index("tensor"), lax.axis_index("chip"), lax.axis_index("core")


def dg(a, b, ca, cb):
    return lax.dot_general(a, b, (((ca,), (cb,)), ((), ())), preferred_element_type=F32)


def prep_kernel(sizes, scal, fc, proj_t, out_w, qkv, *refs):
    ins, (mine, other, block, rows_o, tile) = refs[: len(sizes)], refs[len(sizes) :]
    core = place()[2]
    half = mine.shape[2]
    rows = fc.shape[0]
    for to, side in ((mine, core), (other, 1 - core)):
        lanes = pl.ds(pl.multiple_of(side * half, 128), half)
        to[0] = fc[:, lanes]
        to[1] = proj_t[:, lanes]
    tile[...] = jnp.zeros_like(tile)
    for i, n in enumerate(sizes):
        tile[i : i + 1, 0:n] = ins[i][...].astype(F32)
    block[0:rows, :] = out_w[...].T
    block[rows:, :] = tile[...].astype(BF16)
    third = qkv.shape[2]
    rows_o[rows:, :] = jnp.zeros((16, rows_o.shape[1]), BF16)
    for i in range(3):
        rows_o[0:rows, i * third : (i + 1) * third] = qkv[i]


def spread(n, cols):
    lane = lax.broadcasted_iota(jnp.int32, (128, cols), 1).astype(F32)
    row = lax.broadcasted_iota(jnp.int32, (128, cols), 0).astype(F32)
    rest = lane - n * jnp.floor((lane + 0.5) * (1.0 / n))
    return jnp.where(rest == row, 1.0, 0.0)


def owner(n, rows, cols):
    lane = lax.broadcasted_iota(jnp.int32, (rows, cols), 1)
    first = lax.broadcasted_iota(jnp.int32, (rows, cols), 0) * n
    return (lane >= first) & (lane < first + n)


def unpack_kernel(sizes, n_t, scal, mine, other, *refs):
    outs, every = refs[:-1], refs[-1]
    rank, chip, core = place()
    n_dev = every.shape[0]
    rows = mine.shape[1] - 16
    wide = outs[2].shape[1]
    for m in range(4):
        for j, ref in ((0, mine), (1, other)):
            for s in range(n_t):
                at = ((chip ^ m) * 2 + (core ^ j)) * n_t + (rank ^ s)
                every[at] = ref[m, rows : rows + 16, s * wide : s * wide + 128].astype(F32)[0:8]
    values = every[...]
    cached = {}
    for i, n in enumerate(sizes):
        cols = n * n_dev
        if n not in cached:
            cached[n] = (spread(n, cols).astype(BF16), owner(n, n_dev, cols))
        full = jnp.dot(values[:, i, :].astype(BF16), cached[n][0], preferred_element_type=F32)
        full = jnp.sum(jnp.where(cached[n][1], full, 0.0), axis=0, keepdims=True)
        lanes = outs[i].shape[1]
        for r in range(outs[i].shape[0]):
            outs[i][r : r + 1, :] = full[:, r * lanes : (r + 1) * lanes]


def pack_kernel(sizes, *refs):
    ins, out = refs[: len(sizes)], refs[len(sizes)]
    n_dev = out.shape[0]
    cached = {}
    for i, n in enumerate(sizes):
        cols = n * n_dev
        if n not in cached:
            cached[n] = (spread(n, cols), owner(n, n_dev, cols))
        rows = jnp.where(cached[n][1], ins[i][...], 0.0)
        out[:, i, :] = lax.dot_general(
            rows, cached[n][0], (((1,), (1,)), ((), ())),
            precision=lax.Precision.HIGHEST, preferred_element_type=F32,
        )


def finish_kernel(sizes, all_ref, *outs):
    total = jnp.sum(all_ref[...], axis=0)
    for i, n in enumerate(sizes):
        outs[i][...] = total[i : i + 1, 0:n]


def row_stats(values):
    center = jnp.mean(values, axis=-1, keepdims=True)
    offset = values - center
    spread_rows = lax.rsqrt(jnp.mean(offset * offset, axis=-1, keepdims=True) + EPS)
    return offset * spread_rows, spread_rows


def mask_of(boundary, first, block, keys):
    qpos = first + lax.broadcasted_iota(jnp.int32, (keys, block), 1)
    kpos = lax.broadcasted_iota(jnp.int32, (keys, block), 0)
    low = jnp.where(qpos >= boundary, boundary, 0)
    return (kpos >= low) & (kpos <= qpos)


LOG2E = 1.4426950408889634


def attn_kernel(n_t, heads, *refs):
    (scal,) = refs[:1]
    own, two, odd = refs[1:4]
    at = 4
    stacks = refs[at : at + 2]
    gain, shift, bias = refs[at + 2 : at + 5]
    outs = refs[at + 5 :]
    q_o, k_o, v_o, lse_o, normed_o, unit_o, w_o = outs[:7]
    send = outs[7 : 7 + n_t]
    mixed = outs[7 + n_t]
    rank, chip, core, boundary = (*place(), scal[0, 0])
    tok, width = own.shape
    wide = w_o.shape[1]
    rows_dev = stacks[0].shape[1] - 16
    for m in range(4):
        for j in range(2):
            to = pl.multiple_of(((chip ^ m) * 2 + (core ^ j)) * rows_dev, 16)
            w_o[pl.ds(to, rows_dev), :] = stacks[j][m, 0:rows_dev, width : width + wide]

    def put(values, to):
        unit, _ = row_stats(values.astype(F32))
        unit_o[pl.ds(to, values.shape[0]), :] = unit.astype(BF16)
        normed_o[pl.ds(to, values.shape[0]), :] = (unit * gain[...] + shift[...]).astype(BF16)

    put(own[...], pl.multiple_of(rank * tok, tok))
    put(two[...], pl.multiple_of((rank ^ 2) * tok, tok))
    put(odd[0], pl.multiple_of((rank ^ 1) * tok, tok))
    put(odd[1], pl.multiple_of((rank ^ 3) * tok, tok))
    third = wide // 3
    qb = bias[pl.ds(rank, 1), :]
    vb = bias[pl.ds(n_t + rank, 1), :]
    projected = jnp.dot(normed_o[...], w_o[...], preferred_element_type=F32)
    zero = jnp.zeros_like(qb)
    full_bias = jnp.concatenate([qb, zero, vb], axis=1)
    flipped = (projected + full_bias).astype(BF16).T
    q_o[...] = flipped[0:third]
    k_o[...] = flipped[third : 2 * third]
    v_o[...] = flipped[2 * third : 3 * third]
    lse_o[...] = jnp.zeros_like(lse_o)
    masks = [mask_of(boundary, b * tok, tok, (b + 1) * tok) for b in range(n_t)]
    for h in range(heads):
        lo, hi = h * HEAD_DIM, (h + 1) * HEAD_DIM
        keys = k_o[lo:hi, :].T
        for b in range(n_t):
            n = (b + 1) * tok
            cols = slice(b * tok, n)
            scores = dg(keys[0:n], q_o[lo:hi, cols], 1, 0) * (HEAD_DIM**-0.5 * LOG2E)
            scores = jnp.where(masks[b], scores, -jnp.inf)
            peak = jnp.max(scores, axis=0, keepdims=True)
            probs = jnp.exp2(scores - peak)
            total = jnp.sum(probs, axis=0, keepdims=True)
            lse_o[h : h + 1, cols] = peak + jnp.log2(total)
            out = jnp.dot(v_o[lo:hi, 0:n], probs.astype(BF16), preferred_element_type=F32)
            mixed[b, lo:hi, :] = (out * (1.0 / total)).astype(BF16)
    for s in range(n_t):
        send[s][...] = mixed[rank ^ s]


def mid_kernel(n_t, *refs):
    scal = refs[0]
    blocks = refs[1 : 1 + n_t]
    stacks = refs[1 + n_t : 3 + n_t]
    x, bias, gain, shift = refs[3 + n_t : 7 + n_t]
    hidden_o, normed_o, mixed_o, w_o = refs[7 + n_t :]
    chip, core = place()[1:]
    width = x.shape[1]
    rows_dev = stacks[0].shape[1] - 16
    for m in range(4):
        for j in range(2):
            to = pl.multiple_of(((chip ^ m) * 2 + (core ^ j)) * rows_dev, 16)
            w_o[pl.ds(to, rows_dev), :] = stacks[j][m, 0:rows_dev, 0:width]
    k = blocks[0].shape[0]
    for s in range(n_t):
        mixed_o[s * k : (s + 1) * k, :] = blocks[s][...]
    attn = dg(mixed_o[...], w_o[...], 0, 1)
    hidden = x[...].astype(F32) + (attn + bias[...])
    hidden_o[...] = hidden
    unit, _ = row_stats(hidden)
    normed_o[...] = (unit * gain[...] + shift[...]).astype(BF16)


def ffn_kernel(n_t, *refs):
    scal = refs[0]
    own, other, g_own, g_other, bias = refs[1:6]
    zero, one, diagonal, two, fc_three, pj_three = refs[6:9], refs[9:12], refs[12], refs[13:17], refs[17:21], refs[21:25]
    outs = refs[25:]
    whole = [[*zero, diagonal.at[0]], [*one, diagonal.at[1]], two]
    pieces = [[[p.at[w] for p in group] for w in range(2)] for group in whole]
    pieces.append([list(fc_three), list(pj_three)])
    own_o, send_o, act_o, pre_o, sums_o, x_s, g_s, fc_s, pj_s, mlp_s, n2_s = outs
    rank, chip, core = place()
    tok = own.shape[0]
    x_s[0:tok] = own[...]
    x_s[tok:] = other[...]
    g_s[0:tok] = g_own[...]
    g_s[tok:] = g_other[...]
    cols = fc_three[0].shape[2]
    rows = fc_three[0].shape[1]
    c0 = 0.7978845608028654
    sums_o[...] = jnp.zeros_like(sums_o)
    for s in range(n_t):
        for w, to_ref in ((0, fc_s), (1, pj_s)):
            for m in range(4):
                for j in range(2):
                    to = pl.multiple_of(((chip ^ m) * 2 + (core ^ j)) * rows, 16)
                    to_ref[pl.ds(to, rows), :] = pieces[s][w][m][j]
        fc_w, pj_w = fc_s[...], pj_s[...]
        lanes = slice(s * cols, (s + 1) * cols)
        b = bias[pl.ds((rank ^ s) * 2 + core, 1), :]
        z = jnp.dot(x_s[...], fc_w, preferred_element_type=F32) + b
        ga = jnp.dot(g_s[...], pj_w, preferred_element_type=F32)
        zz = z * z
        t = jnp.tanh(z * (c0 + (c0 * 0.044715) * zz))
        up = 0.5 + 0.5 * t
        act = (z * up).astype(BF16)
        slope = up + (0.5 * z) * (1.0 - t * t) * (c0 + (3.0 * c0 * 0.044715) * zz)
        pre = (ga * slope).astype(BF16)
        act_o[:, lanes] = act
        pre_o[:, lanes] = pre
        sums_o[pl.ds((rank ^ s) * 2 + core, 1), :] = jnp.sum(pre.astype(F32), axis=0, keepdims=True)
        mlp = dg(act, pj_w, 1, 1)
        n2 = dg(pre, fc_w, 1, 1)
        if s == 0:
            mlp_s[...] = mlp
            n2_s[...] = n2
        else:
            mlp_s[...] += mlp
            n2_s[...] += n2
    for i, ref in ((0, mlp_s), (1, n2_s)):
        own_o[i] = ref[0:tok]
        send_o[i] = ref[tok:].astype(BF16)


def ffn_grads_kernel(n_t, *refs):
    scal, own, other, g_own, g_other, act, pre = refs[:7]
    fc_keep, fc_send, pj_keep, pj_send, x_s, g_s, tmp = refs[7:]
    chip, core = place()[1:]
    tok = own.shape[0]
    x_s[0:tok] = own[...]
    x_s[tok:] = other[...]
    g_s[0:tok] = g_own[...]
    g_s[tok:] = g_other[...]
    cols = fc_keep.shape[3]
    rows = fc_keep.shape[2] // 2
    for w, (left, right, keep, send, keep_m, send_m) in enumerate((
        (g_s, act, pj_keep, pj_send, (0, 1), (2, 3)),
        (x_s, pre, fc_keep, fc_send, (0, 2), (1, 3)),
    )):
        for s in range(n_t):
            tmp[...] = dg(left[...], right[:, s * cols : (s + 1) * cols], 0, 0).astype(BF16)
            for to, ms in ((keep, keep_m), (send, send_m)):
                for i, m in enumerate(ms):
                    for j in range(2):
                        at = pl.multiple_of(((chip ^ m) * 2 + (core ^ j)) * rows, 16)
                        to[i, s, j * rows : (j + 1) * rows] = tmp[pl.ds(at, rows), :]


def back_mid_kernel(n_t, *refs):
    kept, got, hidden, grad, w, gain, proj_bias = refs[:7]
    block_out, hg_o, attn_o, gain_o, shift_o, outb_o, projb_o = refs[7:14]
    blocks = refs[14 : 14 + n_t]
    hid = hidden[...]
    top = grad[...].astype(F32)
    g = kept[1] + got[1].astype(F32)
    unit, spread_rows = row_stats(hid)
    gain_o[...] = jnp.sum(g * unit, axis=0, keepdims=True)
    shift_o[...] = jnp.sum(g, axis=0, keepdims=True)
    projb_o[...] = jnp.sum(top, axis=0, keepdims=True)
    scaled = g * gain[...]
    centred = scaled - jnp.mean(scaled, axis=-1, keepdims=True)
    centred = centred - unit * jnp.mean(scaled * unit, axis=-1, keepdims=True)
    hg = top + spread_rows * centred
    hg_o[...] = hg
    low = hg.astype(BF16)
    attn_o[...] = low
    outb_o[...] = jnp.sum(low.astype(F32), axis=0, keepdims=True)
    heads = dg(w[...], low, 0, 1).astype(BF16)
    k = blocks[0].shape[0]
    for s in range(n_t):
        blocks[s][...] = heads[s * k : (s + 1) * k]
    block_out[...] = (hid + (kept[0] + got[0].astype(F32) + proj_bias[...])).astype(BF16)


def attn_back_kernel(n_t, heads, *refs):
    scal, q, k, v, lse, unit, w = refs[:7]
    grads = refs[7 : 7 + n_t]
    outs = refs[7 + n_t :]
    p_o = outs[:3]
    dqkv_o, gain_o, shift_o, bias_o, g_s, dk_s, dv_s, n1_s = outs[3:]
    rank, boundary = place()[0], scal[0, 0]
    tok = grads[0].shape[1]
    third = q.shape[0]
    for s in range(n_t):
        g_s[rank ^ s] = grads[s][...]
    masks = [mask_of(boundary, b * tok, tok, (b + 1) * tok) for b in range(n_t)]
    scale = HEAD_DIM**-0.5
    for h in range(heads):
        lo, hi = h * HEAD_DIM, (h + 1) * HEAD_DIM
        keys = k[lo:hi, :].T
        vals = v[lo:hi, :].T
        dk_s[...] = jnp.zeros_like(dk_s)
        dv_s[...] = jnp.zeros_like(dv_s)
        for b in range(n_t):
            n = (b + 1) * tok
            cols = slice(b * tok, n)
            qb = q[lo:hi, cols]
            gb = g_s[b, lo:hi, :]
            scores = dg(keys[0:n], qb, 1, 0) * (scale * LOG2E)
            probs = jnp.exp2(jnp.where(masks[b], scores - lse[h : h + 1, cols], -jnp.inf))
            pg = dg(vals[0:n], gb, 1, 0)
            dot = jnp.sum(probs * pg, axis=0, keepdims=True)
            ds = (probs * (pg - dot)).astype(BF16)
            low = probs.astype(BF16)
            dq = jnp.dot(k[lo:hi, 0:n], ds, preferred_element_type=F32) * scale
            dqkv_o[lo:hi, cols] = dq.astype(BF16)
            dk_s[:, 0:n] += dg(qb, ds, 1, 1)
            dv_s[:, 0:n] += dg(gb, low, 1, 1)
        dqkv_o[third + lo : third + hi, :] = (dk_s[...] * scale).astype(BF16)
        dqkv_o[2 * third + lo : 2 * third + hi, :] = dv_s[...].astype(BF16)
    flat = dqkv_o[...]
    n1 = dg(flat, w[...], 0, 1)
    n1_s[...] = n1.reshape(n1_s.shape)
    gain_o[...] = jnp.sum(n1 * unit[...].astype(F32), axis=0, keepdims=True)
    shift_o[...] = jnp.sum(n1, axis=0, keepdims=True)
    ones = jnp.ones((8, flat.shape[1]), BF16)
    sums = dg(ones, flat, 1, 1)
    bias_o[...] = jnp.zeros_like(bias_o)
    bias_o[pl.ds(rank, 1), :] = sums[0:1, 0:third]
    bias_o[pl.ds(n_t + rank, 1), :] = sums[0:1, 2 * third : 3 * third]
    p_o[0][0] = n1_s[rank ^ 1].astype(BF16)
    p_o[0][1] = n1_s[rank ^ 3].astype(BF16)
    p_o[1][...] = n1_s[rank]
    p_o[2][...] = n1_s[rank ^ 2]


def half_sum_kernel(mine, got, send):
    send[...] = (mine[...] + got[1].astype(F32)).astype(BF16)


def dp_grads_kernel(scal, attn_grad, mixed, normed, dqkv, keep_o, send_o, out_s, qkv_s):
    chip, core = place()[1:]
    rows = keep_o.shape[1]
    width = out_s.shape[1]
    out_s[...] = dg(attn_grad[...], mixed[...], 0, 1).astype(BF16)
    qkv_s[...] = dg(normed[...], dqkv[...], 0, 1).astype(BF16)
    for m in range(4):
        for j, to in ((0, keep_o), (1, send_o)):
            at = pl.multiple_of(((chip ^ m) * 2 + (core ^ j)) * rows, 16)
            to[m, :, 0:width] = out_s[pl.ds(at, rows), :]
            to[m, :, width:] = qkv_s[pl.ds(at, rows), :]


def dp_core_kernel(keep, got, own_o, *sends):
    for m in range(4):
        total = keep[m].astype(F32) + got[m].astype(F32)
        if m == 0:
            own_o[...] = total
        else:
            sends[m - 1][...] = total.astype(BF16)


def chips_one_kernel(fc_keep, fc_got, pj_keep, pj_got, base_o, fc_send, pj_send):
    for w, (keep, got, send) in enumerate(((fc_keep, fc_got, fc_send), (pj_keep, pj_got, pj_send))):
        base_o[w] = keep[0].astype(F32) + got[0].astype(F32)
        send[...] = (keep[1].astype(F32) + got[1].astype(F32)).astype(BF16)


def chips_two_kernel(n_t, base, fc_got, pj_got, dp_own, *refs):
    dp_got, (own_o, qkv_o), sends = refs[:3], refs[3:5], refs[5:]
    total = dp_own[...]
    for r in dp_got:
        total = total + r[...].astype(F32)
    k = qkv_o.shape[2]
    for i in range(3):
        qkv_o[i] = total[:, (n_t + i) * k : (n_t + i + 1) * k]
    rows, half = fc_got.shape[1], total.shape[0] // 2
    for s in range(n_t):
        to, kind = (own_o, F32) if s == 0 else (sends[s - 1], BF16)
        for w, got in enumerate((fc_got, pj_got)):
            to[w * rows : (w + 1) * rows, :] = (base[w, s] + got[s].astype(F32)).astype(kind)
        part = total[:, s * k : (s + 1) * k].astype(kind)
        to[2 * rows :, :] = jnp.concatenate([part[:half], part[half:]], axis=1)


def tensor_sum_kernel(n_t, own, *refs):
    mine_o, send_o, out_o = refs[n_t - 1 :]
    rows, k = mine_o.shape[1], out_o.shape[0]
    total = own[...]
    for r in refs[: n_t - 1]:
        total = total + r[...].astype(F32)
    for w in range(2):
        mine_o[w] = total[2 * w * rows : (2 * w + 1) * rows]
        send_o[w] = total[(2 * w + 1) * rows : (2 * w + 2) * rows].astype(BF16)
    out_o[...] = jnp.concatenate([total[4 * rows :, 0:k], total[4 * rows :, k:]], axis=0).T


def ffn_last_kernel(scal, mine, got, fc_o, pj_o):
    first = place()[2] == 0
    for w in range(2):
        a, b = mine[w], got[w].astype(F32)
        total = jnp.concatenate([jnp.where(first, a, b), jnp.where(first, b, a)], axis=1)
        if w == 0:
            fc_o[...] = total
        else:
            pj_o[...] = total


def last_kernel(mine, got_one, got_two, x, hg, gain, out):
    g = mine[...] + got_one[0].astype(F32) + got_two[...].astype(F32)
    unit, spread_rows = row_stats(x[...].astype(F32))
    scaled = g * gain[...]
    centred = scaled - jnp.mean(scaled, axis=-1, keepdims=True)
    centred = centred - unit * jnp.mean(scaled * unit, axis=-1, keepdims=True)
    out[...] = hg[...] + spread_rows * centred


def fence(*values):
    return lax.optimization_barrier(values)


def body_four(
    block_input, doc_lengths, first_gain, first_shift, qkv_weight, attn_bias, out_weight, out_bias,
    second_gain, second_shift, fc_weight, fc_bias, proj_weight, proj_bias, block_grad,
):
    n_t = lax.axis_size("tensor")
    n_dev = n_t * 8
    rank, core, chip = lax.axis_index("tensor"), lax.axis_index("core"), lax.axis_index("chip")
    tok, width = block_input.shape
    half = tok // 2
    group = tok * n_t
    width_dev = qkv_weight.shape[2]
    heads = width_dev // HEAD_DIM
    rows_dev = qkv_weight.shape[0]
    hid = fc_weight.shape[1] // 2
    wide = 3 * width_dev
    scal = doc_lengths

    def over_tensor(block):
        return [swap_bit(block, "tensor", m) for m in range(1, n_t)]

    def over_chips(block):
        return [block] + [swap_bit(block, "chip", m) for m in (1, 2, 3)]

    small = [first_gain, first_shift, attn_bias, out_bias, second_gain, second_shift, fc_bias, proj_bias]
    sizes = [p.shape[0] for p in small]
    ffn_mine, ffn_other, out_block, qkv_rows = pcall(
        functools.partial(prep_kernel, sizes),
        [((2, rows_dev, hid), BF16)] * 2 + [((rows_dev + 16, width_dev), BF16), ((rows_dev + 16, wide), BF16)],
        scratch=[pltpu.VMEM((16, width_dev), F32)], n_scalar=1, n_in=12,
    )(scal, fc_weight, proj_weight.T, out_weight, jnp.moveaxis(qkv_weight, 1, 0), *[p.reshape(1, -1) for p in small])
    out_z = over_tensor(out_block)
    ffn_block = jnp.stack([ffn_mine, swap_core(ffn_other)], axis=1)
    grad_other = swap_core(block_grad)
    out_z, ffn_block, first, qkv_rows, out_block, grad_other = fence(
        out_z, ffn_block, block_input, qkv_rows, out_block, grad_other
    )

    row_two = swap_bit(first, "tensor", 2)
    ffn_one = swap_bit(ffn_block, "tensor", 1)
    attn_block = jnp.concatenate([out_block] + list(out_z) + [qkv_rows], axis=1)
    attn_mine = over_chips(attn_block)
    zero_x, zero_y = swap_bit(ffn_block, "chip", 1), swap_bit(ffn_block, "chip", 2)
    row_two, ffn_one, attn_mine, ffn_block, first, zero_x, zero_y = fence(
        row_two, ffn_one, attn_mine, ffn_block, first, zero_x, zero_y
    )

    row_odd = swap_bit(jnp.stack([first, row_two]), "tensor", 1)
    ffn_two = swap_bit(ffn_block, "tensor", 2)
    attn_mine = jnp.stack(attn_mine)
    diagonal = swap_bit(jnp.stack([ffn_block, ffn_one]), "chip", 3)
    ffn_zero = [ffn_block, zero_x, zero_y]
    ffn_one = [ffn_one, swap_bit(ffn_one, "chip", 1), swap_bit(ffn_one, "chip", 2)]
    row_two, row_odd, attn_mine, diagonal, ffn_zero, ffn_one, ffn_two, ffn_block = fence(
        row_two, row_odd, attn_mine, diagonal, ffn_zero, ffn_one, ffn_two, ffn_block
    )
    attn_other = swap_core(attn_mine)

    ffn_two = over_chips(ffn_two)
    ffn_three = swap_bit(ffn_block, "tensor", 3)
    vec = ((1, width), F32)
    params = pcall(
        functools.partial(unpack_kernel, sizes, n_t),
        [vec, vec, ((2 * n_t, width_dev), F32), vec, vec, vec, ((2 * n_t, hid), F32), vec],
        scratch=[pltpu.VMEM((n_dev, 8, 128), F32)], n_scalar=1, n_in=2,
    )(scal, attn_mine, attn_other)
    gain_one, shift_one, attn_shift, out_shift, gain_two, shift_two, fc_shift, proj_shift = params
    attn_outs = pcall(
        functools.partial(attn_kernel, n_t, heads),
        [((width_dev, group), BF16)] * 3 + [((8, group), F32)] + [((group, width), BF16)] * 2
        + [((width, wide), BF16)] + [((width_dev, tok), BF16)] * n_t,
        scratch=[pltpu.VMEM((n_t, width_dev, tok), BF16)],
        n_scalar=1, n_in=3 + 2 + 3, us=12,
    )(scal, block_input, row_two, row_odd, attn_mine, attn_other,
      gain_one, shift_one, attn_shift)
    attn_outs, ffn_two, ffn_three = fence(attn_outs, ffn_two, ffn_three)
    q, k, v, lse, normed_one, unit_one, w_qkv = attn_outs[:7]
    mixed = list(attn_outs[7:])
    mixed = [mixed[0]] + [swap_bit(mixed[m], "tensor", m) for m in range(1, n_t)]
    fc_three, pj_three = ffn_three[0], ffn_three[1]
    fc_x, pj_y = swap_bit(fc_three, "chip", 1), swap_bit(pj_three, "chip", 2)
    mixed, fc_three, pj_three, fc_x, pj_y = fence(mixed, fc_three, pj_three, fc_x, pj_y)
    fc_pair, pj_pair = jnp.stack([fc_three, fc_x]), jnp.stack([pj_three, pj_y])
    fc_next, pj_next = swap_bit(fc_pair, "chip", 2), swap_bit(pj_pair, "chip", 1)
    three = [fc_three, fc_x, fc_next[0], fc_next[1], pj_three, pj_next[0], pj_y, pj_next[1]]

    hidden, normed_two, mixed_all, w_out = pcall(
        functools.partial(mid_kernel, n_t),
        [((tok, width), F32), ((tok, width), BF16), ((width, tok), BF16), ((width, width), BF16)],
        n_scalar=1, n_in=n_t + 2 + 4, us=4,
    )(scal, *mixed, attn_mine, attn_other, block_input, out_shift, gain_two, shift_two)

    normed_other = swap_core(normed_two)
    cols = n_t * hid
    kept, send, act, pre, fc_sums = pcall(
        functools.partial(ffn_kernel, n_t),
        [((2, tok, width), F32), ((2, tok, width), BF16)] + [((2 * tok, cols), BF16)] * 2 + [((2 * n_t, hid), F32)],
        scratch=[pltpu.VMEM((2 * tok, width), BF16)] * 2 + [pltpu.VMEM((width, hid), BF16)] * 2
        + [pltpu.VMEM((2 * tok, width), F32)] * 2,
        n_scalar=1, n_in=5 + 19, us=13,
    )(scal, normed_two, normed_other, block_grad, grad_other, fc_shift, *ffn_zero, *ffn_one, diagonal, *ffn_two,
      *three)
    got = swap_core(send)

    stack = ((2, n_t, 2 * rows_dev, hid), BF16)
    fc_keep, fc_send, pj_keep, pj_send = pcall(
        functools.partial(ffn_grads_kernel, n_t), [stack] * 4,
        scratch=[pltpu.VMEM((2 * tok, width), BF16)] * 2 + [pltpu.VMEM((width, hid), BF16)],
        n_scalar=1, n_in=6, us=8,
    )(scal, normed_two, normed_other, block_grad, grad_other, act, pre)
    got, fc_keep, fc_send, pj_keep, pj_send = fence(got, fc_keep, fc_send, pj_keep, pj_send)
    fc_got, pj_got = swap_bit(fc_send, "chip", 1), swap_bit(pj_send, "chip", 2)

    back = pcall(
        functools.partial(back_mid_kernel, n_t),
        [((tok, width), BF16), ((tok, width), F32), ((tok, width), BF16)] + [((1, width), F32)] * 4
        + [((width_dev, tok), BF16)] * n_t,
        n_in=7, us=4,
    )(kept, got, hidden, block_grad, w_out, gain_two, proj_shift)
    block_out, hidden_grad, attn_grad, gain_two_grad, shift_two_grad, out_bias_grad, proj_bias_grad = back[:7]
    blocks = list(back[7:])
    blocks = [blocks[0]] + [swap_bit(blocks[m], "tensor", m) for m in range(1, n_t)]


    outs = pcall(
        functools.partial(attn_back_kernel, n_t, heads),
        [((2, tok, width), BF16)] + [((tok, width), F32)] * 2
        + [((wide, group), BF16), ((1, width), F32), ((1, width), F32), ((2 * n_t, width_dev), F32)],
        scratch=[
            pltpu.VMEM((n_t, width_dev, tok), BF16), pltpu.VMEM((HEAD_DIM, group), F32),
            pltpu.VMEM((HEAD_DIM, group), F32), pltpu.VMEM((n_t, tok, width), F32),
        ],
        n_scalar=1, n_in=6 + n_t, us=13,
    )(scal, q, k, v, lse, unit_one, w_qkv, *blocks)
    outs, attn_grad = fence(outs, attn_grad)
    part_odd, part_own, part_two = outs[:3]
    dqkv, gain_one_grad, shift_one_grad, bias_grads = outs[3:]
    got_one = swap_bit(part_odd, "tensor", 1)
    both = (rows_dev, width + wide)
    keep, dp_send = pcall(
        dp_grads_kernel, [((4,) + both, BF16)] * 2,
        scratch=[pltpu.VMEM((width, width), BF16), pltpu.VMEM((width, wide), BF16)], n_scalar=1, n_in=4, us=6,
    )(scal, attn_grad, mixed_all, normed_one, dqkv)
    half_stack = ((n_t, 2 * rows_dev, hid), BF16)
    base, fc_send, pj_send = pcall(
        chips_one_kernel, [((2, n_t, 2 * rows_dev, hid), F32)] + [half_stack] * 2, n_in=4,
    )(fc_keep, fc_got, pj_keep, pj_got)
    grads = [
        gain_one_grad, shift_one_grad, bias_grads.reshape(1, -1), out_bias_grad,
        gain_two_grad, shift_two_grad, fc_sums.reshape(1, -1), proj_bias_grad,
    ]
    (packed,) = pcall(functools.partial(pack_kernel, sizes), [((n_dev, 8, 128), F32)], n_in=8)(*grads)
    got_one, packed, keep, dp_send, base, fc_send, pj_send = fence(
        got_one, packed, keep, dp_send, base, fc_send, pj_send
    )

    (part_two,) = pcall(half_sum_kernel, [((tok, width), BF16)], n_in=2)(part_two, got_one)
    got_two = swap_bit(part_two, "tensor", 2)
    fc_got, pj_got = swap_bit(fc_send, "chip", 2), swap_bit(pj_send, "chip", 1)
    own = pcall(dp_core_kernel, [(both, F32)] + [(both, BF16)] * 3, n_in=2)(keep, swap_core(dp_send))
    own = [own[0]] + [swap_bit(own[m], "chip", m) for m in (1, 2, 3)]
    block = (4 * rows_dev + rows_dev // 2, hid)
    total, qkv_weight_grad, *sends = pcall(
        functools.partial(chips_two_kernel, n_t),
        [(block, F32), ((3, rows_dev, width_dev), F32)] + [(block, BF16)] * (n_t - 1), n_in=7,
    )(base, fc_got, pj_got, *own)
    got_two, total, packed, sends = fence(got_two, total, packed, sends)
    packed = lax.all_to_all(packed, EVERY, 0, 0, tiled=True)

    total = [total] + [swap_bit(sends[m - 1], "tensor", m) for m in range(1, n_t)]
    (input_grad,) = pcall(last_kernel, [((tok, width), F32)], n_in=6)(
        part_own, got_one, got_two, block_input, hidden_grad, gain_one
    )
    small_outs = pcall(functools.partial(finish_kernel, sizes), [((1, n), F32) for n in sizes], n_in=1)(packed)
    small_outs = [s.reshape(-1) for s in small_outs]
    qkv_weight_grad = jnp.moveaxis(qkv_weight_grad, 0, 1)
    total, input_grad, small_outs, qkv_weight_grad = fence(total, input_grad, small_outs, qkv_weight_grad)
    pair = (2, rows_dev, hid)
    mine, send, out_weight_grad = pcall(
        functools.partial(tensor_sum_kernel, n_t), [(pair, F32), (pair, BF16), (out_weight.shape, F32)], n_in=n_t,
    )(*total)
    fc_weight_grad, proj_weight_grad = pcall(
        ffn_last_kernel, [(fc_weight.shape, F32)] * 2, n_scalar=1, n_in=2,
    )(scal, mine, swap_core(send))
    return (
        block_out, input_grad, small_outs[0], small_outs[1], qkv_weight_grad,
        small_outs[2], out_weight_grad,
        small_outs[3], small_outs[4], small_outs[5], fc_weight_grad, small_outs[6], proj_weight_grad.T, small_outs[7],
    )


def solution(mesh):
    n_dp, n_tensor = mesh.shape["dp"], mesh.shape["tensor"]
    grid = Mesh(mesh.devices.reshape(n_dp // 2, 2, n_tensor), EVERY)
    dp = ("chip", "core")
    vec, rows, cols = P(EVERY), P(EVERY, None), P("tensor", dp)
    return jax.shard_map(
        body_four if n_dp == 8 and n_tensor == 4 else body,
        mesh=grid,
        in_specs=(
            rows, P(dp, None), vec, vec, P(dp, None, "tensor"), vec, cols, vec,
            vec, vec, P(dp, "tensor"), vec, cols, vec, rows,
        ),
        out_specs=(
            rows, rows, vec, vec, P(dp, None, "tensor"), vec, cols, vec,
            vec, vec, P(dp, "tensor"), vec, cols, vec,
        ),
        check_vma=False,
    )
```

```python
import functools
import jax
import jax.numpy as jnp
from jax import lax
from jax.experimental import pallas as pl
from jax.experimental.pallas import tpu as pltpu
from jax.sharding import Mesh, PartitionSpec as P

HEAD_DIM = 64
EPS = 1e-05
F32, BF16 = jnp.float32, jnp.bfloat16
EVERY = ("chip", "core", "tensor")


def swap_bit(values, axis, mask):
    size = lax.axis_size(axis)
    return lax.ppermute(values, axis, [(i, i ^ mask) for i in range(size)])


def swap_core(values):
    return swap_bit(values, "core", 1)


def shift_tensor(values, step):
    size = lax.axis_size("tensor")
    return lax.ppermute(values, "tensor", [(i, (i + step) % size) for i in range(size)])


def after(values, *first):
    return lax.optimization_barrier((values, *first))[0]


def sort_pieces(pieces, offsets):
    rows = pieces[0].shape[0]
    out = jnp.zeros((rows * len(pieces),) + pieces[0].shape[1:], pieces[0].dtype)
    for piece, at in zip(pieces, offsets):
        out = lax.dynamic_update_slice_in_dim(out, piece, at * rows, 0)
    return out


def gather_chips(block):
    return lax.all_gather(block, "chip", axis=0, tiled=True)


def scatter_chips(full):
    arrived = lax.all_to_all(full, "chip", 0, 0, tiled=True)
    return arrived.astype(F32).sum(axis=0)


def norm_stats(values):
    center = jnp.mean(values, axis=-1, keepdims=True)
    offset = values - center
    spread = lax.rsqrt(jnp.mean(offset * offset, axis=-1, keepdims=True) + EPS)
    return offset * spread, spread


def norm_back(grad_out, unit_rows, spread, gain_vec):
    scaled = grad_out * gain_vec
    centred = scaled - jnp.mean(scaled, axis=-1, keepdims=True)
    centred = centred - unit_rows * jnp.mean(scaled * unit_rows, axis=-1, keepdims=True)
    return spread * centred


def gelu_tanh(values):
    return jax.nn.gelu(values, approximate=True)


def score_block(query_block, key_heads, block_start, boundary, score_scale):
    block_rows = query_block.shape[0]
    key_pos = jnp.arange(key_heads.shape[0])
    query_pos = block_start + jnp.arange(block_rows)
    allowed = (key_pos[None, :] <= query_pos[:, None]) & (
        (key_pos[None, :] >= boundary) == (query_pos[:, None] >= boundary)
    )
    scores = (
        jnp.einsum("ihd,jhd->hij", query_block, key_heads, preferred_element_type=F32)
        * score_scale
    )
    return jnp.where(allowed[None], scores, -jnp.inf)


def attend(query_heads, key_heads, value_heads, boundary, score_scale):
    row_count, heads_dev, head_dim = query_heads.shape
    block_rows = min(512, row_count)
    outputs, totals = [], []
    for block_start in range(0, row_count, block_rows):
        scores = score_block(
            query_heads[block_start : block_start + block_rows],
            key_heads, block_start, boundary, score_scale,
        )
        row_peak = jnp.max(scores, axis=-1, keepdims=True)
        log_total = row_peak + jnp.log(jnp.sum(jnp.exp(scores - row_peak), axis=-1, keepdims=True))
        probs_low = jnp.exp(scores - log_total).astype(BF16)
        mixed_block = jnp.einsum("hij,jhd->ihd", probs_low, value_heads, preferred_element_type=F32)
        outputs.append(mixed_block.reshape(block_rows, heads_dev * head_dim).astype(BF16))
        totals.append(log_total)
    return jnp.concatenate(outputs, axis=0), totals


def attend_back(query_heads, key_heads, value_heads, totals, grad_heads, boundary, score_scale):
    row_count = query_heads.shape[0]
    block_rows = min(512, row_count)
    query_grads = []
    key_acc = jnp.zeros(key_heads.shape, F32)
    value_acc = jnp.zeros(value_heads.shape, F32)
    for block_index, block_start in enumerate(range(0, row_count, block_rows)):
        query_block = query_heads[block_start : block_start + block_rows]
        grad_block = grad_heads[block_start : block_start + block_rows]
        scores = score_block(query_block, key_heads, block_start, boundary, score_scale)
        probs = jnp.exp(scores - totals[block_index])
        probs_low = probs.astype(BF16)
        prob_grads = jnp.einsum("ihd,jhd->hij", grad_block, value_heads, preferred_element_type=F32)
        row_dot = jnp.sum(probs * prob_grads, axis=-1, keepdims=True)
        score_grads = (probs * (prob_grads - row_dot)).astype(BF16)
        query_grads.append(
            jnp.einsum("hij,jhd->ihd", score_grads, key_heads, preferred_element_type=F32) * score_scale
        )
        key_acc = key_acc + jnp.einsum("hij,ihd->jhd", score_grads, query_block, preferred_element_type=F32)
        value_acc = value_acc + jnp.einsum("hij,ihd->jhd", probs_low, grad_block, preferred_element_type=F32)
    return jnp.concatenate(query_grads, axis=0), key_acc * score_scale, value_acc


def body(
    block_input, doc_lengths, first_gain, first_shift, qkv_weight, attn_bias, out_weight, out_bias,
    second_gain, second_shift, fc_weight, fc_bias, proj_weight, proj_bias, block_grad,
):
    n_tensor = lax.axis_size("tensor")
    n_chip = lax.axis_size("chip")
    n_dev = n_tensor * n_chip * 2
    rank = lax.axis_index("tensor")
    core = lax.axis_index("core")
    tok, width = block_input.shape
    boundary = doc_lengths[0, 0]

    small = [first_gain, first_shift, attn_bias, out_bias, second_gain, second_shift, fc_bias, proj_bias]
    small_flat = jnp.concatenate(small)
    small_all = lax.all_to_all(
        jnp.broadcast_to(small_flat[None], (n_dev,) + small_flat.shape), EVERY, 0, 0, tiled=True
    ).astype(F32)
    params, at = [], 0
    for p in small:
        params.append(small_all[:, at : at + p.shape[0]].reshape(-1))
        at += p.shape[0]
    gain_one, shift_one, attn_shift, out_shift, gain_two, shift_two, fc_shift, proj_shift = params

    def ffn_rows(shard):
        rows, cols = shard.shape
        half = cols // 2
        mine = lax.dynamic_slice_in_dim(shard, core * half, half, 1)
        other = swap_core(lax.dynamic_slice_in_dim(shard, (1 - core) * half, half, 1))
        first = jnp.where(core == 0, mine, other)
        last = jnp.where(core == 0, other, mine)
        return jnp.concatenate([first, last], axis=0)

    def tensor_pieces(block):
        return [block] + [swap_bit(block, "tensor", m) for m in range(1, n_tensor)]

    fc_block = jnp.concatenate(tensor_pieces(ffn_rows(fc_weight)), axis=1)
    fc_full = gather_chips(fc_block)

    width_dev = qkv_weight.shape[2]
    out_t = out_weight.T
    out_block = jnp.concatenate(tensor_pieces(out_t), axis=1)
    attn_block = jnp.concatenate([qkv_weight.reshape(-1, 3 * width_dev), out_block], axis=1)
    rows_dev = attn_block.shape[0]
    attn_chips = gather_chips(attn_block).reshape(n_chip, rows_dev, -1)
    attn_other = swap_core(attn_chips)
    attn_pair = jnp.where(core == 0, jnp.stack([attn_chips, attn_other], 1), jnp.stack([attn_other, attn_chips], 1))
    attn_full = attn_pair.reshape(width, -1)
    qkv_full, out_full = attn_full[:, : 3 * width_dev], attn_full[:, 3 * width_dev :]

    half = tok // 2
    cur = [block_input[:half], block_input[half:]]
    pieces = [block_input]
    for step in range(1, n_tensor):
        cur = [shift_tensor(c, 1) for c in cur]
        pieces.append(jnp.concatenate(cur, axis=0))
    rows_in = sort_pieces(pieces, [(rank - s) % n_tensor for s in range(n_tensor)])

    proj_block = after(proj_weight.T, pieces[-1])
    proj_block = jnp.concatenate(tensor_pieces(ffn_rows(proj_block)), axis=1)
    proj_full = gather_chips(proj_block)

    unit_rows, _ = norm_stats(rows_in.astype(F32))
    normed_one = (unit_rows * gain_one + shift_one).astype(BF16)
    row_count = normed_one.shape[0]
    heads_dev = width_dev // HEAD_DIM
    score_scale = HEAD_DIM ** (-0.5)
    projected = jnp.dot(normed_one, qkv_full, preferred_element_type=F32).reshape(row_count, 3, width_dev)
    query_shift = lax.dynamic_slice_in_dim(attn_shift, rank * width_dev, width_dev)
    value_shift = lax.dynamic_slice_in_dim(attn_shift, width + rank * width_dev, width_dev)
    head_shape = (row_count, heads_dev, HEAD_DIM)
    queries = (projected[:, 0] + query_shift).astype(BF16).reshape(head_shape)
    key_rows = projected[:, 1].astype(BF16).reshape(head_shape)
    value_rows = (projected[:, 2] + value_shift).astype(BF16).reshape(head_shape)
    mixed_heads, totals = attend(queries, key_rows, value_rows, boundary, score_scale)

    def to_tokens(block_of):
        return jnp.concatenate(
            [block_of(rank)] + [swap_bit(block_of(rank ^ m), "tensor", m) for m in range(1, n_tensor)], axis=1
        )

    mixed = to_tokens(lambda z: lax.dynamic_slice_in_dim(mixed_heads, z * tok, tok, 0))

    inputs = block_input.astype(F32)
    attn_out = lax.dot_general(mixed, out_full, (((1,), (1,)), ((), ())), preferred_element_type=F32)
    hidden = inputs + (attn_out + out_shift)
    unit_two, spread_two = norm_stats(hidden)
    normed_two = (unit_two * gain_two + shift_two).astype(BF16)

    rows_two = jnp.concatenate([normed_two, swap_core(normed_two)], axis=0)
    rows_grad = jnp.concatenate([block_grad, swap_core(block_grad)], axis=0)
    fc_cols = fc_shift.reshape(n_tensor, 2, -1)
    fc_cols = lax.dynamic_index_in_dim(fc_cols, core, 1, False)
    fc_cols = jnp.stack([lax.dynamic_index_in_dim(fc_cols, rank ^ m, 0, False) for m in range(n_tensor)])
    pre_act = jnp.dot(rows_two, fc_full, preferred_element_type=F32) + fc_cols.reshape(-1)
    gelu_values, gelu_pull = jax.vjp(gelu_tanh, pre_act)
    activated = gelu_values.astype(BF16)
    act_grad = jnp.dot(rows_grad, proj_full, preferred_element_type=F32)
    pre_grad = gelu_pull(act_grad)[0].astype(BF16)
    n2g_part = lax.dot_general(pre_grad, fc_full, (((1,), (1,)), ((), ())), preferred_element_type=F32)
    normed_two_grad = n2g_part[:tok] + swap_core(n2g_part[tok:].astype(BF16)).astype(F32)
    mlp_part = lax.dot_general(activated, proj_full, (((1,), (1,)), ((), ())), preferred_element_type=F32)
    mlp_out = mlp_part[:tok] + swap_core(mlp_part[tok:].astype(BF16)).astype(F32)
    block_out = (hidden + (mlp_out + proj_shift)).astype(BF16)

    top_grad = block_grad.astype(F32)
    hidden_grad = top_grad + norm_back(normed_two_grad, unit_two, spread_two, gain_two)
    attn_grad = hidden_grad.astype(BF16)

    heads_grad = jnp.dot(attn_grad, out_full, preferred_element_type=F32).astype(BF16)
    grad_pieces = [heads_grad[:, m * width_dev : (m + 1) * width_dev] for m in range(n_tensor)]
    grad_pieces = [grad_pieces[0]] + [swap_bit(grad_pieces[m], "tensor", m) for m in range(1, n_tensor)]
    heads_rows = sort_pieces(grad_pieces, [rank ^ m for m in range(n_tensor)])

    def ffn_scatter(partial):
        cols = partial.shape[1]
        block = scatter_chips(partial.reshape(n_chip, -1, cols))
        part = cols // n_tensor
        total = block[:, :part]
        for m in range(1, n_tensor):
            total = total + swap_bit(block[:, m * part : (m + 1) * part].astype(BF16), "tensor", m).astype(F32)
        rows = total.shape[0] // 2
        mine = lax.dynamic_slice_in_dim(total, core * rows, rows, 0)
        other = swap_core(lax.dynamic_slice_in_dim(total, (1 - core) * rows, rows, 0))
        first = jnp.where(core == 0, mine, other)
        last = jnp.where(core == 0, other, mine)
        return jnp.concatenate([first, last], axis=1)

    proj_grad = lax.dot_general(rows_grad, activated, (((0,), (0,)), ((), ())), preferred_element_type=F32)
    proj_weight_grad = ffn_scatter(proj_grad.astype(BF16)).T
    fc_grad = lax.dot_general(rows_two, pre_grad, (((0,), (0,)), ((), ())), preferred_element_type=F32)
    fc_weight_grad = ffn_scatter(fc_grad.astype(BF16))

    def core_scatter(partial):
        cols = partial.shape[1]
        split = partial.reshape(n_chip, 2, -1, cols)
        keep = lax.dynamic_index_in_dim(split, core, 1, False)
        send = lax.dynamic_index_in_dim(split, 1 - core, 1, False)
        return keep.astype(F32) + swap_core(send.astype(BF16)).astype(F32)

    out_grad = lax.dot_general(attn_grad, mixed, (((0,), (0,)), ((), ())), preferred_element_type=F32)
    out_block_grad = scatter_chips(core_scatter(out_grad).astype(BF16))
    out_total = out_block_grad[:, :width_dev]
    for m in range(1, n_tensor):
        piece = out_block_grad[:, m * width_dev : (m + 1) * width_dev].astype(BF16)
        out_total = out_total + swap_bit(piece, "tensor", m).astype(F32)
    out_weight_grad = out_total.T

    query_grad, key_grad, value_grad = attend_back(
        queries, key_rows, value_rows, totals, heads_rows.reshape(head_shape), boundary, score_scale
    )
    flat_shape = (row_count, width_dev)
    query_low = query_grad.reshape(flat_shape).astype(BF16)
    key_low = key_grad.reshape(flat_shape).astype(BF16)
    value_low = value_grad.reshape(flat_shape).astype(BF16)
    projection_grads = jnp.concatenate([query_low, key_low, value_low], axis=1)
    n1g_part = lax.dot_general(projection_grads, qkv_full, (((1,), (1,)), ((), ())), preferred_element_type=F32)
    n1g_blocks = n1g_part.reshape(n_tensor, tok, width)

    def part_block(z):
        return lax.dynamic_index_in_dim(n1g_blocks, z % n_tensor, 0, False)

    running = part_block(rank - 1)
    acc = [running[:half], running[half:]]
    for step in range(1, n_tensor):
        mine = part_block(rank - 1 - step)
        acc = [
            shift_tensor(a.astype(BF16), 1).astype(F32) + m
            for a, m in zip(acc, (mine[:half], mine[half:]))
        ]
    normed_one_grad = jnp.concatenate(acc, axis=0)

    first_gain_grad = jnp.sum(n1g_part * unit_rows, axis=0)
    first_shift_grad = jnp.sum(n1g_part, axis=0)
    zeros = jnp.zeros((2 * width,), F32)
    attn_bias_grad = lax.dynamic_update_slice_in_dim(
        zeros, jnp.sum(query_low.astype(F32), axis=0), rank * width_dev, 0
    )
    attn_bias_grad = lax.dynamic_update_slice_in_dim(
        attn_bias_grad, jnp.sum(value_low.astype(F32), axis=0), width + rank * width_dev, 0
    )
    out_bias_grad = jnp.sum(attn_grad.astype(F32), axis=0)
    second_gain_grad = jnp.sum(normed_two_grad * unit_two, axis=0)
    second_shift_grad = jnp.sum(normed_two_grad, axis=0)
    proj_bias_grad = jnp.sum(top_grad, axis=0)
    fc_sums = jnp.sum(pre_grad.astype(F32), axis=0).reshape(n_tensor, -1)
    fc_bias_grad = jnp.zeros((n_tensor, 2, fc_sums.shape[1]), F32)
    for m in range(n_tensor):
        fc_bias_grad = lax.dynamic_update_slice(fc_bias_grad, fc_sums[m][None, None], (rank ^ m, core, 0))
    fc_bias_grad = fc_bias_grad.reshape(-1)

    smalls = [
        first_gain_grad, first_shift_grad, attn_bias_grad, out_bias_grad,
        second_gain_grad, second_shift_grad, fc_bias_grad, proj_bias_grad,
    ]
    small_grads = jnp.concatenate([g.reshape(n_dev, -1) for g in smalls], axis=1)
    small_grads = lax.all_to_all(small_grads, EVERY, 0, 0, tiled=True).sum(axis=0)
    small_outs, at = [], 0
    for g in smalls:
        n = g.shape[0] // n_dev
        small_outs.append(small_grads[at : at + n])
        at += n

    qkv_grad = lax.dot_general(normed_one, projection_grads, (((0,), (0,)), ((), ())), preferred_element_type=F32)
    qkv_weight_grad = scatter_chips(core_scatter(qkv_grad).astype(BF16)).reshape(qkv_weight.shape)

    own_unit, own_spread = norm_stats(inputs)
    input_grad = hidden_grad + norm_back(normed_one_grad, own_unit, own_spread, gain_one)
    return (
        block_out, input_grad, small_outs[0], small_outs[1], qkv_weight_grad, small_outs[2], out_weight_grad,
        small_outs[3], small_outs[4], small_outs[5], fc_weight_grad, small_outs[6], proj_weight_grad, small_outs[7],
    )


def pcall(kernel, outs, scratch=(), n_scalar=0, n_in=0, us=2, flops=0):
    whole = pl.BlockSpec(memory_space=pltpu.VMEM)
    return pl.pallas_call(
        kernel,
        in_specs=[pl.BlockSpec(memory_space=pltpu.SMEM)] * n_scalar + [whole] * n_in,
        out_specs=[whole] * len(outs),
        out_shape=[jax.ShapeDtypeStruct(s, d) for s, d in outs],
        scratch_shapes=list(scratch),
        cost_estimate=pl.CostEstimate(flops=max(1, flops), bytes_accessed=max(1, flops // 300), transcendentals=0),
        compiler_params=pltpu.CompilerParams(vmem_limit_bytes=56 * 1024 * 1024),
    )


def place():
    return lax.axis_index("tensor"), lax.axis_index("chip"), lax.axis_index("core")


def dg(a, b, ca, cb):
    return lax.dot_general(a, b, (((ca,), (cb,)), ((), ())), preferred_element_type=F32)


def prep_kernel(sizes, scal, fc, proj_t, out_w, qkv, *refs):
    ins, (mine, other, block, rows_o, tile) = refs[: len(sizes)], refs[len(sizes) :]
    core = place()[2]
    half = mine.shape[2]
    rows = fc.shape[0]
    for to, side in ((mine, core), (other, 1 - core)):
        lanes = pl.ds(pl.multiple_of(side * half, 128), half)
        to[0] = fc[:, lanes]
        to[1] = proj_t[:, lanes]
    tile[...] = jnp.zeros_like(tile)
    for i, n in enumerate(sizes):
        tile[i : i + 1, 0:n] = ins[i][...].astype(F32)
    block[0:rows, :] = out_w[...].T
    block[rows:, :] = tile[...].astype(BF16)
    third = qkv.shape[2]
    rows_o[rows:, :] = jnp.zeros((16, rows_o.shape[1]), BF16)
    for i in range(3):
        rows_o[0:rows, i * third : (i + 1) * third] = qkv[i]


def spread(n, cols):
    lane = lax.broadcasted_iota(jnp.int32, (128, cols), 1).astype(F32)
    row = lax.broadcasted_iota(jnp.int32, (128, cols), 0).astype(F32)
    rest = lane - n * jnp.floor((lane + 0.5) * (1.0 / n))
    return jnp.where(rest == row, 1.0, 0.0)


def owner(n, rows, cols):
    lane = lax.broadcasted_iota(jnp.int32, (rows, cols), 1)
    first = lax.broadcasted_iota(jnp.int32, (rows, cols), 0) * n
    return (lane >= first) & (lane < first + n)


def unpack_kernel(sizes, n_t, scal, mine, other, *refs):
    outs, every = refs[:-1], refs[-1]
    rank, chip, core = place()
    n_dev = every.shape[0]
    rows = mine.shape[1] - 16
    wide = outs[2].shape[1]
    for m in range(4):
        for j, ref in ((0, mine), (1, other)):
            for s in range(n_t):
                at = ((chip ^ m) * 2 + (core ^ j)) * n_t + (rank ^ s)
                every[at] = ref[m, rows : rows + 16, s * wide : s * wide + 128].astype(F32)[0:8]
    values = every[...]
    cached = {}
    for i, n in enumerate(sizes):
        cols = n * n_dev
        if n not in cached:
            cached[n] = (spread(n, cols).astype(BF16), owner(n, n_dev, cols))
        full = jnp.dot(values[:, i, :].astype(BF16), cached[n][0], preferred_element_type=F32)
        full = jnp.sum(jnp.where(cached[n][1], full, 0.0), axis=0, keepdims=True)
        lanes = outs[i].shape[1]
        for r in range(outs[i].shape[0]):
            outs[i][r : r + 1, :] = full[:, r * lanes : (r + 1) * lanes]


def pack_kernel(sizes, *refs):
    ins, out = refs[: len(sizes)], refs[len(sizes)]
    n_dev = out.shape[0]
    cached = {}
    for i, n in enumerate(sizes):
        cols = n * n_dev
        if n not in cached:
            cached[n] = (spread(n, cols), owner(n, n_dev, cols))
        rows = jnp.where(cached[n][1], ins[i][...], 0.0)
        out[:, i, :] = lax.dot_general(
            rows, cached[n][0], (((1,), (1,)), ((), ())),
            precision=lax.Precision.HIGHEST, preferred_element_type=F32,
        )


def finish_kernel(sizes, all_ref, *outs):
    total = jnp.sum(all_ref[...], axis=0)
    for i, n in enumerate(sizes):
        outs[i][...] = total[i : i + 1, 0:n]


def row_stats(values):
    center = jnp.mean(values, axis=-1, keepdims=True)
    offset = values - center
    spread_rows = lax.rsqrt(jnp.mean(offset * offset, axis=-1, keepdims=True) + EPS)
    return offset * spread_rows, spread_rows


def mask_of(boundary, first, block, keys):
    qpos = first + lax.broadcasted_iota(jnp.int32, (keys, block), 1)
    kpos = lax.broadcasted_iota(jnp.int32, (keys, block), 0)
    low = jnp.where(qpos >= boundary, boundary, 0)
    return (kpos >= low) & (kpos <= qpos)


LOG2E = 1.4426950408889634


def attn_kernel(n_t, heads, *refs):
    (scal,) = refs[:1]
    own, two, odd = refs[1:4]
    at = 4
    stacks = refs[at : at + 2]
    gain, shift, bias = refs[at + 2 : at + 5]
    outs = refs[at + 5 :]
    q_o, k_o, v_o, lse_o, normed_o, unit_o, w_o = outs[:7]
    send = outs[7 : 7 + n_t]
    mixed = outs[7 + n_t]
    rank, chip, core, boundary = (*place(), scal[0, 0])
    tok, width = own.shape
    wide = w_o.shape[1]
    rows_dev = stacks[0].shape[1] - 16
    for m in range(4):
        for j in range(2):
            to = pl.multiple_of(((chip ^ m) * 2 + (core ^ j)) * rows_dev, 16)
            w_o[pl.ds(to, rows_dev), :] = stacks[j][m, 0:rows_dev, width : width + wide]

    def put(values, to):
        unit, _ = row_stats(values.astype(F32))
        unit_o[pl.ds(to, values.shape[0]), :] = unit.astype(BF16)
        normed_o[pl.ds(to, values.shape[0]), :] = (unit * gain[...] + shift[...]).astype(BF16)

    put(own[...], pl.multiple_of(rank * tok, tok))
    put(two[...], pl.multiple_of((rank ^ 2) * tok, tok))
    put(odd[0], pl.multiple_of((rank ^ 1) * tok, tok))
    put(odd[1], pl.multiple_of((rank ^ 3) * tok, tok))
    third = wide // 3
    qb = bias[pl.ds(rank, 1), :]
    vb = bias[pl.ds(n_t + rank, 1), :]
    projected = jnp.dot(normed_o[...], w_o[...], preferred_element_type=F32)
    zero = jnp.zeros_like(qb)
    full_bias = jnp.concatenate([qb, zero, vb], axis=1)
    flipped = (projected + full_bias).astype(BF16).T
    q_o[...] = flipped[0:third]
    k_o[...] = flipped[third : 2 * third]
    v_o[...] = flipped[2 * third : 3 * third]
    lse_o[...] = jnp.zeros_like(lse_o)
    masks = [mask_of(boundary, b * tok, tok, (b + 1) * tok) for b in range(n_t)]
    for h in range(heads):
        lo, hi = h * HEAD_DIM, (h + 1) * HEAD_DIM
        keys = k_o[lo:hi, :].T
        for b in range(n_t):
            n = (b + 1) * tok
            cols = slice(b * tok, n)
            scores = dg(keys[0:n], q_o[lo:hi, cols], 1, 0) * (HEAD_DIM**-0.5 * LOG2E)
            scores = jnp.where(masks[b], scores, -jnp.inf)
            peak = jnp.max(scores, axis=0, keepdims=True)
            probs = jnp.exp2(scores - peak)
            total = jnp.sum(probs, axis=0, keepdims=True)
            lse_o[h : h + 1, cols] = peak + jnp.log2(total)
            out = jnp.dot(v_o[lo:hi, 0:n], probs.astype(BF16), preferred_element_type=F32)
            mixed[b, lo:hi, :] = (out * (1.0 / total)).astype(BF16)
    for s in range(n_t):
        send[s][...] = mixed[rank ^ s]


def mid_kernel(n_t, *refs):
    scal = refs[0]
    blocks = refs[1 : 1 + n_t]
    stacks = refs[1 + n_t : 3 + n_t]
    x, bias, gain, shift = refs[3 + n_t : 7 + n_t]
    hidden_o, normed_o, mixed_o, w_o = refs[7 + n_t :]
    chip, core = place()[1:]
    width = x.shape[1]
    rows_dev = stacks[0].shape[1] - 16
    for m in range(4):
        for j in range(2):
            to = pl.multiple_of(((chip ^ m) * 2 + (core ^ j)) * rows_dev, 16)
            w_o[pl.ds(to, rows_dev), :] = stacks[j][m, 0:rows_dev, 0:width]
    k = blocks[0].shape[0]
    for s in range(n_t):
        mixed_o[s * k : (s + 1) * k, :] = blocks[s][...]
    attn = dg(mixed_o[...], w_o[...], 0, 1)
    hidden = x[...].astype(F32) + (attn + bias[...])
    hidden_o[...] = hidden
    unit, _ = row_stats(hidden)
    normed_o[...] = (unit * gain[...] + shift[...]).astype(BF16)


def ffn_kernel(n_t, *refs):
    scal = refs[0]
    own, other, g_own, g_other, bias = refs[1:6]
    zero, one, diagonal, two, fc_three, pj_three = refs[6:9], refs[9:12], refs[12], refs[13:17], refs[17:21], refs[21:25]
    outs = refs[25:]
    whole = [[*zero, diagonal.at[0]], [*one, diagonal.at[1]], two]
    pieces = [[[p.at[w] for p in group] for w in range(2)] for group in whole]
    pieces.append([list(fc_three), list(pj_three)])
    own_o, send_o, act_o, pre_o, sums_o, x_s, g_s, fc_s, pj_s, mlp_s, n2_s = outs
    rank, chip, core = place()
    tok = own.shape[0]
    x_s[0:tok] = own[...]
    x_s[tok:] = other[...]
    g_s[0:tok] = g_own[...]
    g_s[tok:] = g_other[...]
    cols = fc_three[0].shape[2]
    rows = fc_three[0].shape[1]
    c0 = 0.7978845608028654
    sums_o[...] = jnp.zeros_like(sums_o)
    for s in range(n_t):
        for w, to_ref in ((0, fc_s), (1, pj_s)):
            for m in range(4):
                for j in range(2):
                    to = pl.multiple_of(((chip ^ m) * 2 + (core ^ j)) * rows, 16)
                    to_ref[pl.ds(to, rows), :] = pieces[s][w][m][j]
        fc_w, pj_w = fc_s[...], pj_s[...]
        lanes = slice(s * cols, (s + 1) * cols)
        b = bias[pl.ds((rank ^ s) * 2 + core, 1), :]
        z = jnp.dot(x_s[...], fc_w, preferred_element_type=F32) + b
        ga = jnp.dot(g_s[...], pj_w, preferred_element_type=F32)
        zz = z * z
        t = jnp.tanh(z * (c0 + (c0 * 0.044715) * zz))
        up = 0.5 + 0.5 * t
        act = (z * up).astype(BF16)
        slope = up + (0.5 * z) * (1.0 - t * t) * (c0 + (3.0 * c0 * 0.044715) * zz)
        pre = (ga * slope).astype(BF16)
        act_o[:, lanes] = act
        pre_o[:, lanes] = pre
        sums_o[pl.ds((rank ^ s) * 2 + core, 1), :] = jnp.sum(pre.astype(F32), axis=0, keepdims=True)
        mlp = dg(act, pj_w, 1, 1)
        n2 = dg(pre, fc_w, 1, 1)
        if s == 0:
            mlp_s[...] = mlp
            n2_s[...] = n2
        else:
            mlp_s[...] += mlp
            n2_s[...] += n2
    for i, ref in ((0, mlp_s), (1, n2_s)):
        own_o[i] = ref[0:tok]
        send_o[i] = ref[tok:].astype(BF16)


def ffn_grads_kernel(n_t, *refs):
    scal, own, other, g_own, g_other, act, pre = refs[:7]
    fc_keep, fc_send, pj_keep, pj_send, x_s, g_s, tmp = refs[7:]
    chip, core = place()[1:]
    tok = own.shape[0]
    x_s[0:tok] = own[...]
    x_s[tok:] = other[...]
    g_s[0:tok] = g_own[...]
    g_s[tok:] = g_other[...]
    cols = fc_keep.shape[3]
    rows = fc_keep.shape[2] // 2
    for w, (left, right, keep, send, keep_m, send_m) in enumerate((
        (g_s, act, pj_keep, pj_send, (0, 1), (2, 3)),
        (x_s, pre, fc_keep, fc_send, (0, 2), (1, 3)),
    )):
        for s in range(n_t):
            tmp[...] = dg(left[...], right[:, s * cols : (s + 1) * cols], 0, 0).astype(BF16)
            for to, ms in ((keep, keep_m), (send, send_m)):
                for i, m in enumerate(ms):
                    for j in range(2):
                        at = pl.multiple_of(((chip ^ m) * 2 + (core ^ j)) * rows, 16)
                        to[i, s, j * rows : (j + 1) * rows] = tmp[pl.ds(at, rows), :]


def back_mid_kernel(n_t, *refs):
    kept, got, hidden, grad, w, gain, proj_bias = refs[:7]
    block_out, hg_o, attn_o, gain_o, shift_o, outb_o, projb_o = refs[7:14]
    blocks = refs[14 : 14 + n_t]
    hid = hidden[...]
    top = grad[...].astype(F32)
    g = kept[1] + got[1].astype(F32)
    unit, spread_rows = row_stats(hid)
    gain_o[...] = jnp.sum(g * unit, axis=0, keepdims=True)
    shift_o[...] = jnp.sum(g, axis=0, keepdims=True)
    projb_o[...] = jnp.sum(top, axis=0, keepdims=True)
    scaled = g * gain[...]
    centred = scaled - jnp.mean(scaled, axis=-1, keepdims=True)
    centred = centred - unit * jnp.mean(scaled * unit, axis=-1, keepdims=True)
    hg = top + spread_rows * centred
    hg_o[...] = hg
    low = hg.astype(BF16)
    attn_o[...] = low
    outb_o[...] = jnp.sum(low.astype(F32), axis=0, keepdims=True)
    heads = dg(w[...], low, 0, 1).astype(BF16)
    k = blocks[0].shape[0]
    for s in range(n_t):
        blocks[s][...] = heads[s * k : (s + 1) * k]
    block_out[...] = (hid + (kept[0] + got[0].astype(F32) + proj_bias[...])).astype(BF16)


def attn_back_kernel(n_t, heads, *refs):
    scal, q, k, v, lse, unit, w = refs[:7]
    grads = refs[7 : 7 + n_t]
    outs = refs[7 + n_t :]
    p_o = outs[:3]
    dqkv_o, gain_o, shift_o, bias_o, g_s, dk_s, dv_s, n1_s = outs[3:]
    rank, boundary = place()[0], scal[0, 0]
    tok = grads[0].shape[1]
    third = q.shape[0]
    for s in range(n_t):
        g_s[rank ^ s] = grads[s][...]
    masks = [mask_of(boundary, b * tok, tok, (b + 1) * tok) for b in range(n_t)]
    scale = HEAD_DIM**-0.5
    for h in range(heads):
        lo, hi = h * HEAD_DIM, (h + 1) * HEAD_DIM
        keys = k[lo:hi, :].T
        vals = v[lo:hi, :].T
        dk_s[...] = jnp.zeros_like(dk_s)
        dv_s[...] = jnp.zeros_like(dv_s)
        for b in range(n_t):
            n = (b + 1) * tok
            cols = slice(b * tok, n)
            qb = q[lo:hi, cols]
            gb = g_s[b, lo:hi, :]
            scores = dg(keys[0:n], qb, 1, 0) * (scale * LOG2E)
            probs = jnp.exp2(jnp.where(masks[b], scores - lse[h : h + 1, cols], -jnp.inf))
            pg = dg(vals[0:n], gb, 1, 0)
            dot = jnp.sum(probs * pg, axis=0, keepdims=True)
            ds = (probs * (pg - dot)).astype(BF16)
            low = probs.astype(BF16)
            dq = jnp.dot(k[lo:hi, 0:n], ds, preferred_element_type=F32) * scale
            dqkv_o[lo:hi, cols] = dq.astype(BF16)
            dk_s[:, 0:n] += dg(qb, ds, 1, 1)
            dv_s[:, 0:n] += dg(gb, low, 1, 1)
        dqkv_o[third + lo : third + hi, :] = (dk_s[...] * scale).astype(BF16)
        dqkv_o[2 * third + lo : 2 * third + hi, :] = dv_s[...].astype(BF16)
    flat = dqkv_o[...]
    n1 = dg(flat, w[...], 0, 1)
    n1_s[...] = n1.reshape(n1_s.shape)
    gain_o[...] = jnp.sum(n1 * unit[...].astype(F32), axis=0, keepdims=True)
    shift_o[...] = jnp.sum(n1, axis=0, keepdims=True)
    ones = jnp.ones((8, flat.shape[1]), BF16)
    sums = dg(ones, flat, 1, 1)
    bias_o[...] = jnp.zeros_like(bias_o)
    bias_o[pl.ds(rank, 1), :] = sums[0:1, 0:third]
    bias_o[pl.ds(n_t + rank, 1), :] = sums[0:1, 2 * third : 3 * third]
    p_o[0][0] = n1_s[rank ^ 1].astype(BF16)
    p_o[0][1] = n1_s[rank ^ 3].astype(BF16)
    p_o[1][...] = n1_s[rank]
    p_o[2][...] = n1_s[rank ^ 2]


def half_sum_kernel(mine, got, send):
    send[...] = (mine[...] + got[1].astype(F32)).astype(BF16)


def dp_grads_kernel(scal, attn_grad, mixed, normed, dqkv, keep_o, send_o, out_s, qkv_s):
    chip, core = place()[1:]
    rows = keep_o.shape[1]
    width = out_s.shape[1]
    out_s[...] = dg(attn_grad[...], mixed[...], 0, 1).astype(BF16)
    qkv_s[...] = dg(normed[...], dqkv[...], 0, 1).astype(BF16)
    for m in range(4):
        for j, to in ((0, keep_o), (1, send_o)):
            at = pl.multiple_of(((chip ^ m) * 2 + (core ^ j)) * rows, 16)
            to[m, :, 0:width] = out_s[pl.ds(at, rows), :]
            to[m, :, width:] = qkv_s[pl.ds(at, rows), :]


def dp_core_kernel(keep, got, own_o, *sends):
    for m in range(4):
        total = keep[m].astype(F32) + got[m].astype(F32)
        if m == 0:
            own_o[...] = total
        else:
            sends[m - 1][...] = total.astype(BF16)


def chips_one_kernel(fc_keep, fc_got, pj_keep, pj_got, base_o, fc_send, pj_send):
    for w, (keep, got, send) in enumerate(((fc_keep, fc_got, fc_send), (pj_keep, pj_got, pj_send))):
        base_o[w] = keep[0].astype(F32) + got[0].astype(F32)
        send[...] = (keep[1].astype(F32) + got[1].astype(F32)).astype(BF16)


def chips_two_kernel(n_t, base, fc_got, pj_got, dp_own, *refs):
    dp_got, (own_o, qkv_o), sends = refs[:3], refs[3:5], refs[5:]
    total = dp_own[...]
    for r in dp_got:
        total = total + r[...].astype(F32)
    k = qkv_o.shape[2]
    for i in range(3):
        qkv_o[i] = total[:, (n_t + i) * k : (n_t + i + 1) * k]
    rows, half = fc_got.shape[1], total.shape[0] // 2
    for s in range(n_t):
        to, kind = (own_o, F32) if s == 0 else (sends[s - 1], BF16)
        for w, got in enumerate((fc_got, pj_got)):
            to[w * rows : (w + 1) * rows, :] = (base[w, s] + got[s].astype(F32)).astype(kind)
        part = total[:, s * k : (s + 1) * k].astype(kind)
        to[2 * rows :, :] = jnp.concatenate([part[:half], part[half:]], axis=1)


def tensor_sum_kernel(n_t, own, *refs):
    mine_o, send_o, out_o = refs[n_t - 1 :]
    rows, k = mine_o.shape[1], out_o.shape[0]
    total = own[...]
    for r in refs[: n_t - 1]:
        total = total + r[...].astype(F32)
    for w in range(2):
        mine_o[w] = total[2 * w * rows : (2 * w + 1) * rows]
        send_o[w] = total[(2 * w + 1) * rows : (2 * w + 2) * rows].astype(BF16)
    out_o[...] = jnp.concatenate([total[4 * rows :, 0:k], total[4 * rows :, k:]], axis=0).T


def ffn_last_kernel(scal, mine, got, fc_o, pj_o):
    first = place()[2] == 0
    for w in range(2):
        a, b = mine[w], got[w].astype(F32)
        total = jnp.concatenate([jnp.where(first, a, b), jnp.where(first, b, a)], axis=1)
        if w == 0:
            fc_o[...] = total
        else:
            pj_o[...] = total


def last_kernel(mine, got_one, got_two, x, hg, gain, out):
    g = mine[...] + got_one[0].astype(F32) + got_two[...].astype(F32)
    unit, spread_rows = row_stats(x[...].astype(F32))
    scaled = g * gain[...]
    centred = scaled - jnp.mean(scaled, axis=-1, keepdims=True)
    centred = centred - unit * jnp.mean(scaled * unit, axis=-1, keepdims=True)
    out[...] = hg[...] + spread_rows * centred


def fence(*values):
    return lax.optimization_barrier(values)


def body_four(
    block_input, doc_lengths, first_gain, first_shift, qkv_weight, attn_bias, out_weight, out_bias,
    second_gain, second_shift, fc_weight, fc_bias, proj_weight, proj_bias, block_grad,
):
    n_t = lax.axis_size("tensor")
    n_dev = n_t * 8
    rank, core, chip = lax.axis_index("tensor"), lax.axis_index("core"), lax.axis_index("chip")
    tok, width = block_input.shape
    half = tok // 2
    group = tok * n_t
    width_dev = qkv_weight.shape[2]
    heads = width_dev // HEAD_DIM
    rows_dev = qkv_weight.shape[0]
    hid = fc_weight.shape[1] // 2
    wide = 3 * width_dev
    scal = doc_lengths

    def over_tensor(block):
        return [swap_bit(block, "tensor", m) for m in range(1, n_t)]

    def over_chips(block):
        return [block] + [swap_bit(block, "chip", m) for m in (1, 2, 3)]

    small = [first_gain, first_shift, attn_bias, out_bias, second_gain, second_shift, fc_bias, proj_bias]
    sizes = [p.shape[0] for p in small]
    ffn_mine, ffn_other, out_block, qkv_rows = pcall(
        functools.partial(prep_kernel, sizes),
        [((2, rows_dev, hid), BF16)] * 2 + [((rows_dev + 16, width_dev), BF16), ((rows_dev + 16, wide), BF16)],
        scratch=[pltpu.VMEM((16, width_dev), F32)], n_scalar=1, n_in=12,
    )(scal, fc_weight, proj_weight.T, out_weight, jnp.moveaxis(qkv_weight, 1, 0), *[p.reshape(1, -1) for p in small])
    out_z = over_tensor(out_block)
    ffn_block = jnp.stack([ffn_mine, swap_core(ffn_other)], axis=1)
    grad_other = swap_core(block_grad)
    out_z, ffn_block, first, qkv_rows, out_block, grad_other = fence(
        out_z, ffn_block, block_input, qkv_rows, out_block, grad_other
    )

    row_two = swap_bit(first, "tensor", 2)
    ffn_one = swap_bit(ffn_block, "tensor", 1)
    attn_block = jnp.concatenate([out_block] + list(out_z) + [qkv_rows], axis=1)
    attn_mine = over_chips(attn_block)
    zero_x, zero_y = swap_bit(ffn_block, "chip", 1), swap_bit(ffn_block, "chip", 2)
    row_two, ffn_one, attn_mine, ffn_block, first, zero_x, zero_y = fence(
        row_two, ffn_one, attn_mine, ffn_block, first, zero_x, zero_y
    )

    row_odd = swap_bit(jnp.stack([first, row_two]), "tensor", 1)
    ffn_two = swap_bit(ffn_block, "tensor", 2)
    attn_mine = jnp.stack(attn_mine)
    diagonal = swap_bit(jnp.stack([ffn_block, ffn_one]), "chip", 3)
    ffn_zero = [ffn_block, zero_x, zero_y]
    ffn_one = [ffn_one, swap_bit(ffn_one, "chip", 1), swap_bit(ffn_one, "chip", 2)]
    row_two, row_odd, attn_mine, diagonal, ffn_zero, ffn_one, ffn_two, ffn_block = fence(
        row_two, row_odd, attn_mine, diagonal, ffn_zero, ffn_one, ffn_two, ffn_block
    )
    attn_other = swap_core(attn_mine)

    ffn_two = over_chips(ffn_two)
    ffn_three = swap_bit(ffn_block, "tensor", 3)
    vec = ((1, width), F32)
    params = pcall(
        functools.partial(unpack_kernel, sizes, n_t),
        [vec, vec, ((2 * n_t, width_dev), F32), vec, vec, vec, ((2 * n_t, hid), F32), vec],
        scratch=[pltpu.VMEM((n_dev, 8, 128), F32)], n_scalar=1, n_in=2,
    )(scal, attn_mine, attn_other)
    gain_one, shift_one, attn_shift, out_shift, gain_two, shift_two, fc_shift, proj_shift = params
    attn_outs = pcall(
        functools.partial(attn_kernel, n_t, heads),
        [((width_dev, group), BF16)] * 3 + [((8, group), F32)] + [((group, width), BF16)] * 2
        + [((width, wide), BF16)] + [((width_dev, tok), BF16)] * n_t,
        scratch=[pltpu.VMEM((n_t, width_dev, tok), BF16)],
        n_scalar=1, n_in=3 + 2 + 3, us=12,
    )(scal, block_input, row_two, row_odd, attn_mine, attn_other,
      gain_one, shift_one, attn_shift)
    attn_outs, ffn_two, ffn_three = fence(attn_outs, ffn_two, ffn_three)
    q, k, v, lse, normed_one, unit_one, w_qkv = attn_outs[:7]
    mixed = list(attn_outs[7:])
    mixed = [mixed[0]] + [swap_bit(mixed[m], "tensor", m) for m in range(1, n_t)]
    fc_three, pj_three = ffn_three[0], ffn_three[1]
    fc_x, pj_y = swap_bit(fc_three, "chip", 1), swap_bit(pj_three, "chip", 2)
    mixed, fc_three, pj_three, fc_x, pj_y = fence(mixed, fc_three, pj_three, fc_x, pj_y)
    fc_pair, pj_pair = jnp.stack([fc_three, fc_x]), jnp.stack([pj_three, pj_y])
    fc_next, pj_next = swap_bit(fc_pair, "chip", 2), swap_bit(pj_pair, "chip", 1)
    three = [fc_three, fc_x, fc_next[0], fc_next[1], pj_three, pj_next[0], pj_y, pj_next[1]]

    hidden, normed_two, mixed_all, w_out = pcall(
        functools.partial(mid_kernel, n_t),
        [((tok, width), F32), ((tok, width), BF16), ((width, tok), BF16), ((width, width), BF16)],
        n_scalar=1, n_in=n_t + 2 + 4, us=4,
    )(scal, *mixed, attn_mine, attn_other, block_input, out_shift, gain_two, shift_two)

    normed_other = swap_core(normed_two)
    cols = n_t * hid
    kept, send, act, pre, fc_sums = pcall(
        functools.partial(ffn_kernel, n_t),
        [((2, tok, width), F32), ((2, tok, width), BF16)] + [((2 * tok, cols), BF16)] * 2 + [((2 * n_t, hid), F32)],
        scratch=[pltpu.VMEM((2 * tok, width), BF16)] * 2 + [pltpu.VMEM((width, hid), BF16)] * 2
        + [pltpu.VMEM((2 * tok, width), F32)] * 2,
        n_scalar=1, n_in=5 + 19, us=13,
    )(scal, normed_two, normed_other, block_grad, grad_other, fc_shift, *ffn_zero, *ffn_one, diagonal, *ffn_two,
      *three)
    got = swap_core(send)

    back = pcall(
        functools.partial(back_mid_kernel, n_t),
        [((tok, width), BF16), ((tok, width), F32), ((tok, width), BF16)] + [((1, width), F32)] * 4
        + [((width_dev, tok), BF16)] * n_t,
        n_in=7, us=4,
    )(kept, got, hidden, block_grad, w_out, gain_two, proj_shift)
    block_out, hidden_grad, attn_grad, gain_two_grad, shift_two_grad, out_bias_grad, proj_bias_grad = back[:7]
    blocks = list(back[7:])
    blocks = [blocks[0]] + [swap_bit(blocks[m], "tensor", m) for m in range(1, n_t)]


    stack = ((2, n_t, 2 * rows_dev, hid), BF16)
    fc_keep, fc_send, pj_keep, pj_send = pcall(
        functools.partial(ffn_grads_kernel, n_t), [stack] * 4,
        scratch=[pltpu.VMEM((2 * tok, width), BF16)] * 2 + [pltpu.VMEM((width, hid), BF16)],
        n_scalar=1, n_in=6, flops=8 * 10**9,
    )(scal, normed_two, normed_other, block_grad, grad_other, after(act, back[7]), pre)
    fc_got, pj_got = swap_bit(fc_send, "chip", 1), swap_bit(pj_send, "chip", 2)
    q, blocks, fc_keep, pj_keep = fence(q, blocks, fc_keep, pj_keep)

    outs = pcall(
        functools.partial(attn_back_kernel, n_t, heads),
        [((2, tok, width), BF16)] + [((tok, width), F32)] * 2
        + [((wide, group), BF16), ((1, width), F32), ((1, width), F32), ((2 * n_t, width_dev), F32)],
        scratch=[
            pltpu.VMEM((n_t, width_dev, tok), BF16), pltpu.VMEM((HEAD_DIM, group), F32),
            pltpu.VMEM((HEAD_DIM, group), F32), pltpu.VMEM((n_t, tok, width), F32),
        ],
        n_scalar=1, n_in=6 + n_t, flops=14 * 10**9,
    )(scal, q, k, v, lse, unit_one, w_qkv, *blocks)
    outs, attn_grad = fence(outs, attn_grad)
    part_odd, part_own, part_two = outs[:3]
    dqkv, gain_one_grad, shift_one_grad, bias_grads = outs[3:]
    got_one = swap_bit(part_odd, "tensor", 1)
    both = (rows_dev, width + wide)
    keep, dp_send = pcall(
        dp_grads_kernel, [((4,) + both, BF16)] * 2,
        scratch=[pltpu.VMEM((width, width), BF16), pltpu.VMEM((width, wide), BF16)], n_scalar=1, n_in=4, us=6,
    )(scal, attn_grad, mixed_all, normed_one, dqkv)
    half_stack = ((n_t, 2 * rows_dev, hid), BF16)
    base, fc_send, pj_send = pcall(
        chips_one_kernel, [((2, n_t, 2 * rows_dev, hid), F32)] + [half_stack] * 2, n_in=4,
    )(fc_keep, fc_got, pj_keep, pj_got)
    grads = [
        gain_one_grad, shift_one_grad, bias_grads.reshape(1, -1), out_bias_grad,
        gain_two_grad, shift_two_grad, fc_sums.reshape(1, -1), proj_bias_grad,
    ]
    (packed,) = pcall(functools.partial(pack_kernel, sizes), [((n_dev, 8, 128), F32)], n_in=8)(*grads)
    got_one, packed, keep, dp_send, base, fc_send, pj_send = fence(
        got_one, packed, keep, dp_send, base, fc_send, pj_send
    )

    (part_two,) = pcall(half_sum_kernel, [((tok, width), BF16)], n_in=2)(part_two, got_one)
    got_two = swap_bit(part_two, "tensor", 2)
    packed = lax.all_to_all(packed, EVERY, 0, 0, tiled=True)
    fc_got, pj_got = swap_bit(fc_send, "chip", 2), swap_bit(pj_send, "chip", 1)
    own = pcall(dp_core_kernel, [(both, F32)] + [(both, BF16)] * 3, n_in=2, flops=14 * 10**9)(keep, swap_core(dp_send))
    own = [own[0]] + [swap_bit(own[m], "chip", m) for m in (1, 2, 3)]
    block = (4 * rows_dev + rows_dev // 2, hid)
    total, qkv_weight_grad, *sends = pcall(
        functools.partial(chips_two_kernel, n_t),
        [(block, F32), ((3, rows_dev, width_dev), F32)] + [(block, BF16)] * (n_t - 1), n_in=7,
    )(base, fc_got, pj_got, *own)
    got_two, total, packed, sends = fence(got_two, total, packed, sends)

    total = [total] + [swap_bit(sends[m - 1], "tensor", m) for m in range(1, n_t)]
    (input_grad,) = pcall(last_kernel, [((tok, width), F32)], n_in=6)(
        part_own, got_one, got_two, block_input, hidden_grad, gain_one
    )
    small_outs = pcall(functools.partial(finish_kernel, sizes), [((1, n), F32) for n in sizes], n_in=1)(packed)
    small_outs = [s.reshape(-1) for s in small_outs]
    qkv_weight_grad = jnp.moveaxis(qkv_weight_grad, 0, 1)
    total, input_grad, small_outs, qkv_weight_grad = fence(total, input_grad, small_outs, qkv_weight_grad)
    pair = (2, rows_dev, hid)
    mine, send, out_weight_grad = pcall(
        functools.partial(tensor_sum_kernel, n_t), [(pair, F32), (pair, BF16), (out_weight.shape, F32)], n_in=n_t,
    )(*total)
    fc_weight_grad, proj_weight_grad = pcall(
        ffn_last_kernel, [(fc_weight.shape, F32)] * 2, n_scalar=1, n_in=2,
    )(scal, mine, swap_core(send))
    return (
        block_out, input_grad, small_outs[0], small_outs[1], qkv_weight_grad,
        small_outs[2], out_weight_grad,
        small_outs[3], small_outs[4], small_outs[5], fc_weight_grad, small_outs[6], proj_weight_grad.T, small_outs[7],
    )


def solution(mesh):
    n_dp, n_tensor = mesh.shape["dp"], mesh.shape["tensor"]
    grid = Mesh(mesh.devices.reshape(n_dp // 2, 2, n_tensor), EVERY)
    dp = ("chip", "core")
    vec, rows, cols = P(EVERY), P(EVERY, None), P("tensor", dp)
    return jax.shard_map(
        body_four if n_dp == 8 and n_tensor == 4 else body,
        mesh=grid,
        in_specs=(
            rows, P(dp, None), vec, vec, P(dp, None, "tensor"), vec, cols, vec,
            vec, vec, P(dp, "tensor"), vec, cols, vec, rows,
        ),
        out_specs=(
            rows, rows, vec, vec, P(dp, None, "tensor"), vec, cols, vec,
            vec, vec, P(dp, "tensor"), vec, cols, vec,
        ),
        check_vma=False,
    )
```

```python
import functools
import jax
import jax.numpy as jnp
from jax import lax
from jax.experimental import pallas as pl
from jax.experimental.pallas import tpu as pltpu
from jax.sharding import Mesh, PartitionSpec as P

HEAD_DIM = 64
EPS = 1e-05
F32, BF16 = jnp.float32, jnp.bfloat16
EVERY = ("chip", "core", "tensor")


def swap_bit(values, axis, mask):
    size = lax.axis_size(axis)
    return lax.ppermute(values, axis, [(i, i ^ mask) for i in range(size)])


def swap_core(values):
    return swap_bit(values, "core", 1)


def shift_tensor(values, step):
    size = lax.axis_size("tensor")
    return lax.ppermute(values, "tensor", [(i, (i + step) % size) for i in range(size)])


def after(values, *first):
    return lax.optimization_barrier((values, *first))[0]


def sort_pieces(pieces, offsets):
    rows = pieces[0].shape[0]
    out = jnp.zeros((rows * len(pieces),) + pieces[0].shape[1:], pieces[0].dtype)
    for piece, at in zip(pieces, offsets):
        out = lax.dynamic_update_slice_in_dim(out, piece, at * rows, 0)
    return out


def gather_chips(block):
    return lax.all_gather(block, "chip", axis=0, tiled=True)


def scatter_chips(full):
    arrived = lax.all_to_all(full, "chip", 0, 0, tiled=True)
    return arrived.astype(F32).sum(axis=0)


def norm_stats(values):
    center = jnp.mean(values, axis=-1, keepdims=True)
    offset = values - center
    spread = lax.rsqrt(jnp.mean(offset * offset, axis=-1, keepdims=True) + EPS)
    return offset * spread, spread


def norm_back(grad_out, unit_rows, spread, gain_vec):
    scaled = grad_out * gain_vec
    centred = scaled - jnp.mean(scaled, axis=-1, keepdims=True)
    centred = centred - unit_rows * jnp.mean(scaled * unit_rows, axis=-1, keepdims=True)
    return spread * centred


def gelu_tanh(values):
    return jax.nn.gelu(values, approximate=True)


def score_block(query_block, key_heads, block_start, boundary, score_scale):
    block_rows = query_block.shape[0]
    key_pos = jnp.arange(key_heads.shape[0])
    query_pos = block_start + jnp.arange(block_rows)
    allowed = (key_pos[None, :] <= query_pos[:, None]) & (
        (key_pos[None, :] >= boundary) == (query_pos[:, None] >= boundary)
    )
    scores = (
        jnp.einsum("ihd,jhd->hij", query_block, key_heads, preferred_element_type=F32)
        * score_scale
    )
    return jnp.where(allowed[None], scores, -jnp.inf)


def attend(query_heads, key_heads, value_heads, boundary, score_scale):
    row_count, heads_dev, head_dim = query_heads.shape
    block_rows = min(512, row_count)
    outputs, totals = [], []
    for block_start in range(0, row_count, block_rows):
        scores = score_block(
            query_heads[block_start : block_start + block_rows],
            key_heads, block_start, boundary, score_scale,
        )
        row_peak = jnp.max(scores, axis=-1, keepdims=True)
        log_total = row_peak + jnp.log(jnp.sum(jnp.exp(scores - row_peak), axis=-1, keepdims=True))
        probs_low = jnp.exp(scores - log_total).astype(BF16)
        mixed_block = jnp.einsum("hij,jhd->ihd", probs_low, value_heads, preferred_element_type=F32)
        outputs.append(mixed_block.reshape(block_rows, heads_dev * head_dim).astype(BF16))
        totals.append(log_total)
    return jnp.concatenate(outputs, axis=0), totals


def attend_back(query_heads, key_heads, value_heads, totals, grad_heads, boundary, score_scale):
    row_count = query_heads.shape[0]
    block_rows = min(512, row_count)
    query_grads = []
    key_acc = jnp.zeros(key_heads.shape, F32)
    value_acc = jnp.zeros(value_heads.shape, F32)
    for block_index, block_start in enumerate(range(0, row_count, block_rows)):
        query_block = query_heads[block_start : block_start + block_rows]
        grad_block = grad_heads[block_start : block_start + block_rows]
        scores = score_block(query_block, key_heads, block_start, boundary, score_scale)
        probs = jnp.exp(scores - totals[block_index])
        probs_low = probs.astype(BF16)
        prob_grads = jnp.einsum("ihd,jhd->hij", grad_block, value_heads, preferred_element_type=F32)
        row_dot = jnp.sum(probs * prob_grads, axis=-1, keepdims=True)
        score_grads = (probs * (prob_grads - row_dot)).astype(BF16)
        query_grads.append(
            jnp.einsum("hij,jhd->ihd", score_grads, key_heads, preferred_element_type=F32) * score_scale
        )
        key_acc = key_acc + jnp.einsum("hij,ihd->jhd", score_grads, query_block, preferred_element_type=F32)
        value_acc = value_acc + jnp.einsum("hij,ihd->jhd", probs_low, grad_block, preferred_element_type=F32)
    return jnp.concatenate(query_grads, axis=0), key_acc * score_scale, value_acc


def body(
    block_input, doc_lengths, first_gain, first_shift, qkv_weight, attn_bias, out_weight, out_bias,
    second_gain, second_shift, fc_weight, fc_bias, proj_weight, proj_bias, block_grad,
):
    n_tensor = lax.axis_size("tensor")
    n_chip = lax.axis_size("chip")
    n_dev = n_tensor * n_chip * 2
    rank = lax.axis_index("tensor")
    core = lax.axis_index("core")
    tok, width = block_input.shape
    boundary = doc_lengths[0, 0]

    small = [first_gain, first_shift, attn_bias, out_bias, second_gain, second_shift, fc_bias, proj_bias]
    small_flat = jnp.concatenate(small)
    small_all = lax.all_to_all(
        jnp.broadcast_to(small_flat[None], (n_dev,) + small_flat.shape), EVERY, 0, 0, tiled=True
    ).astype(F32)
    params, at = [], 0
    for p in small:
        params.append(small_all[:, at : at + p.shape[0]].reshape(-1))
        at += p.shape[0]
    gain_one, shift_one, attn_shift, out_shift, gain_two, shift_two, fc_shift, proj_shift = params

    def ffn_rows(shard):
        rows, cols = shard.shape
        half = cols // 2
        mine = lax.dynamic_slice_in_dim(shard, core * half, half, 1)
        other = swap_core(lax.dynamic_slice_in_dim(shard, (1 - core) * half, half, 1))
        first = jnp.where(core == 0, mine, other)
        last = jnp.where(core == 0, other, mine)
        return jnp.concatenate([first, last], axis=0)

    def tensor_pieces(block):
        return [block] + [swap_bit(block, "tensor", m) for m in range(1, n_tensor)]

    fc_block = jnp.concatenate(tensor_pieces(ffn_rows(fc_weight)), axis=1)
    fc_full = gather_chips(fc_block)

    width_dev = qkv_weight.shape[2]
    out_t = out_weight.T
    out_block = jnp.concatenate(tensor_pieces(out_t), axis=1)
    attn_block = jnp.concatenate([qkv_weight.reshape(-1, 3 * width_dev), out_block], axis=1)
    rows_dev = attn_block.shape[0]
    attn_chips = gather_chips(attn_block).reshape(n_chip, rows_dev, -1)
    attn_other = swap_core(attn_chips)
    attn_pair = jnp.where(core == 0, jnp.stack([attn_chips, attn_other], 1), jnp.stack([attn_other, attn_chips], 1))
    attn_full = attn_pair.reshape(width, -1)
    qkv_full, out_full = attn_full[:, : 3 * width_dev], attn_full[:, 3 * width_dev :]

    half = tok // 2
    cur = [block_input[:half], block_input[half:]]
    pieces = [block_input]
    for step in range(1, n_tensor):
        cur = [shift_tensor(c, 1) for c in cur]
        pieces.append(jnp.concatenate(cur, axis=0))
    rows_in = sort_pieces(pieces, [(rank - s) % n_tensor for s in range(n_tensor)])

    proj_block = after(proj_weight.T, pieces[-1])
    proj_block = jnp.concatenate(tensor_pieces(ffn_rows(proj_block)), axis=1)
    proj_full = gather_chips(proj_block)

    unit_rows, _ = norm_stats(rows_in.astype(F32))
    normed_one = (unit_rows * gain_one + shift_one).astype(BF16)
    row_count = normed_one.shape[0]
    heads_dev = width_dev // HEAD_DIM
    score_scale = HEAD_DIM ** (-0.5)
    projected = jnp.dot(normed_one, qkv_full, preferred_element_type=F32).reshape(row_count, 3, width_dev)
    query_shift = lax.dynamic_slice_in_dim(attn_shift, rank * width_dev, width_dev)
    value_shift = lax.dynamic_slice_in_dim(attn_shift, width + rank * width_dev, width_dev)
    head_shape = (row_count, heads_dev, HEAD_DIM)
    queries = (projected[:, 0] + query_shift).astype(BF16).reshape(head_shape)
    key_rows = projected[:, 1].astype(BF16).reshape(head_shape)
    value_rows = (projected[:, 2] + value_shift).astype(BF16).reshape(head_shape)
    mixed_heads, totals = attend(queries, key_rows, value_rows, boundary, score_scale)

    def to_tokens(block_of):
        return jnp.concatenate(
            [block_of(rank)] + [swap_bit(block_of(rank ^ m), "tensor", m) for m in range(1, n_tensor)], axis=1
        )

    mixed = to_tokens(lambda z: lax.dynamic_slice_in_dim(mixed_heads, z * tok, tok, 0))

    inputs = block_input.astype(F32)
    attn_out = lax.dot_general(mixed, out_full, (((1,), (1,)), ((), ())), preferred_element_type=F32)
    hidden = inputs + (attn_out + out_shift)
    unit_two, spread_two = norm_stats(hidden)
    normed_two = (unit_two * gain_two + shift_two).astype(BF16)

    rows_two = jnp.concatenate([normed_two, swap_core(normed_two)], axis=0)
    rows_grad = jnp.concatenate([block_grad, swap_core(block_grad)], axis=0)
    fc_cols = fc_shift.reshape(n_tensor, 2, -1)
    fc_cols = lax.dynamic_index_in_dim(fc_cols, core, 1, False)
    fc_cols = jnp.stack([lax.dynamic_index_in_dim(fc_cols, rank ^ m, 0, False) for m in range(n_tensor)])
    pre_act = jnp.dot(rows_two, fc_full, preferred_element_type=F32) + fc_cols.reshape(-1)
    gelu_values, gelu_pull = jax.vjp(gelu_tanh, pre_act)
    activated = gelu_values.astype(BF16)
    act_grad = jnp.dot(rows_grad, proj_full, preferred_element_type=F32)
    pre_grad = gelu_pull(act_grad)[0].astype(BF16)
    n2g_part = lax.dot_general(pre_grad, fc_full, (((1,), (1,)), ((), ())), preferred_element_type=F32)
    normed_two_grad = n2g_part[:tok] + swap_core(n2g_part[tok:].astype(BF16)).astype(F32)
    mlp_part = lax.dot_general(activated, proj_full, (((1,), (1,)), ((), ())), preferred_element_type=F32)
    mlp_out = mlp_part[:tok] + swap_core(mlp_part[tok:].astype(BF16)).astype(F32)
    block_out = (hidden + (mlp_out + proj_shift)).astype(BF16)

    top_grad = block_grad.astype(F32)
    hidden_grad = top_grad + norm_back(normed_two_grad, unit_two, spread_two, gain_two)
    attn_grad = hidden_grad.astype(BF16)

    heads_grad = jnp.dot(attn_grad, out_full, preferred_element_type=F32).astype(BF16)
    grad_pieces = [heads_grad[:, m * width_dev : (m + 1) * width_dev] for m in range(n_tensor)]
    grad_pieces = [grad_pieces[0]] + [swap_bit(grad_pieces[m], "tensor", m) for m in range(1, n_tensor)]
    heads_rows = sort_pieces(grad_pieces, [rank ^ m for m in range(n_tensor)])

    def ffn_scatter(partial):
        cols = partial.shape[1]
        block = scatter_chips(partial.reshape(n_chip, -1, cols))
        part = cols // n_tensor
        total = block[:, :part]
        for m in range(1, n_tensor):
            total = total + swap_bit(block[:, m * part : (m + 1) * part].astype(BF16), "tensor", m).astype(F32)
        rows = total.shape[0] // 2
        mine = lax.dynamic_slice_in_dim(total, core * rows, rows, 0)
        other = swap_core(lax.dynamic_slice_in_dim(total, (1 - core) * rows, rows, 0))
        first = jnp.where(core == 0, mine, other)
        last = jnp.where(core == 0, other, mine)
        return jnp.concatenate([first, last], axis=1)

    proj_grad = lax.dot_general(rows_grad, activated, (((0,), (0,)), ((), ())), preferred_element_type=F32)
    proj_weight_grad = ffn_scatter(proj_grad.astype(BF16)).T
    fc_grad = lax.dot_general(rows_two, pre_grad, (((0,), (0,)), ((), ())), preferred_element_type=F32)
    fc_weight_grad = ffn_scatter(fc_grad.astype(BF16))

    def core_scatter(partial):
        cols = partial.shape[1]
        split = partial.reshape(n_chip, 2, -1, cols)
        keep = lax.dynamic_index_in_dim(split, core, 1, False)
        send = lax.dynamic_index_in_dim(split, 1 - core, 1, False)
        return keep.astype(F32) + swap_core(send.astype(BF16)).astype(F32)

    out_grad = lax.dot_general(attn_grad, mixed, (((0,), (0,)), ((), ())), preferred_element_type=F32)
    out_block_grad = scatter_chips(core_scatter(out_grad).astype(BF16))
    out_total = out_block_grad[:, :width_dev]
    for m in range(1, n_tensor):
        piece = out_block_grad[:, m * width_dev : (m + 1) * width_dev].astype(BF16)
        out_total = out_total + swap_bit(piece, "tensor", m).astype(F32)
    out_weight_grad = out_total.T

    query_grad, key_grad, value_grad = attend_back(
        queries, key_rows, value_rows, totals, heads_rows.reshape(head_shape), boundary, score_scale
    )
    flat_shape = (row_count, width_dev)
    query_low = query_grad.reshape(flat_shape).astype(BF16)
    key_low = key_grad.reshape(flat_shape).astype(BF16)
    value_low = value_grad.reshape(flat_shape).astype(BF16)
    projection_grads = jnp.concatenate([query_low, key_low, value_low], axis=1)
    n1g_part = lax.dot_general(projection_grads, qkv_full, (((1,), (1,)), ((), ())), preferred_element_type=F32)
    n1g_blocks = n1g_part.reshape(n_tensor, tok, width)

    def part_block(z):
        return lax.dynamic_index_in_dim(n1g_blocks, z % n_tensor, 0, False)

    running = part_block(rank - 1)
    acc = [running[:half], running[half:]]
    for step in range(1, n_tensor):
        mine = part_block(rank - 1 - step)
        acc = [
            shift_tensor(a.astype(BF16), 1).astype(F32) + m
            for a, m in zip(acc, (mine[:half], mine[half:]))
        ]
    normed_one_grad = jnp.concatenate(acc, axis=0)

    first_gain_grad = jnp.sum(n1g_part * unit_rows, axis=0)
    first_shift_grad = jnp.sum(n1g_part, axis=0)
    zeros = jnp.zeros((2 * width,), F32)
    attn_bias_grad = lax.dynamic_update_slice_in_dim(
        zeros, jnp.sum(query_low.astype(F32), axis=0), rank * width_dev, 0
    )
    attn_bias_grad = lax.dynamic_update_slice_in_dim(
        attn_bias_grad, jnp.sum(value_low.astype(F32), axis=0), width + rank * width_dev, 0
    )
    out_bias_grad = jnp.sum(attn_grad.astype(F32), axis=0)
    second_gain_grad = jnp.sum(normed_two_grad * unit_two, axis=0)
    second_shift_grad = jnp.sum(normed_two_grad, axis=0)
    proj_bias_grad = jnp.sum(top_grad, axis=0)
    fc_sums = jnp.sum(pre_grad.astype(F32), axis=0).reshape(n_tensor, -1)
    fc_bias_grad = jnp.zeros((n_tensor, 2, fc_sums.shape[1]), F32)
    for m in range(n_tensor):
        fc_bias_grad = lax.dynamic_update_slice(fc_bias_grad, fc_sums[m][None, None], (rank ^ m, core, 0))
    fc_bias_grad = fc_bias_grad.reshape(-1)

    smalls = [
        first_gain_grad, first_shift_grad, attn_bias_grad, out_bias_grad,
        second_gain_grad, second_shift_grad, fc_bias_grad, proj_bias_grad,
    ]
    small_grads = jnp.concatenate([g.reshape(n_dev, -1) for g in smalls], axis=1)
    small_grads = lax.all_to_all(small_grads, EVERY, 0, 0, tiled=True).sum(axis=0)
    small_outs, at = [], 0
    for g in smalls:
        n = g.shape[0] // n_dev
        small_outs.append(small_grads[at : at + n])
        at += n

    qkv_grad = lax.dot_general(normed_one, projection_grads, (((0,), (0,)), ((), ())), preferred_element_type=F32)
    qkv_weight_grad = scatter_chips(core_scatter(qkv_grad).astype(BF16)).reshape(qkv_weight.shape)

    own_unit, own_spread = norm_stats(inputs)
    input_grad = hidden_grad + norm_back(normed_one_grad, own_unit, own_spread, gain_one)
    return (
        block_out, input_grad, small_outs[0], small_outs[1], qkv_weight_grad, small_outs[2], out_weight_grad,
        small_outs[3], small_outs[4], small_outs[5], fc_weight_grad, small_outs[6], proj_weight_grad, small_outs[7],
    )


def pcall(kernel, outs, scratch=(), n_scalar=0, n_in=0, us=2, flops=0):
    whole = pl.BlockSpec(memory_space=pltpu.VMEM)
    return pl.pallas_call(
        kernel,
        in_specs=[pl.BlockSpec(memory_space=pltpu.SMEM)] * n_scalar + [whole] * n_in,
        out_specs=[whole] * len(outs),
        out_shape=[jax.ShapeDtypeStruct(s, d) for s, d in outs],
        scratch_shapes=list(scratch),
        cost_estimate=pl.CostEstimate(flops=max(1, flops), bytes_accessed=max(1, flops // 300), transcendentals=0),
        compiler_params=pltpu.CompilerParams(vmem_limit_bytes=56 * 1024 * 1024),
    )


def place():
    return lax.axis_index("tensor"), lax.axis_index("chip"), lax.axis_index("core")


def dg(a, b, ca, cb):
    return lax.dot_general(a, b, (((ca,), (cb,)), ((), ())), preferred_element_type=F32)


def prep_kernel(sizes, scal, fc, proj_t, out_w, qkv, *refs):
    ins, (mine, other, block, rows_o, tile) = refs[: len(sizes)], refs[len(sizes) :]
    core = place()[2]
    half = mine.shape[2]
    rows = fc.shape[0]
    for to, side in ((mine, core), (other, 1 - core)):
        lanes = pl.ds(pl.multiple_of(side * half, 128), half)
        to[0] = fc[:, lanes]
        to[1] = proj_t[:, lanes]
    tile[...] = jnp.zeros_like(tile)
    for i, n in enumerate(sizes):
        tile[i : i + 1, 0:n] = ins[i][...].astype(F32)
    block[0:rows, :] = out_w[...].T
    block[rows:, :] = tile[...].astype(BF16)
    third = qkv.shape[2]
    rows_o[rows:, :] = jnp.zeros((16, rows_o.shape[1]), BF16)
    for i in range(3):
        rows_o[0:rows, i * third : (i + 1) * third] = qkv[i]


def spread(n, cols):
    lane = lax.broadcasted_iota(jnp.int32, (128, cols), 1).astype(F32)
    row = lax.broadcasted_iota(jnp.int32, (128, cols), 0).astype(F32)
    rest = lane - n * jnp.floor((lane + 0.5) * (1.0 / n))
    return jnp.where(rest == row, 1.0, 0.0)


def owner(n, rows, cols):
    lane = lax.broadcasted_iota(jnp.int32, (rows, cols), 1)
    first = lax.broadcasted_iota(jnp.int32, (rows, cols), 0) * n
    return (lane >= first) & (lane < first + n)


def unpack_kernel(sizes, n_t, scal, mine, other, *refs):
    outs, every = refs[:-1], refs[-1]
    rank, chip, core = place()
    n_dev = every.shape[0]
    rows = mine.shape[1] - 16
    wide = outs[2].shape[1]
    for m in range(4):
        for j, ref in ((0, mine), (1, other)):
            for s in range(n_t):
                at = ((chip ^ m) * 2 + (core ^ j)) * n_t + (rank ^ s)
                every[at] = ref[m, rows : rows + 16, s * wide : s * wide + 128].astype(F32)[0:8]
    values = every[...]
    cached = {}
    for i, n in enumerate(sizes):
        cols = n * n_dev
        if n not in cached:
            cached[n] = (spread(n, cols).astype(BF16), owner(n, n_dev, cols))
        full = jnp.dot(values[:, i, :].astype(BF16), cached[n][0], preferred_element_type=F32)
        full = jnp.sum(jnp.where(cached[n][1], full, 0.0), axis=0, keepdims=True)
        lanes = outs[i].shape[1]
        for r in range(outs[i].shape[0]):
            outs[i][r : r + 1, :] = full[:, r * lanes : (r + 1) * lanes]


def pack_kernel(sizes, *refs):
    ins, out = refs[: len(sizes)], refs[len(sizes)]
    n_dev = out.shape[0]
    cached = {}
    for i, n in enumerate(sizes):
        cols = n * n_dev
        if n not in cached:
            cached[n] = (spread(n, cols), owner(n, n_dev, cols))
        rows = jnp.where(cached[n][1], ins[i][...], 0.0)
        out[:, i, :] = lax.dot_general(
            rows, cached[n][0], (((1,), (1,)), ((), ())),
            precision=lax.Precision.HIGHEST, preferred_element_type=F32,
        )


def finish_kernel(sizes, all_ref, *outs):
    total = jnp.sum(all_ref[...], axis=0)
    for i, n in enumerate(sizes):
        outs[i][...] = total[i : i + 1, 0:n]


def row_stats(values):
    center = jnp.mean(values, axis=-1, keepdims=True)
    offset = values - center
    spread_rows = lax.rsqrt(jnp.mean(offset * offset, axis=-1, keepdims=True) + EPS)
    return offset * spread_rows, spread_rows


def mask_of(boundary, first, block, keys):
    qpos = first + lax.broadcasted_iota(jnp.int32, (keys, block), 1)
    kpos = lax.broadcasted_iota(jnp.int32, (keys, block), 0)
    low = jnp.where(qpos >= boundary, boundary, 0)
    return (kpos >= low) & (kpos <= qpos)


LOG2E = 1.4426950408889634


def attn_kernel(n_t, heads, *refs):
    (scal,) = refs[:1]
    own, two, odd = refs[1:4]
    at = 4
    stacks = refs[at : at + 2]
    gain, shift, bias = refs[at + 2 : at + 5]
    outs = refs[at + 5 :]
    q_o, k_o, v_o, lse_o, normed_o, unit_o, w_o = outs[:7]
    send = outs[7 : 7 + n_t]
    mixed = outs[7 + n_t]
    rank, chip, core, boundary = (*place(), scal[0, 0])
    tok, width = own.shape
    wide = w_o.shape[1]
    rows_dev = stacks[0].shape[1] - 16
    for m in range(4):
        for j in range(2):
            to = pl.multiple_of(((chip ^ m) * 2 + (core ^ j)) * rows_dev, 16)
            w_o[pl.ds(to, rows_dev), :] = stacks[j][m, 0:rows_dev, width : width + wide]

    def put(values, to):
        unit, _ = row_stats(values.astype(F32))
        unit_o[pl.ds(to, values.shape[0]), :] = unit.astype(BF16)
        normed_o[pl.ds(to, values.shape[0]), :] = (unit * gain[...] + shift[...]).astype(BF16)

    put(own[...], pl.multiple_of(rank * tok, tok))
    put(two[...], pl.multiple_of((rank ^ 2) * tok, tok))
    put(odd[0], pl.multiple_of((rank ^ 1) * tok, tok))
    put(odd[1], pl.multiple_of((rank ^ 3) * tok, tok))
    third = wide // 3
    qb = bias[pl.ds(rank, 1), :]
    vb = bias[pl.ds(n_t + rank, 1), :]
    projected = jnp.dot(normed_o[...], w_o[...], preferred_element_type=F32)
    zero = jnp.zeros_like(qb)
    full_bias = jnp.concatenate([qb, zero, vb], axis=1)
    flipped = (projected + full_bias).astype(BF16).T
    q_o[...] = flipped[0:third]
    k_o[...] = flipped[third : 2 * third]
    v_o[...] = flipped[2 * third : 3 * third]
    lse_o[...] = jnp.zeros_like(lse_o)
    masks = [mask_of(boundary, b * tok, tok, (b + 1) * tok) for b in range(n_t)]
    for h in range(heads):
        lo, hi = h * HEAD_DIM, (h + 1) * HEAD_DIM
        keys = k_o[lo:hi, :].T
        for b in range(n_t):
            n = (b + 1) * tok
            cols = slice(b * tok, n)
            scores = dg(keys[0:n], q_o[lo:hi, cols], 1, 0) * (HEAD_DIM**-0.5 * LOG2E)
            scores = jnp.where(masks[b], scores, -jnp.inf)
            peak = jnp.max(scores, axis=0, keepdims=True)
            probs = jnp.exp2(scores - peak)
            total = jnp.sum(probs, axis=0, keepdims=True)
            lse_o[h : h + 1, cols] = peak + jnp.log2(total)
            out = jnp.dot(v_o[lo:hi, 0:n], probs.astype(BF16), preferred_element_type=F32)
            mixed[b, lo:hi, :] = (out * (1.0 / total)).astype(BF16)
    for s in range(n_t):
        send[s][...] = mixed[rank ^ s]


def mid_kernel(n_t, *refs):
    scal = refs[0]
    blocks = refs[1 : 1 + n_t]
    stacks = refs[1 + n_t : 3 + n_t]
    x, bias, gain, shift = refs[3 + n_t : 7 + n_t]
    hidden_o, normed_o, mixed_o, w_o = refs[7 + n_t :]
    chip, core = place()[1:]
    width = x.shape[1]
    rows_dev = stacks[0].shape[1] - 16
    for m in range(4):
        for j in range(2):
            to = pl.multiple_of(((chip ^ m) * 2 + (core ^ j)) * rows_dev, 16)
            w_o[pl.ds(to, rows_dev), :] = stacks[j][m, 0:rows_dev, 0:width]
    k = blocks[0].shape[0]
    for s in range(n_t):
        mixed_o[s * k : (s + 1) * k, :] = blocks[s][...]
    attn = dg(mixed_o[...], w_o[...], 0, 1)
    hidden = x[...].astype(F32) + (attn + bias[...])
    hidden_o[...] = hidden
    unit, _ = row_stats(hidden)
    normed_o[...] = (unit * gain[...] + shift[...]).astype(BF16)


def ffn_kernel(n_t, *refs):
    scal = refs[0]
    own, other, g_own, g_other, bias = refs[1:6]
    zero, one, diagonal, two, fc_three, pj_three = refs[6:9], refs[9:12], refs[12], refs[13:17], refs[17:21], refs[21:25]
    outs = refs[25:]
    whole = [[*zero, diagonal.at[0]], [*one, diagonal.at[1]], two]
    pieces = [[[p.at[w] for p in group] for w in range(2)] for group in whole]
    pieces.append([list(fc_three), list(pj_three)])
    own_o, send_o, act_o, pre_o, sums_o, x_s, g_s, fc_s, pj_s, mlp_s, n2_s = outs
    rank, chip, core = place()
    tok = own.shape[0]
    x_s[0:tok] = own[...]
    x_s[tok:] = other[...]
    g_s[0:tok] = g_own[...]
    g_s[tok:] = g_other[...]
    cols = fc_three[0].shape[2]
    rows = fc_three[0].shape[1]
    c0 = 0.7978845608028654
    sums_o[...] = jnp.zeros_like(sums_o)
    for s in range(n_t):
        for w, to_ref in ((0, fc_s), (1, pj_s)):
            for m in range(4):
                for j in range(2):
                    to = pl.multiple_of(((chip ^ m) * 2 + (core ^ j)) * rows, 16)
                    to_ref[pl.ds(to, rows), :] = pieces[s][w][m][j]
        fc_w, pj_w = fc_s[...], pj_s[...]
        lanes = slice(s * cols, (s + 1) * cols)
        b = bias[pl.ds((rank ^ s) * 2 + core, 1), :]
        z = jnp.dot(x_s[...], fc_w, preferred_element_type=F32) + b
        ga = jnp.dot(g_s[...], pj_w, preferred_element_type=F32)
        zz = z * z
        t = jnp.tanh(z * (c0 + (c0 * 0.044715) * zz))
        up = 0.5 + 0.5 * t
        act = (z * up).astype(BF16)
        slope = up + (0.5 * z) * (1.0 - t * t) * (c0 + (3.0 * c0 * 0.044715) * zz)
        pre = (ga * slope).astype(BF16)
        act_o[:, lanes] = act
        pre_o[:, lanes] = pre
        sums_o[pl.ds((rank ^ s) * 2 + core, 1), :] = jnp.sum(pre.astype(F32), axis=0, keepdims=True)
        mlp = dg(act, pj_w, 1, 1)
        n2 = dg(pre, fc_w, 1, 1)
        if s == 0:
            mlp_s[...] = mlp
            n2_s[...] = n2
        else:
            mlp_s[...] += mlp
            n2_s[...] += n2
    for i, ref in ((0, mlp_s), (1, n2_s)):
        own_o[i] = ref[0:tok]
        send_o[i] = ref[tok:].astype(BF16)


def ffn_grads_kernel(n_t, *refs):
    scal, own, other, g_own, g_other, act, pre = refs[:7]
    fc_keep, fc_send, pj_keep, pj_send, x_s, g_s, tmp = refs[7:]
    chip, core = place()[1:]
    tok = own.shape[0]
    x_s[0:tok] = own[...]
    x_s[tok:] = other[...]
    g_s[0:tok] = g_own[...]
    g_s[tok:] = g_other[...]
    cols = fc_keep.shape[3]
    rows = fc_keep.shape[2] // 2
    for w, (left, right, keep, send, keep_m, send_m) in enumerate((
        (g_s, act, pj_keep, pj_send, (0, 1), (2, 3)),
        (x_s, pre, fc_keep, fc_send, (0, 2), (1, 3)),
    )):
        for s in range(n_t):
            tmp[...] = dg(left[...], right[:, s * cols : (s + 1) * cols], 0, 0).astype(BF16)
            for to, ms in ((keep, keep_m), (send, send_m)):
                for i, m in enumerate(ms):
                    for j in range(2):
                        at = pl.multiple_of(((chip ^ m) * 2 + (core ^ j)) * rows, 16)
                        to[i, s, j * rows : (j + 1) * rows] = tmp[pl.ds(at, rows), :]


def back_mid_kernel(n_t, *refs):
    kept, got, hidden, grad, w, gain, proj_bias = refs[:7]
    block_out, hg_o, attn_o, gain_o, shift_o, outb_o, projb_o = refs[7:14]
    blocks = refs[14 : 14 + n_t]
    hid = hidden[...]
    top = grad[...].astype(F32)
    g = kept[1] + got[1].astype(F32)
    unit, spread_rows = row_stats(hid)
    gain_o[...] = jnp.sum(g * unit, axis=0, keepdims=True)
    shift_o[...] = jnp.sum(g, axis=0, keepdims=True)
    projb_o[...] = jnp.sum(top, axis=0, keepdims=True)
    scaled = g * gain[...]
    centred = scaled - jnp.mean(scaled, axis=-1, keepdims=True)
    centred = centred - unit * jnp.mean(scaled * unit, axis=-1, keepdims=True)
    hg = top + spread_rows * centred
    hg_o[...] = hg
    low = hg.astype(BF16)
    attn_o[...] = low
    outb_o[...] = jnp.sum(low.astype(F32), axis=0, keepdims=True)
    heads = dg(w[...], low, 0, 1).astype(BF16)
    k = blocks[0].shape[0]
    for s in range(n_t):
        blocks[s][...] = heads[s * k : (s + 1) * k]
    block_out[...] = (hid + (kept[0] + got[0].astype(F32) + proj_bias[...])).astype(BF16)


def attn_back_kernel(n_t, heads, *refs):
    scal, q, k, v, lse, unit, w = refs[:7]
    grads = refs[7 : 7 + n_t]
    outs = refs[7 + n_t :]
    p_o = outs[:3]
    dqkv_o, gain_o, shift_o, bias_o, g_s, dk_s, dv_s = outs[3:]
    rank, boundary = place()[0], scal[0, 0]
    tok = grads[0].shape[1]
    third = q.shape[0]
    for s in range(n_t):
        g_s[rank ^ s] = grads[s][...]
    masks = [mask_of(boundary, b * tok, tok, (b + 1) * tok) for b in range(n_t)]
    scale = HEAD_DIM**-0.5
    for h in range(heads):
        lo, hi = h * HEAD_DIM, (h + 1) * HEAD_DIM
        keys = k[lo:hi, :].T
        vals = v[lo:hi, :].T
        dk_s[...] = jnp.zeros_like(dk_s)
        dv_s[...] = jnp.zeros_like(dv_s)
        for b in range(n_t):
            n = (b + 1) * tok
            cols = slice(b * tok, n)
            qb = q[lo:hi, cols]
            gb = g_s[b, lo:hi, :]
            scores = dg(keys[0:n], qb, 1, 0) * (scale * LOG2E)
            probs = jnp.exp2(jnp.where(masks[b], scores - lse[h : h + 1, cols], -jnp.inf))
            pg = dg(vals[0:n], gb, 1, 0)
            dot = jnp.sum(probs * pg, axis=0, keepdims=True)
            ds = (probs * (pg - dot)).astype(BF16)
            low = probs.astype(BF16)
            dq = jnp.dot(k[lo:hi, 0:n], ds, preferred_element_type=F32) * scale
            dqkv_o[lo:hi, cols] = dq.astype(BF16)
            dk_s[:, 0:n] += dg(qb, ds, 1, 1)
            dv_s[:, 0:n] += dg(gb, low, 1, 1)
        dqkv_o[third + lo : third + hi, :] = (dk_s[...] * scale).astype(BF16)
        dqkv_o[2 * third + lo : 2 * third + hi, :] = dv_s[...].astype(BF16)
    flat = dqkv_o[...]
    ones = jnp.ones((8, flat.shape[1]), BF16)
    sums = dg(ones, flat, 1, 1)
    bias_o[...] = jnp.zeros_like(bias_o)
    bias_o[pl.ds(rank, 1), :] = sums[0:1, 0:third]
    bias_o[pl.ds(n_t + rank, 1), :] = sums[0:1, 2 * third : 3 * third]
    gain, shift = 0.0, 0.0
    for s in range(n_t):
        at = pl.multiple_of((rank ^ s) * tok, tok)
        n1 = dg(dqkv_o[:, pl.ds(at, tok)], w[...], 0, 1)
        gain = gain + jnp.sum(n1 * unit[pl.ds(at, tok), :].astype(F32), axis=0, keepdims=True)
        shift = shift + jnp.sum(n1, axis=0, keepdims=True)
        if s % 2:
            p_o[0][s // 2] = n1.astype(BF16)
        else:
            p_o[1 + s // 2][...] = n1
    gain_o[...] = gain
    shift_o[...] = shift


def half_sum_kernel(mine, got, send):
    send[...] = (mine[...] + got[1].astype(F32)).astype(BF16)


def dp_grads_kernel(scal, attn_grad, mixed, normed, dqkv, keep_o, send_o, out_s, qkv_s):
    chip, core = place()[1:]
    rows = keep_o.shape[1]
    width = out_s.shape[1]
    out_s[...] = dg(attn_grad[...], mixed[...], 0, 1).astype(BF16)
    qkv_s[...] = dg(normed[...], dqkv[...], 0, 1).astype(BF16)
    for m in range(4):
        for j, to in ((0, keep_o), (1, send_o)):
            at = pl.multiple_of(((chip ^ m) * 2 + (core ^ j)) * rows, 16)
            to[m, :, 0:width] = out_s[pl.ds(at, rows), :]
            to[m, :, width:] = qkv_s[pl.ds(at, rows), :]


def dp_core_kernel(keep, got, own_o, *sends):
    for m in range(4):
        total = keep[m].astype(F32) + got[m].astype(F32)
        if m == 0:
            own_o[...] = total
        else:
            sends[m - 1][...] = total.astype(BF16)


def chips_one_kernel(fc_keep, fc_got, pj_keep, pj_got, base_o, fc_send, pj_send):
    for w, (keep, got, send) in enumerate(((fc_keep, fc_got, fc_send), (pj_keep, pj_got, pj_send))):
        base_o[w] = keep[0].astype(F32) + got[0].astype(F32)
        send[...] = (keep[1].astype(F32) + got[1].astype(F32)).astype(BF16)


def chips_two_kernel(n_t, base, fc_got, pj_got, dp_own, *refs):
    dp_got, (own_o, qkv_o), sends = refs[:3], refs[3:5], refs[5:]
    total = dp_own[...]
    for r in dp_got:
        total = total + r[...].astype(F32)
    k = qkv_o.shape[2]
    for i in range(3):
        qkv_o[i] = total[:, (n_t + i) * k : (n_t + i + 1) * k]
    rows, half = fc_got.shape[1], total.shape[0] // 2
    for s in range(n_t):
        to, kind = (own_o, F32) if s == 0 else (sends[s - 1], BF16)
        for w, got in enumerate((fc_got, pj_got)):
            to[w * rows : (w + 1) * rows, :] = (base[w, s] + got[s].astype(F32)).astype(kind)
        part = total[:, s * k : (s + 1) * k].astype(kind)
        to[2 * rows :, :] = jnp.concatenate([part[:half], part[half:]], axis=1)


def tensor_sum_kernel(n_t, own, *refs):
    mine_o, send_o, out_o = refs[n_t - 1 :]
    rows, k = mine_o.shape[1], out_o.shape[0]
    total = own[...]
    for r in refs[: n_t - 1]:
        total = total + r[...].astype(F32)
    for w in range(2):
        mine_o[w] = total[2 * w * rows : (2 * w + 1) * rows]
        send_o[w] = total[(2 * w + 1) * rows : (2 * w + 2) * rows].astype(BF16)
    out_o[...] = jnp.concatenate([total[4 * rows :, 0:k], total[4 * rows :, k:]], axis=0).T


def ffn_last_kernel(scal, mine, got, fc_o, pj_o):
    first = place()[2] == 0
    for w in range(2):
        a, b = mine[w], got[w].astype(F32)
        total = jnp.concatenate([jnp.where(first, a, b), jnp.where(first, b, a)], axis=1)
        if w == 0:
            fc_o[...] = total
        else:
            pj_o[...] = total


def last_kernel(mine, got_one, got_two, x, hg, gain, out):
    g = mine[...] + got_one[0].astype(F32) + got_two[...].astype(F32)
    unit, spread_rows = row_stats(x[...].astype(F32))
    scaled = g * gain[...]
    centred = scaled - jnp.mean(scaled, axis=-1, keepdims=True)
    centred = centred - unit * jnp.mean(scaled * unit, axis=-1, keepdims=True)
    out[...] = hg[...] + spread_rows * centred


def fence(*values):
    return lax.optimization_barrier(values)


def body_four(
    block_input, doc_lengths, first_gain, first_shift, qkv_weight, attn_bias, out_weight, out_bias,
    second_gain, second_shift, fc_weight, fc_bias, proj_weight, proj_bias, block_grad,
):
    n_t = lax.axis_size("tensor")
    n_dev = n_t * 8
    rank, core, chip = lax.axis_index("tensor"), lax.axis_index("core"), lax.axis_index("chip")
    tok, width = block_input.shape
    half = tok // 2
    group = tok * n_t
    width_dev = qkv_weight.shape[2]
    heads = width_dev // HEAD_DIM
    rows_dev = qkv_weight.shape[0]
    hid = fc_weight.shape[1] // 2
    wide = 3 * width_dev
    scal = doc_lengths

    def over_tensor(block):
        return [swap_bit(block, "tensor", m) for m in range(1, n_t)]

    def over_chips(block):
        return [block] + [swap_bit(block, "chip", m) for m in (1, 2, 3)]

    small = [first_gain, first_shift, attn_bias, out_bias, second_gain, second_shift, fc_bias, proj_bias]
    sizes = [p.shape[0] for p in small]
    ffn_mine, ffn_other, out_block, qkv_rows = pcall(
        functools.partial(prep_kernel, sizes),
        [((2, rows_dev, hid), BF16)] * 2 + [((rows_dev + 16, width_dev), BF16), ((rows_dev + 16, wide), BF16)],
        scratch=[pltpu.VMEM((16, width_dev), F32)], n_scalar=1, n_in=12,
    )(scal, fc_weight, proj_weight.T, out_weight, jnp.moveaxis(qkv_weight, 1, 0), *[p.reshape(1, -1) for p in small])
    out_z = over_tensor(out_block)
    ffn_block = jnp.stack([ffn_mine, swap_core(ffn_other)], axis=1)
    grad_other = swap_core(block_grad)
    out_z, ffn_block, first, qkv_rows, out_block, grad_other = fence(
        out_z, ffn_block, block_input, qkv_rows, out_block, grad_other
    )

    row_two = swap_bit(first, "tensor", 2)
    ffn_one = swap_bit(ffn_block, "tensor", 1)
    attn_block = jnp.concatenate([out_block] + list(out_z) + [qkv_rows], axis=1)
    attn_mine = over_chips(attn_block)
    zero_x, zero_y = swap_bit(ffn_block, "chip", 1), swap_bit(ffn_block, "chip", 2)
    row_two, ffn_one, attn_mine, ffn_block, first, zero_x, zero_y = fence(
        row_two, ffn_one, attn_mine, ffn_block, first, zero_x, zero_y
    )

    row_odd = swap_bit(jnp.stack([first, row_two]), "tensor", 1)
    ffn_two = swap_bit(ffn_block, "tensor", 2)
    attn_mine = jnp.stack(attn_mine)
    diagonal = swap_bit(jnp.stack([ffn_block, ffn_one]), "chip", 3)
    ffn_zero = [ffn_block, zero_x, zero_y]
    ffn_one = [ffn_one, swap_bit(ffn_one, "chip", 1), swap_bit(ffn_one, "chip", 2)]
    row_two, row_odd, attn_mine, diagonal, ffn_zero, ffn_one, ffn_two, ffn_block = fence(
        row_two, row_odd, attn_mine, diagonal, ffn_zero, ffn_one, ffn_two, ffn_block
    )
    attn_other = swap_core(attn_mine)

    ffn_two = over_chips(ffn_two)
    ffn_three = swap_bit(ffn_block, "tensor", 3)
    vec = ((1, width), F32)
    params = pcall(
        functools.partial(unpack_kernel, sizes, n_t),
        [vec, vec, ((2 * n_t, width_dev), F32), vec, vec, vec, ((2 * n_t, hid), F32), vec],
        scratch=[pltpu.VMEM((n_dev, 8, 128), F32)], n_scalar=1, n_in=2,
    )(scal, attn_mine, attn_other)
    gain_one, shift_one, attn_shift, out_shift, gain_two, shift_two, fc_shift, proj_shift = params
    attn_outs = pcall(
        functools.partial(attn_kernel, n_t, heads),
        [((width_dev, group), BF16)] * 3 + [((8, group), F32)] + [((group, width), BF16)] * 2
        + [((width, wide), BF16)] + [((width_dev, tok), BF16)] * n_t,
        scratch=[pltpu.VMEM((n_t, width_dev, tok), BF16)],
        n_scalar=1, n_in=3 + 2 + 3, us=12,
    )(scal, block_input, row_two, row_odd, attn_mine, attn_other,
      gain_one, shift_one, attn_shift)
    attn_outs, ffn_two, ffn_three = fence(attn_outs, ffn_two, ffn_three)
    q, k, v, lse, normed_one, unit_one, w_qkv = attn_outs[:7]
    mixed = list(attn_outs[7:])
    mixed = [mixed[0]] + [swap_bit(mixed[m], "tensor", m) for m in range(1, n_t)]
    fc_three, pj_three = ffn_three[0], ffn_three[1]
    fc_x, pj_y = swap_bit(fc_three, "chip", 1), swap_bit(pj_three, "chip", 2)
    mixed, fc_three, pj_three, fc_x, pj_y = fence(mixed, fc_three, pj_three, fc_x, pj_y)
    fc_pair, pj_pair = jnp.stack([fc_three, fc_x]), jnp.stack([pj_three, pj_y])
    fc_next, pj_next = swap_bit(fc_pair, "chip", 2), swap_bit(pj_pair, "chip", 1)
    three = [fc_three, fc_x, fc_next[0], fc_next[1], pj_three, pj_next[0], pj_y, pj_next[1]]

    hidden, normed_two, mixed_all, w_out = pcall(
        functools.partial(mid_kernel, n_t),
        [((tok, width), F32), ((tok, width), BF16), ((width, tok), BF16), ((width, width), BF16)],
        n_scalar=1, n_in=n_t + 2 + 4, us=4,
    )(scal, *mixed, attn_mine, attn_other, block_input, out_shift, gain_two, shift_two)

    normed_other = swap_core(normed_two)
    cols = n_t * hid
    kept, send, act, pre, fc_sums = pcall(
        functools.partial(ffn_kernel, n_t),
        [((2, tok, width), F32), ((2, tok, width), BF16)] + [((2 * tok, cols), BF16)] * 2 + [((2 * n_t, hid), F32)],
        scratch=[pltpu.VMEM((2 * tok, width), BF16)] * 2 + [pltpu.VMEM((width, hid), BF16)] * 2
        + [pltpu.VMEM((2 * tok, width), F32)] * 2,
        n_scalar=1, n_in=5 + 19, us=13,
    )(scal, normed_two, normed_other, block_grad, grad_other, fc_shift, *ffn_zero, *ffn_one, diagonal, *ffn_two,
      *three)
    got = swap_core(send)

    back = pcall(
        functools.partial(back_mid_kernel, n_t),
        [((tok, width), BF16), ((tok, width), F32), ((tok, width), BF16)] + [((1, width), F32)] * 4
        + [((width_dev, tok), BF16)] * n_t,
        n_in=7, us=4,
    )(kept, got, hidden, block_grad, w_out, gain_two, proj_shift)
    block_out, hidden_grad, attn_grad, gain_two_grad, shift_two_grad, out_bias_grad, proj_bias_grad = back[:7]
    blocks = list(back[7:])
    blocks = [blocks[0]] + [swap_bit(blocks[m], "tensor", m) for m in range(1, n_t)]


    stack = ((2, n_t, 2 * rows_dev, hid), BF16)
    fc_keep, fc_send, pj_keep, pj_send = pcall(
        functools.partial(ffn_grads_kernel, n_t), [stack] * 4,
        scratch=[pltpu.VMEM((2 * tok, width), BF16)] * 2 + [pltpu.VMEM((width, hid), BF16)],
        n_scalar=1, n_in=6, flops=8 * 10**9,
    )(scal, normed_two, normed_other, block_grad, grad_other, after(act, back[7]), pre)
    fc_got, pj_got = swap_bit(fc_send, "chip", 1), swap_bit(pj_send, "chip", 2)
    q, blocks, fc_keep, pj_keep = fence(q, blocks, fc_keep, pj_keep)

    outs = pcall(
        functools.partial(attn_back_kernel, n_t, heads),
        [((2, tok, width), BF16)] + [((tok, width), F32)] * 2
        + [((wide, group), BF16), ((1, width), F32), ((1, width), F32), ((2 * n_t, width_dev), F32)],
        scratch=[
            pltpu.VMEM((n_t, width_dev, tok), BF16), pltpu.VMEM((HEAD_DIM, group), F32),
            pltpu.VMEM((HEAD_DIM, group), F32),
        ],
        n_scalar=1, n_in=6 + n_t, flops=14 * 10**9,
    )(scal, q, k, v, lse, unit_one, w_qkv, *blocks)
    outs, attn_grad = fence(outs, attn_grad)
    part_odd, part_own, part_two = outs[:3]
    dqkv, gain_one_grad, shift_one_grad, bias_grads = outs[3:]
    got_one = swap_bit(part_odd, "tensor", 1)
    both = (rows_dev, width + wide)
    keep, dp_send = pcall(
        dp_grads_kernel, [((4,) + both, BF16)] * 2,
        scratch=[pltpu.VMEM((width, width), BF16), pltpu.VMEM((width, wide), BF16)], n_scalar=1, n_in=4, us=6,
    )(scal, attn_grad, mixed_all, normed_one, dqkv)
    half_stack = ((n_t, 2 * rows_dev, hid), BF16)
    base, fc_send, pj_send = pcall(
        chips_one_kernel, [((2, n_t, 2 * rows_dev, hid), F32)] + [half_stack] * 2, n_in=4,
    )(fc_keep, fc_got, pj_keep, pj_got)
    grads = [
        gain_one_grad, shift_one_grad, bias_grads.reshape(1, -1), out_bias_grad,
        gain_two_grad, shift_two_grad, fc_sums.reshape(1, -1), proj_bias_grad,
    ]
    (packed,) = pcall(functools.partial(pack_kernel, sizes), [((n_dev, 8, 128), F32)], n_in=8)(*grads)
    got_one, packed, keep, dp_send, base, fc_send, pj_send = fence(
        got_one, packed, keep, dp_send, base, fc_send, pj_send
    )

    (part_two,) = pcall(half_sum_kernel, [((tok, width), BF16)], n_in=2)(part_two, got_one)
    got_two = swap_bit(part_two, "tensor", 2)
    packed = lax.all_to_all(packed, EVERY, 0, 0, tiled=True)
    fc_got, pj_got = swap_bit(fc_send, "chip", 2), swap_bit(pj_send, "chip", 1)
    own = pcall(dp_core_kernel, [(both, F32)] + [(both, BF16)] * 3, n_in=2, flops=14 * 10**9)(keep, swap_core(dp_send))
    own = [own[0]] + [swap_bit(own[m], "chip", m) for m in (1, 2, 3)]
    block = (4 * rows_dev + rows_dev // 2, hid)
    total, qkv_weight_grad, *sends = pcall(
        functools.partial(chips_two_kernel, n_t),
        [(block, F32), ((3, rows_dev, width_dev), F32)] + [(block, BF16)] * (n_t - 1), n_in=7,
    )(base, fc_got, pj_got, *own)
    got_two, total, packed, sends = fence(got_two, total, packed, sends)

    total = [total] + [swap_bit(sends[m - 1], "tensor", m) for m in range(1, n_t)]
    (input_grad,) = pcall(last_kernel, [((tok, width), F32)], n_in=6)(
        part_own, got_one, got_two, block_input, hidden_grad, gain_one
    )
    small_outs = pcall(functools.partial(finish_kernel, sizes), [((1, n), F32) for n in sizes], n_in=1)(packed)
    small_outs = [s.reshape(-1) for s in small_outs]
    qkv_weight_grad = jnp.moveaxis(qkv_weight_grad, 0, 1)
    total, input_grad, small_outs, qkv_weight_grad = fence(total, input_grad, small_outs, qkv_weight_grad)
    pair = (2, rows_dev, hid)
    mine, send, out_weight_grad = pcall(
        functools.partial(tensor_sum_kernel, n_t), [(pair, F32), (pair, BF16), (out_weight.shape, F32)], n_in=n_t,
    )(*total)
    fc_weight_grad, proj_weight_grad = pcall(
        ffn_last_kernel, [(fc_weight.shape, F32)] * 2, n_scalar=1, n_in=2,
    )(scal, mine, swap_core(send))
    return (
        block_out, input_grad, small_outs[0], small_outs[1], qkv_weight_grad,
        small_outs[2], out_weight_grad,
        small_outs[3], small_outs[4], small_outs[5], fc_weight_grad, small_outs[6], proj_weight_grad.T, small_outs[7],
    )


def solution(mesh):
    n_dp, n_tensor = mesh.shape["dp"], mesh.shape["tensor"]
    grid = Mesh(mesh.devices.reshape(n_dp // 2, 2, n_tensor), EVERY)
    dp = ("chip", "core")
    vec, rows, cols = P(EVERY), P(EVERY, None), P("tensor", dp)
    return jax.shard_map(
        body_four if n_dp == 8 and n_tensor == 4 else body,
        mesh=grid,
        in_specs=(
            rows, P(dp, None), vec, vec, P(dp, None, "tensor"), vec, cols, vec,
            vec, vec, P(dp, "tensor"), vec, cols, vec, rows,
        ),
        out_specs=(
            rows, rows, vec, vec, P(dp, None, "tensor"), vec, cols, vec,
            vec, vec, P(dp, "tensor"), vec, cols, vec,
        ),
        check_vma=False,
    )
```
